32 devices in a mesh: groups: 2 (over y), wide: 4 (over z), rep: 2 (over x), sub: 2 (over core).
Axes of the slice: x: 2, y: 2, z: 4, core: 2. Of those that a mesh axis runs over, the one named last changes fastest.
Arguments:
- samples: bfloat16 [8, 2, 10, 128, 1024], P(('groups', 'wide'), 'rep', None, None, 'sub'), parts along dimension 0, may hold values from -8 to 8
- centroids: float32 [8192, 1024], P(('groups', 'wide'), 'sub'), parts along dimension 0, may hold values from -6 to 6
- move_target: int32 [8, 2, 10], P(('groups', 'wide'), 'rep'), parts along dimension 0, may hold values from -1 to 31, as said below
- fetch_ids: int32 [8, 2, 24], P(('groups', 'wide'), 'rep'), parts along dimension 0, may hold values from 0 to 31, as said below
- cand: int32 [8, 2, 8, 8], P(('groups', 'wide'), 'rep'), parts along dimension 0, may hold values from 0 to 23
Outputs:
- new_centroids: float32 [8192, 1024], P(('groups', 'wide', 'rep'), 'sub'), parts along dimension 0
- energy: float32 [8, 2, 8, 128], P(('groups', 'wide'), 'rep', None, 'sub'), parts along dimension 0
The draws below stay inside these ranges and needn't reach their ends.
There are 2 independent parts, one for each index of `groups`. The reference program is written for one: setup_inputs(seed, part) draws one part's arguments, and reference() takes and returns one part's arrays. A program takes and returns all parts, laid end to end along the dimension named above; each array names one. Nothing has to cross between parts.
Inputs may be any that keep to these rules, and one draw needn't show every extreme that they name: `move_target`: entry slots below 8 keep their block on its own device or are -1; entry slot 8 + k - 1, for k = 1 to 2, goes to a work slot of the device k indices further along wide (cyclically) or is -1; within each index of rep the targets are distinct, and a device's filled work slots are the lowest ones; some device hands away 2 blocks. `fetch_ids`: at most 9 of one device's fetched blocks belong to one owner (owner of block g: index g // 8 of wide), and some owner has exactly 9 for every device.
All inputs are finite; a program needn't handle non-finite values.
Results may differ from the reference program's by a relative error of at most 0.0033.
Values may be sent and summed in bfloat16 or wider, within the bound.
No kernel may reach another device: no remote copies, remote signals or barrier semaphores. Data moves between devices by JAX's collectives and lax.ppermute only.
A program may use at most 64 MiB of HBM per device.

```python
import math
import jax
import jax.numpy as jnp
from jax import lax

D = 1024
ROWS = 128
LISTS = 8
CB_DEV = 8
EXTRA = 2
BAL = 8
U = 24
BLK_DEV = 10
CAP = 9
NCB = 32
K = 4096
N_WIDE = 4
N_REP = 2


def draw_samples(key, part):
    key = jax.random.fold_in(key, 11)
    shape = (N_WIDE, N_REP, BLK_DEV, ROWS, D)
    values = jnp.clip(jax.random.normal(key, shape, jnp.float32), -6.0, 6.0)
    return values.astype(jnp.bfloat16)


def move_row(key):
    keep_key, extra_key = jax.random.split(key)
    keep = jax.random.randint(keep_key, (N_WIDE,), 1, BAL - EXTRA + 1).astype(jnp.int32)
    keep = keep.at[N_WIDE - 1].set(BAL - EXTRA)
    extra = jax.random.randint(extra_key, (N_WIDE,), 0, EXTRA + 1).astype(jnp.int32)
    feeders = (N_WIDE - 2 - jnp.arange(EXTRA, dtype=jnp.int32)) % N_WIDE
    extra = extra.at[feeders].set(EXTRA)
    extra = extra.at[0].set(EXTRA)
    device = jnp.arange(N_WIDE, dtype=jnp.int32)
    slot = jnp.arange(BLK_DEV, dtype=jnp.int32)
    index = jnp.maximum(slot - BAL, 0)
    receiver = (device[:, None] + index[None, :] + 1) % N_WIDE
    earlier = jnp.arange(EXTRA, dtype=jnp.int32)
    senders = (receiver[:, :, None] - earlier[None, None, :] - 1) % N_WIDE
    counted = (jnp.take(extra, senders) > earlier[None, None, :]) & (earlier[None, None, :] < index[None, :, None])
    rank = jnp.sum(counted.astype(jnp.int32), axis=2)
    moved = receiver * BAL + jnp.take(keep, receiver) + rank
    kept = jnp.where(slot[None, :] < keep[:, None], device[:, None] * BAL + slot[None, :], -1)
    handed = jnp.where(index[None, :] < extra[:, None], moved, -1)
    return jnp.where(slot[None, :] < BAL, kept, handed).astype(jnp.int32)


def draw_move_target(key, part):
    key = jax.random.fold_in(key, 23)
    keys = jax.random.split(key, N_REP)
    rows_all = jax.vmap(move_row)(keys)
    return jnp.transpose(rows_all, (1, 0, 2)).astype(jnp.int32)


def fetch_row(key):
    first_key, order_key, mix_key, local_key = jax.random.split(key, 4)
    tokens = N_WIDE * CAP
    forced = jax.random.randint(first_key, (), 0, N_WIDE).astype(jnp.int32)
    token_owner = jnp.arange(tokens, dtype=jnp.int32) // CAP
    shuffle = jax.random.permutation(order_key, tokens).astype(jnp.int32)
    priority = jnp.where(token_owner == forced, shuffle - tokens, shuffle)
    picked = jnp.take(token_owner, jnp.argsort(priority)[:U])
    picked = jnp.take(picked, jax.random.permutation(mix_key, U))
    local = jax.random.randint(local_key, (U,), 0, CB_DEV).astype(jnp.int32)
    return (picked * CB_DEV + local).astype(jnp.int32)


def draw_fetch_ids(key, part):
    key = jax.random.fold_in(key, 37)
    keys = jax.random.split(key, N_WIDE * N_REP)
    return jax.vmap(fetch_row)(keys).reshape(N_WIDE, N_REP, U).astype(jnp.int32)


def plant(entries, own_key, least, top_value):
    place = [jax.random.randint(jax.random.fold_in(own_key, axis), (), 0, length) for axis, length in enumerate(entries.shape)]
    longest = entries.shape.index(max(entries.shape))
    beside = place[:longest] + [(place[longest] + 1) % entries.shape[longest]] + place[longest + 1:]
    return entries.at[tuple(place)].set(least).at[tuple(beside)].set(top_value)


def shard_levels(stream_key, shape, pieces, smallest, largest):
    def one(position, blocks):
        heights = jax.random.uniform(jax.random.fold_in(jax.random.fold_in(stream_key, 6), position), (blocks,), jnp.float32, smallest / len(pieces), largest / len(pieces))
        return jnp.repeat(jnp.exp(heights), shape[position] // blocks).reshape((-1,) + (1,) * (len(shape) - position - 1))

    level = one(*pieces[0])
    for cut in pieces[1:]:
        level = level * one(*cut)
    return level


def noise(own_key, dims, scale, reach, cuts=(), held_as=jnp.bfloat16):
    drawn = jax.random.normal(own_key, dims, jnp.float32) * scale
    if len(cuts) > 0:
        drawn = shard_levels(own_key, dims, cuts, -0.22, 0.18) * drawn
    return jnp.clip(drawn, min=-reach, max=reach).astype(held_as)


def setup_inputs(seed: int = 0, part: int = 0) -> dict:
    splits = jax.random.split(jax.random.key(seed), 6)
    part_splits = jax.random.split(jax.random.fold_in(splits[5], part), 6)
    return {
        "samples": draw_samples(jax.random.fold_in(jax.random.fold_in(splits[5], part), 71), part),
        "centroids": noise(part_splits[1], (K, D), 1.0, 6.0, ((0, 4), (1, 2)), jnp.float32),
        "move_target": draw_move_target(jax.random.fold_in(jax.random.fold_in(splits[5], part), 71), part),
        "fetch_ids": draw_fetch_ids(jax.random.fold_in(jax.random.fold_in(splits[5], part), 71), part),
        "cand": plant(jax.random.randint(part_splits[4], (N_WIDE, N_REP, BAL, LISTS), 0, U), jax.random.fold_in(part_splits[4], 1), 0, U - 1).astype(jnp.int32),
    }


PRIOR = 1.0

def soft_block(blocks, live, fetched, lists):
    tau = 2.0 * math.sqrt(D)
    flat = lists.reshape(-1).astype(jnp.int32)
    chosen = jnp.take(fetched, flat, axis=0).reshape(BAL, LISTS * ROWS, D)
    blocks32 = blocks.astype(jnp.float32)
    dots = jnp.einsum('bnd,bmd->bnm', blocks32, chosen.astype(jnp.float32))
    fetched32 = fetched.astype(jnp.float32)
    cent_sq = jnp.take(lax.optimization_barrier(jnp.sum(fetched32 * fetched32, axis=-1)), flat, axis=0).reshape(BAL, LISTS * ROWS)
    work_sq = lax.optimization_barrier(jnp.sum(blocks32 * blocks32, axis=-1))
    logits = (2.0 * dots - cent_sq[:, None, :] - work_sq[:, :, None]) / tau
    top = lax.optimization_barrier(jnp.max(logits, axis=-1, keepdims=True))
    expo = jnp.exp(logits - top)
    total = lax.optimization_barrier(jnp.sum(expo, axis=-1, keepdims=True))
    weights = (expo / total).astype(jnp.bfloat16)
    weights = jnp.where(live[:, None, None], weights, jnp.zeros_like(weights))
    energy = -tau * (top[..., 0] + jnp.log(total[..., 0])) / D
    energy = jnp.where(live[:, None], energy, jnp.zeros_like(energy))
    weights32 = weights.astype(jnp.float32)
    sums = jnp.einsum('bnm,bnd->bmd', weights32, blocks32).reshape(BAL * LISTS, ROWS * D)
    mass = lax.optimization_barrier(jnp.sum(weights32, axis=1)).reshape(BAL * LISTS, ROWS)
    onehot = (flat[None, :] == jnp.arange(U, dtype=jnp.int32)[:, None]).astype(jnp.float32)
    pool_sums = jnp.dot(onehot, sums, precision=lax.Precision.HIGHEST)
    pool_mass = jnp.dot(onehot, mass, precision=lax.Precision.HIGHEST)
    pool_sums = lax.optimization_barrier(pool_sums.astype(jnp.bfloat16)).astype(jnp.float32)
    pool_mass = lax.optimization_barrier(pool_mass.astype(jnp.bfloat16)).astype(jnp.float32)
    return (energy, pool_sums.reshape(U, ROWS, D), pool_mass)

def reference(samples, centroids, move_target, fetch_ids, cand):
    cent_blocks = centroids.reshape(NCB, ROWS, D)
    total_sums = jnp.zeros((NCB, ROWS, D), jnp.float32)
    total_mass = jnp.zeros((NCB, ROWS), jnp.float32)
    energies = []
    for rep in range(N_REP):
        row_blocks = samples[:, rep].reshape(N_WIDE * BLK_DEV, ROWS, D)
        targets = move_target[:, rep].reshape(-1)
        slots = jnp.where(targets >= 0, targets, N_WIDE * BAL).astype(jnp.int32)
        placed = jnp.zeros((N_WIDE * BAL, ROWS, D), jnp.bfloat16).at[slots].set(row_blocks, mode='drop')
        marks = jnp.zeros((N_WIDE * BAL,), jnp.int32).at[slots].set(1, mode='drop')
        placed = placed.reshape(N_WIDE, BAL, ROWS, D)
        alive = marks.reshape(N_WIDE, BAL) > 0

        def one_device(carry, items):
            sums_acc, mass_acc = carry
            blocks, live, ids, lists = items
            ids = ids.astype(jnp.int32)
            fetched = jnp.take(cent_blocks, ids, axis=0).astype(jnp.bfloat16)
            energy, pool_sums, pool_mass = soft_block(blocks, live, fetched, lists)
            sums_acc = sums_acc.at[ids].add(pool_sums)
            mass_acc = mass_acc.at[ids].add(pool_mass)
            return ((sums_acc, mass_acc), energy)
        start = (jnp.zeros((NCB, ROWS, D), jnp.float32), jnp.zeros((NCB, ROWS), jnp.float32))
        (row_sums, row_mass), energy = lax.scan(one_device, start, (placed, alive, fetch_ids[:, rep], cand[:, rep]))
        total_sums = total_sums + lax.optimization_barrier(row_sums.astype(jnp.bfloat16)).astype(jnp.float32)
        total_mass = total_mass + lax.optimization_barrier(row_mass.astype(jnp.bfloat16)).astype(jnp.float32)
        energies.append(energy)
    fresh = (total_sums + PRIOR * cent_blocks) / (total_mass[:, :, None] + PRIOR)
    return (fresh.reshape(K, D), jnp.stack(energies, axis=1))
```

```python
import math

import jax
import jax.numpy as jnp
from jax import lax
from jax.experimental import pallas as pl
from jax.experimental.pallas import tpu as pltpu
from jax.sharding import PartitionSpec as P

D = 1024


PRIOR = 1.0


def passed_along(value, axis, steps):
    count = lax.axis_size(axis)
    pairs = [(source, (source + steps) % count) for source in range(count)]
    return lax.ppermute(value, axis, pairs)


def pick_rows(table, index, present):
    picked = jnp.take(table, jnp.maximum(index, 0), axis=0)
    shape = (present.shape[0],) + (1,) * (picked.ndim - 1)
    return jnp.where(present.reshape(shape), picked, jnp.zeros_like(picked))


def soften(scores, tau):
    logits = scores / tau
    top = jnp.max(logits, axis=-1, keepdims=True)
    expo = jnp.exp(logits - top)
    total = jnp.sum(expo, axis=-1, keepdims=True)
    weights = (expo / total).astype(jnp.bfloat16)
    energy = -tau * (top[..., 0] + jnp.log(total[..., 0])) / D
    return (weights, energy)


def exchange_plan(samples, centroids, move_target, fetch_ids, cand):
    rows = samples.shape[3]
    width = samples.shape[4]
    slots_in = samples.shape[2]
    bal = cand.shape[2]
    lists = cand.shape[3]
    pool = fetch_ids.shape[2]
    owned = centroids.shape[0] // rows
    peers = lax.axis_size("wide")
    myself = lax.axis_index("wide")
    cap = max(1, 3 * pool // (2 * peers))
    tau = 2.0 * math.sqrt(D)
    handed = slots_in - bal
    blocks = samples.reshape(slots_in, rows, width)
    target = move_target.reshape(slots_in)
    dest = jnp.where(target >= 0, target // bal, -1)
    dest_slot = jnp.where(target >= 0, target % bal, -1)
    got_list = []
    slot_list = []
    for step in range(handed):
        entry = bal + step
        present = target[entry] >= 0
        send_block = jnp.where(present, blocks[entry], jnp.zeros_like(blocks[entry]))[None]
        send_slot = jnp.where(present, target[entry] % bal, -1).reshape(1)
        got_block, got_slot = passed_along((send_block, send_slot), "wide", step + 1)
        got_list.append(got_block)
        slot_list.append(got_slot)
    ids = fetch_ids.reshape(pool)
    owner = ids // owned
    local = ids % owned
    before = jnp.arange(pool)[None, :] < jnp.arange(pool)[:, None]
    position = jnp.sum(((owner[None, :] == owner[:, None]) & before).astype(jnp.int32), axis=1)
    slot_of = owner * cap + position
    slot_match = slot_of[None, :] == jnp.arange(peers * cap, dtype=jnp.int32)[:, None]
    slot_used = jnp.any(slot_match, axis=1)
    slot_item = jnp.sum(
        jnp.where(slot_match, jnp.arange(pool, dtype=jnp.int32)[None, :], 0), axis=1
    )
    asks = jnp.where(slot_used, jnp.take(local, slot_item), -1).reshape(peers, cap)
    wanted = lax.all_to_all(asks, "wide", split_axis=0, concat_axis=0, tiled=True)
    table = centroids.reshape(owned, rows, width)
    table_half = table.astype(jnp.bfloat16)
    wanted_flat = wanted.reshape(peers * cap)
    reply = pick_rows(table_half, wanted_flat, wanted_flat >= 0).reshape(peers, cap, rows, width)
    answered = lax.all_to_all(reply, "wide", split_axis=0, concat_axis=0, tiled=True)
    fetched = jnp.take(answered.reshape(peers * cap, rows, width), slot_of, axis=0)
    keep_here = dest == myself
    source_blocks = jnp.concatenate([blocks] + got_list, axis=0)
    source_slots = jnp.concatenate([jnp.where(keep_here, dest_slot, -1)] + slot_list, axis=0)
    fill_match = source_slots[None, :] == jnp.arange(bal, dtype=jnp.int32)[:, None]
    live = jnp.any(fill_match, axis=1)
    anchor = jnp.sum(
        jnp.where(fill_match, jnp.arange(slots_in + handed, dtype=jnp.int32)[None, :], 0), axis=1
    )
    work = pick_rows(source_blocks, anchor, live)
    flat_lists = cand.reshape(bal * lists)
    fetched_sq = jnp.sum(jnp.square(fetched.astype(jnp.float32)), axis=-1)

    def slot_scores(carry, items):
        work_one, lists_one = items
        chosen = jnp.take(fetched, lists_one, axis=0).reshape(lists * rows, width)
        dots = jnp.dot(work_one, chosen.T, preferred_element_type=jnp.float32)
        cent_sq = jnp.take(fetched_sq, lists_one, axis=0).reshape(lists * rows)
        work_sq = jnp.sum(jnp.square(work_one.astype(jnp.float32)), axis=-1)
        return (carry, 2.0 * dots - cent_sq[None, :] - work_sq[:, None])

    unused, partial_scores = lax.scan(slot_scores, 0, (work, cand.reshape(bal, lists)))
    half = rows // lax.axis_size("sub")
    lowest = lax.axis_index("sub") * half
    scores = lax.psum(partial_scores, "sub")
    weights, energy = soften(scores, tau)
    energy = lax.dynamic_slice_in_dim(energy, lowest, half, 1)
    weights = jnp.where(live[:, None, None], weights, jnp.zeros_like(weights))
    energy = jnp.where(live[:, None], energy, jnp.zeros_like(energy))
    pool_range = jnp.arange(pool, dtype=jnp.int32)

    def slot_sums(total, items):
        weights_one, work_one, lists_one = items
        term = jnp.dot(weights_one.T, work_one, preferred_element_type=jnp.float32).reshape(
            lists, rows * width
        )
        hot = (lists_one[None, :] == pool_range[:, None]).astype(jnp.float32)
        return (total + jnp.dot(hot, term, precision=lax.Precision.HIGHEST), 0)

    start_sums = jnp.zeros((pool, rows * width), jnp.float32)
    pooled, unused_two = lax.scan(slot_sums, start_sums, (weights, work, cand.reshape(bal, lists)))
    pool_sums = pooled.astype(jnp.bfloat16)
    mass = jnp.sum(weights.astype(jnp.float32), axis=1).reshape(bal * lists, rows)
    onehot = (flat_lists[None, :] == pool_range[:, None]).astype(jnp.float32)
    pool_mass = jnp.dot(onehot, mass, precision=lax.Precision.HIGHEST).astype(jnp.bfloat16)
    back_sums = pick_rows(pool_sums, slot_item, slot_used).reshape(peers, cap, rows, width)
    back_mass = pick_rows(pool_mass, slot_item, slot_used).reshape(peers, cap, rows)
    came_sums, came_mass = (
        lax.all_to_all(back_sums, "wide", split_axis=0, concat_axis=0, tiled=True),
        lax.all_to_all(back_mass, "wide", split_axis=0, concat_axis=0, tiled=True),
    )
    owner_hot = (wanted_flat[None, :] == jnp.arange(owned, dtype=jnp.int32)[:, None]).astype(
        jnp.bfloat16
    )
    owner_sums = jnp.dot(
        owner_hot, came_sums.reshape(peers * cap, rows * width), preferred_element_type=jnp.float32
    )
    owner_mass = jnp.dot(
        owner_hot, came_mass.reshape(peers * cap, rows), preferred_element_type=jnp.float32
    )
    share_sums, share_mass = (
        lax.psum_scatter(
            owner_sums.reshape(owned, rows, width).astype(jnp.bfloat16),
            "rep",
            scatter_dimension=0,
            tiled=True,
        ).astype(jnp.float32),
        lax.psum_scatter(
            owner_mass.astype(jnp.bfloat16), "rep", scatter_dimension=0, tiled=True
        ).astype(jnp.float32),
    )
    share = share_sums.shape[0]
    first_block = lax.axis_index("rep") * share
    previous = lax.dynamic_slice_in_dim(table, first_block, share, 0)
    fresh = (share_sums + PRIOR * previous) / (share_mass[:, :, None] + PRIOR)
    return (fresh.reshape(share * rows, width), energy.reshape(1, 1, bal, half))


LOW = -1e30
MEGA = 2**20


def swapped(value, axis):
    return lax.ppermute(value, axis, [(0, 1), (1, 0)])


def score_kernel(mult_ref, x_ref, c_ref, csq_ref, em_ref, stats_ref, *, span, tau):
    tile = x_ref.shape[0]
    count = mult_ref.shape[0]
    rows = c_ref.shape[0] // count
    places = tile // span
    first = pl.program_id(0) * places
    em_ref[...] = lax.dot_general(
        c_ref[...], x_ref[...], (((1,), (1,)), ((), ())), preferred_element_type=jnp.float32
    )
    place = lax.broadcasted_iota(jnp.int32, (1, tile), 1) // span
    top = jnp.full((1, tile), LOW, jnp.float32)
    weight = []
    for g in range(count):
        m = jnp.zeros((1, tile), jnp.float32)
        for p in range(places):
            m = jnp.where(place == p, mult_ref[g, first + p].astype(jnp.float32), m)
        weight.append(m)
        part = pl.ds(g * rows, rows)
        logits = (2.0 * em_ref[part, :] - csq_ref[part, 0:1]) / tau
        em_ref[part, :] = logits
        best = jnp.max(logits, axis=0, keepdims=True)
        top = jnp.maximum(top, jnp.where(m > 0, best, LOW))
    total = jnp.zeros((1, tile), jnp.float32)
    for g in range(count):
        part = pl.ds(g * rows, rows)
        listed = weight[g] > 0
        expo = jnp.where(listed, jnp.exp(jnp.where(listed, em_ref[part, :] - top, 0.0)), 0.0)
        expo = expo * weight[g]
        em_ref[part, :] = expo
        total = total + jnp.sum(expo, axis=0, keepdims=True)
    stats_ref[...] = jnp.concatenate([top, total], axis=0)


def score_chunk(mult, x, cent, cent_sq, span, tau):
    lanes, depth = x.shape
    owned_rows = cent.shape[0]
    tile = 256
    return pl.pallas_call(
        lambda *refs: score_kernel(*refs, span=span, tau=tau),
        grid=(lanes // tile,),
        in_specs=[
            pl.BlockSpec(memory_space=pltpu.SMEM),
            pl.BlockSpec((tile, depth), lambda i: (i, 0)),
            pl.BlockSpec((owned_rows, depth), lambda i: (0, 0)),
            pl.BlockSpec((owned_rows, 128), lambda i: (0, 0)),
        ],
        out_specs=[
            pl.BlockSpec((owned_rows, tile), lambda i: (0, i)),
            pl.BlockSpec((2, tile), lambda i: (0, i)),
        ],
        out_shape=[
            jax.ShapeDtypeStruct((owned_rows, lanes), jnp.float32),
            jax.ShapeDtypeStruct((2, lanes), jnp.float32),
        ],
        compiler_params=pltpu.CompilerParams(vmem_limit_bytes=40 * MEGA),
        cost_estimate=pl.CostEstimate(
            flops=2 * lanes * owned_rows * depth,
            bytes_accessed=4 * lanes * owned_rows,
            transcendentals=lanes * owned_rows,
        ),
        name="chunk_scores",
    )(mult, x, cent, cent_sq)


def aligned(stats, chunk, chunks):
    return [stats[k][(chunk - k) % chunks] for k in range(chunks)]


def combine(parts):
    top = parts[0][0:1]
    for part in parts[1:]:
        top = jnp.maximum(top, part[0:1])
    total = jnp.zeros_like(top)
    for part in parts:
        total = total + part[1:2] * jnp.exp(part[0:1] - top)
    return top, total


def sums_kernel(half_ref, *refs, chunks):
    em = refs[:chunks]
    xs = refs[chunks : 2 * chunks]
    stats = refs[2 * chunks : 3 * chunks]
    own_ref, other_ref = refs[3 * chunks : 3 * chunks + 2]
    em_v, x_v, sems = refs[3 * chunks + 2 :]
    count, lanes = em_v.shape[1:]
    width = own_ref.shape[1]
    start = pl.multiple_of(half_ref[0] * count, count)
    copies = []
    for s in range(chunks):
        pair = (
            pltpu.make_async_copy(em[s].at[pl.ds(start, count), :], em_v.at[s], sems.at[2 * s]),
            pltpu.make_async_copy(xs[s], x_v.at[s], sems.at[2 * s + 1]),
        )
        for copy in pair:
            copy.start()
        copies.append(pair)
    sums = jnp.zeros((count, 2 * width), jnp.float32)
    mass = jnp.zeros((count, 128), jnp.float32)
    for s in range(chunks):
        parts = []
        for k in range(chunks):
            c = (s - k) % chunks
            parts.append(stats[k][:, c * lanes : (c + 1) * lanes])
        top, total = combine(parts)
        scale = jnp.exp(parts[0][0:1] - top) * jnp.where(total > 0, 1.0 / total, 0.0)
        for copy in copies[s]:
            copy.wait()
        weights = (em_v[s] * scale).astype(jnp.bfloat16)
        sums = sums + jnp.dot(weights, x_v[s], preferred_element_type=jnp.float32)
        wide = weights.astype(jnp.float32)
        for lane in range(0, lanes, 128):
            mass = mass + wide[:, lane : lane + 128]
    mass = jnp.sum(mass, axis=1, keepdims=True)
    mass = jnp.broadcast_to(mass, (count, 128)).T[0:16]
    own_ref[0:count, :] = sums[:, :width]
    own_ref[count : count + 16, :] = mass
    other_ref[0:count, :] = sums[:, width:].astype(jnp.bfloat16)
    other_ref[count : count + 16, :] = mass.astype(jnp.bfloat16)


def half_sums(half, em, xs, stats):
    chunks = len(em)
    lanes, depth = xs[0].shape
    count = em[0].shape[0] // 2
    width = depth // 2
    return pl.pallas_call(
        lambda *refs: sums_kernel(*refs, chunks=chunks),
        in_specs=[pl.BlockSpec(memory_space=pltpu.SMEM)]
        + [pl.BlockSpec(memory_space=pl.ANY)] * (2 * chunks)
        + [pl.BlockSpec(memory_space=pltpu.VMEM)] * chunks,
        out_specs=[pl.BlockSpec(memory_space=pltpu.VMEM)] * 2,
        out_shape=[
            jax.ShapeDtypeStruct((count + 16, width), jnp.float32),
            jax.ShapeDtypeStruct((count + 16, width), jnp.bfloat16),
        ],
        scratch_shapes=[
            pltpu.VMEM((chunks, count, lanes), jnp.float32),
            pltpu.VMEM((chunks, lanes, depth), jnp.bfloat16),
            pltpu.SemaphoreType.DMA((2 * chunks,)),
        ],
        compiler_params=pltpu.CompilerParams(vmem_limit_bytes=40 * MEGA),
        cost_estimate=pl.CostEstimate(
            flops=2 * chunks * lanes * count * depth,
            bytes_accessed=4 * chunks * lanes * (count + depth),
            transcendentals=0,
        ),
        name="half_sums",
    )(half.reshape(1), *em, *xs, *stats)


def gather_plan(samples, centroids, move_target, fetch_ids, cand):
    rows = samples.shape[3]
    width = samples.shape[4]
    slots_in = samples.shape[2]
    bal = cand.shape[2]
    lists = cand.shape[3]
    owned = centroids.shape[0] // rows
    peers = lax.axis_size("wide")
    myself = lax.axis_index("wide")
    rep = lax.axis_index("rep")
    sub = lax.axis_index("sub")
    tau = 2.0 * math.sqrt(D)
    handed = slots_in - bal
    base = bal - handed
    span = rows // 2
    lanes = bal * span

    blocks = samples.reshape(slots_in, rows, width)
    mine = lax.dynamic_slice_in_dim(blocks, sub * span, span, 1)
    theirs = lax.dynamic_slice_in_dim(blocks, (1 - sub) * span, span, 1)
    full = jnp.concatenate([mine, swapped(theirs, "sub")], axis=2)
    cent_own = centroids.astype(jnp.bfloat16)
    cent = jnp.concatenate([cent_own, swapped(cent_own, "sub")], axis=1)
    cent_sq = jnp.sum(jnp.square(cent.astype(jnp.float32)), axis=1, keepdims=True)
    cent_sq = jnp.broadcast_to(cent_sq, (owned * rows, 128))

    target = move_target.reshape(slots_in)
    ids = fetch_ids.reshape(-1)
    listed = cand.reshape(bal * lists)
    pool_range = jnp.arange(ids.shape[0], dtype=jnp.int32)
    global_ids = jnp.sum(jnp.where(listed[:, None] == pool_range[None, :], ids[None, :], 0), axis=1)
    facts_own = jnp.concatenate([target, global_ids])
    facts = jnp.stack([facts_own] + [passed_along(facts_own, "wide", k) for k in range(1, peers)])
    targets = facts[:, :slots_in]
    ids_all = facts[:, slots_in:].reshape(peers, bal, lists)
    came = jnp.stack(
        [jnp.roll(targets[:, bal + h], -(h + 1), axis=0) for h in range(handed)], axis=1
    )
    got = came >= 0
    kept = targets[:, :bal]
    live = kept >= 0
    before = jnp.arange(bal)[None, :] < jnp.arange(bal)[:, None]
    rank = jnp.sum((live[:, None, :] & before[None]).astype(jnp.int32), axis=2)
    before_h = jnp.arange(handed)[None, :] < jnp.arange(handed)[:, None]
    free_rank = jnp.sum(((~got)[:, None, :] & before_h[None]).astype(jnp.int32), axis=2)
    want = jnp.concatenate(
        [jnp.broadcast_to(jnp.arange(base, dtype=jnp.int32), (peers, base)), base + free_rank],
        axis=1,
    )
    match = live[:, None, :] & (rank[:, None, :] == want[:, :, None])
    kept_slot = jnp.sum(jnp.where(match, kept[:, None, :] % bal + 1, 0), axis=2) - 1
    last_slot = jnp.where(got, came % bal, kept_slot[:, base:])
    slot_at = jnp.concatenate([kept_slot[:, :base], last_slot], axis=1)
    source = jnp.sum(jnp.where(match[0], jnp.arange(bal, dtype=jnp.int32)[None, :], 0), axis=1)
    my_blocks = myself * owned + jnp.arange(owned, dtype=jnp.int32)
    times = jnp.sum((ids_all[:, :, :, None] == my_blocks).astype(jnp.int32), axis=2)
    at_slot = slot_at[:, :, None] == jnp.arange(bal, dtype=jnp.int32)
    mult = jnp.sum(jnp.where(at_slot[..., None], times[:, None, :, :], 0), axis=2)
    mult = jnp.swapaxes(mult, 1, 2)

    came_blocks = jnp.stack([passed_along(full[bal + h], "wide", h + 1) for h in range(handed)])
    packed = jnp.take(full[:bal], source, axis=0)
    packed = jnp.concatenate(
        [packed[:base], jnp.where(got[0][:, None, None], came_blocks, packed[base:])], axis=0
    )
    work = packed.reshape(lanes, 2 * width)
    xs = [work] + [passed_along(work, "wide", k) for k in range(1, peers)]

    em = []
    stats = []
    for k in range(peers):
        em_k, stats_k = score_chunk(mult[k], xs[k], cent, cent_sq, span, tau)
        em.append(em_k)
        stats.append(stats_k)
    local = jnp.concatenate(stats, axis=1)
    all_stats = [local] + [passed_along(local, "wide", k) for k in range(1, peers)]

    own_far, other_far = half_sums(1 - rep, em, xs, all_stats)
    far = (own_far + swapped(other_far, "sub").astype(jnp.float32)).astype(jnp.bfloat16)
    came_far = swapped(far, "rep")
    own_near, other_near = half_sums(rep, em, xs, all_stats)
    near = own_near + swapped(other_near, "sub").astype(jnp.float32)
    total = near + came_far.astype(jnp.float32)
    share = owned * rows // 2
    previous = lax.dynamic_slice_in_dim(centroids, rep * share, share, 0)
    fresh = (total[:share] + PRIOR * previous) / (total[share][:, None] + PRIOR)

    parts = [all_stats[k][:, (-k) % peers * lanes :][:, :lanes] for k in range(peers)]
    top, denom = combine(parts)
    work_sq = jnp.sum(jnp.square(work.astype(jnp.float32)), axis=1)
    energy = -tau * (top[0] - work_sq / tau + jnp.log(denom[0])) / D
    energy = energy.reshape(bal, span)
    place = slot_at[0][None, :] == jnp.arange(bal, dtype=jnp.int32)[:, None]
    energy = jnp.sum(jnp.where(place[:, :, None], energy[None], 0.0), axis=1)
    return (fresh, energy.reshape(1, 1, bal, span))


def body(samples, centroids, move_target, fetch_ids, cand):
    peers = lax.axis_size("wide")
    pairs = lax.axis_size("rep") == 2 and lax.axis_size("sub") == 2
    if pairs and peers * cand.shape[2] <= 2 * fetch_ids.shape[2]:
        return gather_plan(samples, centroids, move_target, fetch_ids, cand)
    return exchange_plan(samples, centroids, move_target, fetch_ids, cand)


def solution(mesh):
    return jax.shard_map(
        body,
        mesh=mesh,
        in_specs=(
            P(("groups", "wide"), "rep", None, None, "sub"),
            P(("groups", "wide"), "sub"),
            P(("groups", "wide"), "rep", None),
            P(("groups", "wide"), "rep", None),
            P(("groups", "wide"), "rep", None, None),
        ),
        out_specs=(P(("groups", "wide", "rep"), "sub"), P(("groups", "wide"), "rep", None, "sub")),
        check_vma=False,
    )
```

```python
import math

import jax
import jax.numpy as jnp
from jax import lax
from jax.experimental import pallas as pl
from jax.experimental.pallas import tpu as pltpu
from jax.sharding import PartitionSpec as P

D = 1024


PRIOR = 1.0


def passed_along(value, axis, steps):
    count = lax.axis_size(axis)
    pairs = [(source, (source + steps) % count) for source in range(count)]
    return lax.ppermute(value, axis, pairs)


def pick_rows(table, index, present):
    picked = jnp.take(table, jnp.maximum(index, 0), axis=0)
    shape = (present.shape[0],) + (1,) * (picked.ndim - 1)
    return jnp.where(present.reshape(shape), picked, jnp.zeros_like(picked))


def soften(scores, tau):
    logits = scores / tau
    top = jnp.max(logits, axis=-1, keepdims=True)
    expo = jnp.exp(logits - top)
    total = jnp.sum(expo, axis=-1, keepdims=True)
    weights = (expo / total).astype(jnp.bfloat16)
    energy = -tau * (top[..., 0] + jnp.log(total[..., 0])) / D
    return (weights, energy)


def exchange_plan(samples, centroids, move_target, fetch_ids, cand):
    rows = samples.shape[3]
    width = samples.shape[4]
    slots_in = samples.shape[2]
    bal = cand.shape[2]
    lists = cand.shape[3]
    pool = fetch_ids.shape[2]
    owned = centroids.shape[0] // rows
    peers = lax.axis_size("wide")
    myself = lax.axis_index("wide")
    cap = max(1, 3 * pool // (2 * peers))
    tau = 2.0 * math.sqrt(D)
    handed = slots_in - bal
    blocks = samples.reshape(slots_in, rows, width)
    target = move_target.reshape(slots_in)
    dest = jnp.where(target >= 0, target // bal, -1)
    dest_slot = jnp.where(target >= 0, target % bal, -1)
    got_list = []
    slot_list = []
    for step in range(handed):
        entry = bal + step
        present = target[entry] >= 0
        send_block = jnp.where(present, blocks[entry], jnp.zeros_like(blocks[entry]))[None]
        send_slot = jnp.where(present, target[entry] % bal, -1).reshape(1)
        got_block, got_slot = passed_along((send_block, send_slot), "wide", step + 1)
        got_list.append(got_block)
        slot_list.append(got_slot)
    ids = fetch_ids.reshape(pool)
    owner = ids // owned
    local = ids % owned
    before = jnp.arange(pool)[None, :] < jnp.arange(pool)[:, None]
    position = jnp.sum(((owner[None, :] == owner[:, None]) & before).astype(jnp.int32), axis=1)
    slot_of = owner * cap + position
    slot_match = slot_of[None, :] == jnp.arange(peers * cap, dtype=jnp.int32)[:, None]
    slot_used = jnp.any(slot_match, axis=1)
    slot_item = jnp.sum(
        jnp.where(slot_match, jnp.arange(pool, dtype=jnp.int32)[None, :], 0), axis=1
    )
    asks = jnp.where(slot_used, jnp.take(local, slot_item), -1).reshape(peers, cap)
    wanted = lax.all_to_all(asks, "wide", split_axis=0, concat_axis=0, tiled=True)
    table = centroids.reshape(owned, rows, width)
    table_half = table.astype(jnp.bfloat16)
    wanted_flat = wanted.reshape(peers * cap)
    reply = pick_rows(table_half, wanted_flat, wanted_flat >= 0).reshape(peers, cap, rows, width)
    answered = lax.all_to_all(reply, "wide", split_axis=0, concat_axis=0, tiled=True)
    fetched = jnp.take(answered.reshape(peers * cap, rows, width), slot_of, axis=0)
    keep_here = dest == myself
    source_blocks = jnp.concatenate([blocks] + got_list, axis=0)
    source_slots = jnp.concatenate([jnp.where(keep_here, dest_slot, -1)] + slot_list, axis=0)
    fill_match = source_slots[None, :] == jnp.arange(bal, dtype=jnp.int32)[:, None]
    live = jnp.any(fill_match, axis=1)
    anchor = jnp.sum(
        jnp.where(fill_match, jnp.arange(slots_in + handed, dtype=jnp.int32)[None, :], 0), axis=1
    )
    work = pick_rows(source_blocks, anchor, live)
    flat_lists = cand.reshape(bal * lists)
    fetched_sq = jnp.sum(jnp.square(fetched.astype(jnp.float32)), axis=-1)

    def slot_scores(carry, items):
        work_one, lists_one = items
        chosen = jnp.take(fetched, lists_one, axis=0).reshape(lists * rows, width)
        dots = jnp.dot(work_one, chosen.T, preferred_element_type=jnp.float32)
        cent_sq = jnp.take(fetched_sq, lists_one, axis=0).reshape(lists * rows)
        work_sq = jnp.sum(jnp.square(work_one.astype(jnp.float32)), axis=-1)
        return (carry, 2.0 * dots - cent_sq[None, :] - work_sq[:, None])

    unused, partial_scores = lax.scan(slot_scores, 0, (work, cand.reshape(bal, lists)))
    half = rows // lax.axis_size("sub")
    lowest = lax.axis_index("sub") * half
    scores = lax.psum(partial_scores, "sub")
    weights, energy = soften(scores, tau)
    energy = lax.dynamic_slice_in_dim(energy, lowest, half, 1)
    weights = jnp.where(live[:, None, None], weights, jnp.zeros_like(weights))
    energy = jnp.where(live[:, None], energy, jnp.zeros_like(energy))
    pool_range = jnp.arange(pool, dtype=jnp.int32)

    def slot_sums(total, items):
        weights_one, work_one, lists_one = items
        term = jnp.dot(weights_one.T, work_one, preferred_element_type=jnp.float32).reshape(
            lists, rows * width
        )
        hot = (lists_one[None, :] == pool_range[:, None]).astype(jnp.float32)
        return (total + jnp.dot(hot, term, precision=lax.Precision.HIGHEST), 0)

    start_sums = jnp.zeros((pool, rows * width), jnp.float32)
    pooled, unused_two = lax.scan(slot_sums, start_sums, (weights, work, cand.reshape(bal, lists)))
    pool_sums = pooled.astype(jnp.bfloat16)
    mass = jnp.sum(weights.astype(jnp.float32), axis=1).reshape(bal * lists, rows)
    onehot = (flat_lists[None, :] == pool_range[:, None]).astype(jnp.float32)
    pool_mass = jnp.dot(onehot, mass, precision=lax.Precision.HIGHEST).astype(jnp.bfloat16)
    back_sums = pick_rows(pool_sums, slot_item, slot_used).reshape(peers, cap, rows, width)
    back_mass = pick_rows(pool_mass, slot_item, slot_used).reshape(peers, cap, rows)
    came_sums, came_mass = (
        lax.all_to_all(back_sums, "wide", split_axis=0, concat_axis=0, tiled=True),
        lax.all_to_all(back_mass, "wide", split_axis=0, concat_axis=0, tiled=True),
    )
    owner_hot = (wanted_flat[None, :] == jnp.arange(owned, dtype=jnp.int32)[:, None]).astype(
        jnp.bfloat16
    )
    owner_sums = jnp.dot(
        owner_hot, came_sums.reshape(peers * cap, rows * width), preferred_element_type=jnp.float32
    )
    owner_mass = jnp.dot(
        owner_hot, came_mass.reshape(peers * cap, rows), preferred_element_type=jnp.float32
    )
    share_sums, share_mass = (
        lax.psum_scatter(
            owner_sums.reshape(owned, rows, width).astype(jnp.bfloat16),
            "rep",
            scatter_dimension=0,
            tiled=True,
        ).astype(jnp.float32),
        lax.psum_scatter(
            owner_mass.astype(jnp.bfloat16), "rep", scatter_dimension=0, tiled=True
        ).astype(jnp.float32),
    )
    share = share_sums.shape[0]
    first_block = lax.axis_index("rep") * share
    previous = lax.dynamic_slice_in_dim(table, first_block, share, 0)
    fresh = (share_sums + PRIOR * previous) / (share_mass[:, :, None] + PRIOR)
    return (fresh.reshape(share * rows, width), energy.reshape(1, 1, bal, half))


LOW = -1e30
MEGA = 2**20
PAD = 16
HBM = pl.BlockSpec(memory_space=pl.ANY)
VMEM = pl.BlockSpec(memory_space=pltpu.VMEM)
SMEM = pl.BlockSpec(memory_space=pltpu.SMEM)


def swapped(value, axis):
    return lax.ppermute(value, axis, [(0, 1), (1, 0)])


def paired(value, flip):
    count = lax.axis_size("wide")
    return lax.ppermute(value, "wide", [(w, w ^ flip) for w in range(count)])


def after(value, *others):
    return lax.optimization_barrier((value, *others))[0]


def shape(dims, dtype=jnp.float32):
    return jax.ShapeDtypeStruct(dims, dtype)


def call(kernel, name, in_specs, args, outs, scratch=(), out_specs=None):
    return pl.pallas_call(
        kernel,
        in_specs=in_specs,
        out_specs=out_specs or [VMEM] * len(outs),
        out_shape=outs,
        scratch_shapes=scratch,
        compiler_params=pltpu.CompilerParams(vmem_limit_bytes=16 * MEGA),
        cost_estimate=pl.CostEstimate(flops=1, bytes_accessed=1, transcendentals=0),
        name=name,
    )(*args)


def bias_kernel(facts_ref, bias_ref, logs_ref, *, slots_in, pool, bal, lists, owned, flips):
    pair_x, pair_c = flips
    peers = facts_ref.shape[0]
    me = lax.axis_index("wide")
    logs_ref[0] = jnp.float32(LOW)
    for m in range(1, lists + 1):
        logs_ref[m] = jnp.float32(math.log(m))

    def entry(at, unused):
        k, e = at // slots_in, at % slots_in
        source = jnp.where(k == 0, me, me ^ pair_x)
        target = facts_ref[(me - source) % peers, e]
        live = target >= 0
        target = jnp.maximum(target, 0)
        row = (me - target // bal) % peers
        first = slots_in + pool + (target % bal) * lists
        listed = [facts_ref[row, slots_in + facts_ref[row, first + j]] for j in range(lists)]
        for s in range(2):
            owner = me if s == 0 else me ^ pair_c
            for g in range(owned):
                times = jnp.int32(0)
                for block in listed:
                    times = times + jnp.where(block == owner * owned + g, 1, 0)
                bias_ref[k, (s * owned + g) * slots_in + e] = logs_ref[jnp.where(live, times, 0)]
        return unused

    lax.fori_loop(0, 2 * slots_in, entry, 0)


def tiles(lanes):
    return [(lo, min(256, lanes - lo)) for lo in range(0, lanes, 256)]


def score_kernel(bias_ref, *refs, pieces, first, span, chunk, entries):
    x_refs = refs[:pieces]
    c_refs = refs[pieces : pieces + 6]
    em_refs = refs[pieces + 6 : pieces + 8]
    stats_ref, logits_ref = refs[pieces + 8 :]
    count = bias_ref.shape[1] // (2 * entries)
    rows = logits_ref.shape[1] // count
    width = c_refs[0].shape[1]
    dims = (((1,), (1,)), ((), ()))
    turn = 0
    base = 0
    for x_ref in x_refs:
        for lo, size in tiles(x_ref.shape[0]):
            out = base + lo
            place = lax.broadcasted_iota(jnp.int32, (1, size), 1) // span
            for s in range(2):
                c_own_ref, c_oth_ref, csq_ref = c_refs[3 * s : 3 * s + 3]
                em_ref = em_refs[s]
                buf = logits_ref.at[turn % 2]
                turn += 1
                buf[:, 0:size] = lax.dot_general(
                    c_own_ref[...], x_ref[lo : lo + size, 0:width], dims,
                    preferred_element_type=jnp.float32,
                ) + lax.dot_general(
                    c_oth_ref[...], x_ref[lo : lo + size, width:], dims,
                    preferred_element_type=jnp.float32,
                )
                best = jnp.full((8, size), 2 * LOW, jnp.float32)
                for g in range(count):
                    bias = jnp.zeros((1, size), jnp.float32)
                    for p in range(size // span):
                        at = (s * count + g) * entries + first + out // span + p
                        bias = jnp.where(place == p, bias_ref[chunk, at], bias)
                    block = pl.ds(g * rows, rows)
                    less = jnp.concatenate([csq_ref[block, :]] * (size // 128), axis=1)
                    logits = (buf[block, 0:size] - less) + bias
                    buf[block, 0:size] = logits
                    best = jnp.maximum(best, jnp.max(logits.reshape(rows // 8, 8, size), axis=0))
                top = jnp.max(best, axis=0, keepdims=True)
                total = jnp.zeros((8, size), jnp.float32)
                for g in range(count):
                    block = pl.ds(g * rows, rows)
                    expo = jnp.exp(buf[block, 0:size] - top)
                    em_ref[block, out : out + size] = expo.astype(jnp.bfloat16)
                    total = total + jnp.sum(expo.reshape(rows // 8, 8, size), axis=0)
                stats_ref[2 * s : 2 * s + 1, out : out + size] = top
                stats_ref[2 * s + 1 : 2 * s + 2, out : out + size] = jnp.sum(
                    total, axis=0, keepdims=True
                )
        base += x_ref.shape[0]


def score(bias, chunk, xs, sets, first, span, entries):
    lanes = sum(x.shape[0] for x in xs)
    cols = sets[0][0].shape[0]
    return call(
        lambda *refs: score_kernel(
            *refs, pieces=len(xs), first=first, span=span, chunk=chunk, entries=entries
        ),
        "scores",
        [SMEM] + [VMEM] * (len(xs) + 6),
        [bias, *xs, *sets[0], *sets[1]],
        [shape((cols, lanes), jnp.bfloat16)] * 2 + [shape((4, lanes))],
        [pltpu.VMEM((2, cols, 256), jnp.float32)],
    )


def combine(parts):
    top = parts[0][0:1]
    for part in parts[1:]:
        top = jnp.maximum(top, part[0:1])
    total = jnp.zeros_like(top)
    for part in parts:
        total = total + part[1:2] * jnp.exp(part[0:1] - top)
    return top, total


def chunk_parts(mine, peer, chunk):
    other = 1 - chunk
    return [
        mine[4 * chunk : 4 * chunk + 2],
        mine[4 * chunk + 2 : 4 * chunk + 4],
        peer[4 * other : 4 * other + 2],
        peer[4 * other + 2 : 4 * other + 4],
    ]


def half_rows(mine, count):
    rep = lax.axis_index("rep")
    return pl.ds(pl.multiple_of((rep if mine else 1 - rep) * count, count), count)


def weighted(mine_ref, peer_ref, em_refs, x_refs, rows, cols, which, mass):
    stats, peer = mine_ref[...], peer_ref[...]
    count = rows.size
    total = jnp.zeros((count, cols.stop - cols.start), jnp.float32)
    masses = jnp.zeros((count, 128), jnp.float32)
    pieces = [(0, em_refs[0], x_refs[0:2]), (1, em_refs[1], x_refs[2:3]), (1, em_refs[2], x_refs[3:4])]
    lo = 0
    for at, (chunk, em_ref, xs) in enumerate(pieces):
        parts = chunk_parts(stats, peer, chunk)
        top, denom = combine(parts)
        factor = jnp.where(top > 0.5 * LOW, jnp.exp(parts[which][0:1] - top) / denom, 0.0)
        lo = lo if at == 2 else 0
        size = em_ref.shape[1]
        scaled = em_ref[rows, :].astype(jnp.float32) * factor[:, lo : lo + size]
        weights = scaled.astype(jnp.bfloat16)
        if mass:
            wide = weights.astype(jnp.float32)
            for lane in range(0, size, 128):
                masses = masses + wide[:, lane : lane + 128]
        lo += size
        begin = 0
        for x_ref in xs:
            end = begin + x_ref.shape[0]
            total = total + jnp.dot(
                weights[:, begin:end], x_ref[:, cols], preferred_element_type=jnp.float32
            )
            begin = end
    return total, masses


def far_kernel(*refs, which, mine):
    stats_ref, peer_ref = refs[0:2]
    em_refs, x_refs, (far_ref, mass_ref) = refs[2:5], refs[5:9], refs[9:]
    count, width = far_ref.shape[0] - PAD, far_ref.shape[1]
    total, masses = weighted(
        stats_ref, peer_ref, em_refs, x_refs, half_rows(mine, count), slice(width, 2 * width), which, True
    )
    masses = jnp.broadcast_to(jnp.sum(masses, axis=1, keepdims=True), (count, 128)).T[0:PAD]
    far_ref[0:count, :] = total.astype(jnp.bfloat16)
    far_ref[count:, :] = masses.astype(jnp.bfloat16)
    mass_ref[...] = masses


def near_kernel(*refs, which, mine, final):
    stats_ref, peer_ref = refs[0:2]
    em_refs, x_refs, (mass_ref, came_ref) = refs[2:5], refs[5:9], refs[9:11]
    out_ref = refs[12] if final else refs[11]
    count, width = out_ref.shape[0] - PAD, out_ref.shape[1]
    if final:
        previous_ref, sem = refs[13:]
        copy = pltpu.make_async_copy(refs[11].at[half_rows(mine, count), :], previous_ref, sem)
        copy.start()
    total, unused = weighted(
        stats_ref, peer_ref, em_refs, x_refs, half_rows(mine, count), slice(0, width), which, False
    )
    came = came_ref[...].astype(jnp.float32)
    total = total + came[0:count]
    masses = mass_ref[...] + came[count:]
    if final:
        copy.wait()
        total = total + PRIOR * previous_ref[...]
        masses = masses + PRIOR
    out_ref[0:count, :] = total.astype(out_ref.dtype)
    out_ref[count:, :] = masses.astype(out_ref.dtype)


def far_sums(stats, peer, em, xs, which, mine):
    count, width = em[0].shape[0] // 2, xs[0].shape[1] // 2
    return call(
        lambda *refs: far_kernel(*refs, which=which, mine=mine),
        "far",
        [VMEM] * 9,
        [stats, peer, *em, *xs],
        [shape((count + PAD, width), jnp.bfloat16), shape((PAD, width))],
    )


def near_sums(stats, peer, em, xs, which, mine, mass, came, dtype, previous=None):
    count, width = em[0].shape[0] // 2, xs[0].shape[1] // 2
    final = previous is not None
    return call(
        lambda *refs: near_kernel(*refs, which=which, mine=mine, final=final),
        "near",
        [VMEM] * 11 + [HBM] * final,
        [stats, peer, *em, *xs, mass, came] + [previous] * final,
        [shape((count + PAD, width), dtype)],
        [pltpu.VMEM((count, width), jnp.float32), pltpu.SemaphoreType.DMA] * final,
    )[0]


def add_kernel(a_ref, b_ref, out_ref):
    out_ref[...] = (a_ref[...] + b_ref[...].astype(jnp.float32)).astype(out_ref.dtype)


def final_kernel(sums_ref, rep_ref, back_ref, out_ref):
    count = out_ref.shape[0]
    sums = sums_ref[...] + rep_ref[...].astype(jnp.float32) + back_ref[...].astype(jnp.float32)
    mass = jnp.broadcast_to(sums[count : count + 1], (128, count)).T
    mass = jnp.concatenate([mass] * (out_ref.shape[1] // 128), axis=1)
    out_ref[...] = sums[0:count] / mass


def energy_kernel(stats_ref, peer_ref, square_ref, out_ref, *last_refs, tau, span):
    top, denom = combine(chunk_parts(stats_ref[...], peer_ref[...], 0))
    energy = -tau * (top - square_ref[...] / tau + jnp.log(denom)) / D
    entries = energy.shape[1] // span
    out_ref[...] = jnp.zeros_like(out_ref)
    for e in range(entries):
        part = energy[:, e * span : (e + 1) * span]
        out_ref[e : e + 1, :] = part
        back = e - (entries - len(last_refs))
        if back >= 0:
            last_refs[back][...] = jnp.broadcast_to(part, last_refs[back].shape)


def place_kernel(facts_ref, energy_ref, *refs, bal):
    came_refs, out_ref = refs[:-1], refs[-1]
    me = lax.axis_index("wide")
    out_ref[...] = jnp.zeros_like(out_ref)

    def put(target, row):
        @pl.when((target >= 0) & (target // bal == me))
        def _():
            out_ref[pl.ds(target % bal, 1), :] = row

    for e in range(bal):
        put(facts_ref[0, e], energy_ref[e : e + 1, :])
    for h, came_ref in enumerate(came_refs):
        put(facts_ref[h + 1, bal + h], came_ref[0:1, :])


def grid_plan(samples, centroids, move_target, fetch_ids, cand):
    rows = samples.shape[3]
    width = samples.shape[4]
    slots_in = samples.shape[2]
    bal = cand.shape[2]
    lists = cand.shape[3]
    pool = fetch_ids.shape[2]
    owned = centroids.shape[0] // rows
    peers = lax.axis_size("wide")
    sub = lax.axis_index("sub")
    tau = 2.0 * math.sqrt(D)
    handed = slots_in - bal
    span = rows // 2
    lanes = slots_in * span
    cut = bal * span
    pair_x, pair_c = 2, 1

    c0_own = (centroids * (2.0 / tau)).astype(jnp.bfloat16)
    c0_oth = swapped(c0_own, "sub")
    c1_own = paired(c0_own, pair_c)

    facts_own = jnp.concatenate(
        [move_target.reshape(slots_in), fetch_ids.reshape(pool), cand.reshape(bal * lists)]
    )
    facts = jnp.stack([facts_own] + [passed_along(facts_own, "wide", k) for k in range(1, peers)])
    bias = call(
        lambda *refs: bias_kernel(
            *refs, slots_in=slots_in, pool=pool, bal=bal, lists=lists, owned=owned, flips=(pair_x, pair_c)
        ),
        "bias",
        [SMEM],
        [facts],
        [shape((2, 2 * owned * slots_in))],
        [pltpu.SMEM((lists + 1,), jnp.float32)],
        [SMEM],
    )[0]

    blocks = samples.reshape(slots_in, rows, width)
    give = lax.dynamic_slice_in_dim(blocks, (1 - sub) * span, span, 1).reshape(lanes, width)
    took = swapped(give, "sub")
    own = lax.dynamic_slice_in_dim(blocks, sub * span, span, 1).reshape(lanes, width)
    full = jnp.concatenate([own, took], axis=1)
    x0 = (full[:cut], full[cut:])
    x1a = paired(x0[0], pair_x)
    c1_own, x1a, bias = lax.optimization_barrier((c1_own, x1a, bias))
    x1b = paired(after(x0[1], c1_own), pair_x)
    c1_oth = swapped(c1_own, "sub")

    def squares(*parts):
        total = sum(jnp.sum(jnp.square(part.astype(jnp.float32)), axis=1, keepdims=True) for part in parts)
        return jnp.broadcast_to(total * (tau / 4.0), (owned * rows, 128))

    work_sq = jnp.sum(jnp.square(full.astype(jnp.float32)), axis=1).reshape(1, lanes)
    sets = ((c0_own, c0_oth, squares(c0_own, c0_oth)), (c1_own, c1_oth, squares(c1_own, c1_oth)))

    *em0, stats0 = score(bias, 0, x0, sets, 0, span, slots_in)
    *em1a, stats1a = score(bias, 1, [x1a], sets, 0, span, slots_in)
    *em1b, stats1b = score(bias, 1, [x1b], sets, bal, span, slots_in)
    em = list(zip(em0, em1a, em1b))
    stats = jnp.concatenate([stats0, jnp.concatenate([stats1a, stats1b], axis=1)], axis=0)
    peer = paired(stats, pair_x)

    xs = (*x0, x1a, x1b)
    half = jnp.bfloat16
    far_a, mass_a = far_sums(stats, peer, em[1], xs, 1, False)
    far_b, mass_b = far_sums(after(stats, far_a), peer, em[1], xs, 1, True)
    came = swapped(far_a, "sub")
    sent_a = near_sums(after(stats, far_b), peer, em[1], xs, 1, False, mass_a, came, half)
    came_a = swapped(sent_a, "rep")
    came = swapped(far_b, "sub")
    part_b = near_sums(after(stats, sent_a), peer, em[1], xs, 1, True, mass_b, came, jnp.float32)

    far_c, mass_c = far_sums(after(stats, part_b), peer, em[0], xs, 0, False)
    far_d, mass_d = far_sums(after(stats, far_c), peer, em[0], xs, 0, True)
    came = swapped(far_c, "sub")
    sent_c = near_sums(after(stats, far_d), peer, em[0], xs, 0, False, mass_c, came, half)
    came_c = swapped(sent_c, "rep")
    came = swapped(far_d, "sub")
    part_d = near_sums(
        after(stats, sent_c), peer, em[0], xs, 0, True, mass_d, came, jnp.float32, centroids
    )

    back = call(add_kernel, "add", [VMEM] * 2, [part_b, came_a], [shape(part_b.shape, half)])[0]
    came_back = paired(back, pair_c)
    fresh = call(
        final_kernel, "final", [VMEM] * 3, [part_d, came_c, came_back], [shape((owned * rows // 2, width))]
    )[0]

    energy, *last = call(
        lambda *refs: energy_kernel(*refs, tau=tau, span=span),
        "energy",
        [VMEM] * 3,
        [after(stats, part_d), peer, work_sq],
        [shape((slots_in, span))] + [shape((8, span))] * handed,
    )
    came = [passed_along(last[h], "wide", h + 1) for h in range(handed)]
    energy = call(
        lambda *refs: place_kernel(*refs, bal=bal),
        "place",
        [SMEM] + [VMEM] * (1 + handed),
        [facts, energy, *came],
        [shape((bal, span))],
    )[0]
    return (fresh, energy.reshape(1, 1, bal, span))


def body(samples, centroids, move_target, fetch_ids, cand):
    sizes = [lax.axis_size(axis) for axis in ("wide", "rep", "sub")]
    if sizes == [4, 2, 2]:
        return grid_plan(samples, centroids, move_target, fetch_ids, cand)
    return exchange_plan(samples, centroids, move_target, fetch_ids, cand)


def solution(mesh):
    return jax.shard_map(
        body,
        mesh=mesh,
        in_specs=(
            P(("groups", "wide"), "rep", None, None, "sub"),
            P(("groups", "wide"), "sub"),
            P(("groups", "wide"), "rep", None),
            P(("groups", "wide"), "rep", None),
            P(("groups", "wide"), "rep", None, None),
        ),
        out_specs=(P(("groups", "wide", "rep"), "sub"), P(("groups", "wide"), "rep", None, "sub")),
        check_vma=False,
    )
```

```python
import math

import jax
import jax.numpy as jnp
from jax import lax
from jax.experimental import pallas as pl
from jax.experimental.pallas import tpu as pltpu
from jax.sharding import PartitionSpec as P

D = 1024


PRIOR = 1.0


def passed_along(value, axis, steps):
    count = lax.axis_size(axis)
    pairs = [(source, (source + steps) % count) for source in range(count)]
    return lax.ppermute(value, axis, pairs)


def pick_rows(table, index, present):
    picked = jnp.take(table, jnp.maximum(index, 0), axis=0)
    shape = (present.shape[0],) + (1,) * (picked.ndim - 1)
    return jnp.where(present.reshape(shape), picked, jnp.zeros_like(picked))


def soften(scores, tau):
    logits = scores / tau
    top = jnp.max(logits, axis=-1, keepdims=True)
    expo = jnp.exp(logits - top)
    total = jnp.sum(expo, axis=-1, keepdims=True)
    weights = (expo / total).astype(jnp.bfloat16)
    energy = -tau * (top[..., 0] + jnp.log(total[..., 0])) / D
    return (weights, energy)


def exchange_plan(samples, centroids, move_target, fetch_ids, cand):
    rows = samples.shape[3]
    width = samples.shape[4]
    slots_in = samples.shape[2]
    bal = cand.shape[2]
    lists = cand.shape[3]
    pool = fetch_ids.shape[2]
    owned = centroids.shape[0] // rows
    peers = lax.axis_size("wide")
    myself = lax.axis_index("wide")
    cap = max(1, 3 * pool // (2 * peers))
    tau = 2.0 * math.sqrt(D)
    handed = slots_in - bal
    blocks = samples.reshape(slots_in, rows, width)
    target = move_target.reshape(slots_in)
    dest = jnp.where(target >= 0, target // bal, -1)
    dest_slot = jnp.where(target >= 0, target % bal, -1)
    got_list = []
    slot_list = []
    for step in range(handed):
        entry = bal + step
        present = target[entry] >= 0
        send_block = jnp.where(present, blocks[entry], jnp.zeros_like(blocks[entry]))[None]
        send_slot = jnp.where(present, target[entry] % bal, -1).reshape(1)
        got_block, got_slot = passed_along((send_block, send_slot), "wide", step + 1)
        got_list.append(got_block)
        slot_list.append(got_slot)
    ids = fetch_ids.reshape(pool)
    owner = ids // owned
    local = ids % owned
    before = jnp.arange(pool)[None, :] < jnp.arange(pool)[:, None]
    position = jnp.sum(((owner[None, :] == owner[:, None]) & before).astype(jnp.int32), axis=1)
    slot_of = owner * cap + position
    slot_match = slot_of[None, :] == jnp.arange(peers * cap, dtype=jnp.int32)[:, None]
    slot_used = jnp.any(slot_match, axis=1)
    slot_item = jnp.sum(
        jnp.where(slot_match, jnp.arange(pool, dtype=jnp.int32)[None, :], 0), axis=1
    )
    asks = jnp.where(slot_used, jnp.take(local, slot_item), -1).reshape(peers, cap)
    wanted = lax.all_to_all(asks, "wide", split_axis=0, concat_axis=0, tiled=True)
    table = centroids.reshape(owned, rows, width)
    table_half = table.astype(jnp.bfloat16)
    wanted_flat = wanted.reshape(peers * cap)
    reply = pick_rows(table_half, wanted_flat, wanted_flat >= 0).reshape(peers, cap, rows, width)
    answered = lax.all_to_all(reply, "wide", split_axis=0, concat_axis=0, tiled=True)
    fetched = jnp.take(answered.reshape(peers * cap, rows, width), slot_of, axis=0)
    keep_here = dest == myself
    source_blocks = jnp.concatenate([blocks] + got_list, axis=0)
    source_slots = jnp.concatenate([jnp.where(keep_here, dest_slot, -1)] + slot_list, axis=0)
    fill_match = source_slots[None, :] == jnp.arange(bal, dtype=jnp.int32)[:, None]
    live = jnp.any(fill_match, axis=1)
    anchor = jnp.sum(
        jnp.where(fill_match, jnp.arange(slots_in + handed, dtype=jnp.int32)[None, :], 0), axis=1
    )
    work = pick_rows(source_blocks, anchor, live)
    flat_lists = cand.reshape(bal * lists)
    fetched_sq = jnp.sum(jnp.square(fetched.astype(jnp.float32)), axis=-1)

    def slot_scores(carry, items):
        work_one, lists_one = items
        chosen = jnp.take(fetched, lists_one, axis=0).reshape(lists * rows, width)
        dots = jnp.dot(work_one, chosen.T, preferred_element_type=jnp.float32)
        cent_sq = jnp.take(fetched_sq, lists_one, axis=0).reshape(lists * rows)
        work_sq = jnp.sum(jnp.square(work_one.astype(jnp.float32)), axis=-1)
        return (carry, 2.0 * dots - cent_sq[None, :] - work_sq[:, None])

    unused, partial_scores = lax.scan(slot_scores, 0, (work, cand.reshape(bal, lists)))
    half = rows // lax.axis_size("sub")
    lowest = lax.axis_index("sub") * half
    scores = lax.psum(partial_scores, "sub")
    weights, energy = soften(scores, tau)
    energy = lax.dynamic_slice_in_dim(energy, lowest, half, 1)
    weights = jnp.where(live[:, None, None], weights, jnp.zeros_like(weights))
    energy = jnp.where(live[:, None], energy, jnp.zeros_like(energy))
    pool_range = jnp.arange(pool, dtype=jnp.int32)

    def slot_sums(total, items):
        weights_one, work_one, lists_one = items
        term = jnp.dot(weights_one.T, work_one, preferred_element_type=jnp.float32).reshape(
            lists, rows * width
        )
        hot = (lists_one[None, :] == pool_range[:, None]).astype(jnp.float32)
        return (total + jnp.dot(hot, term, precision=lax.Precision.HIGHEST), 0)

    start_sums = jnp.zeros((pool, rows * width), jnp.float32)
    pooled, unused_two = lax.scan(slot_sums, start_sums, (weights, work, cand.reshape(bal, lists)))
    pool_sums = pooled.astype(jnp.bfloat16)
    mass = jnp.sum(weights.astype(jnp.float32), axis=1).reshape(bal * lists, rows)
    onehot = (flat_lists[None, :] == pool_range[:, None]).astype(jnp.float32)
    pool_mass = jnp.dot(onehot, mass, precision=lax.Precision.HIGHEST).astype(jnp.bfloat16)
    back_sums = pick_rows(pool_sums, slot_item, slot_used).reshape(peers, cap, rows, width)
    back_mass = pick_rows(pool_mass, slot_item, slot_used).reshape(peers, cap, rows)
    came_sums, came_mass = (
        lax.all_to_all(back_sums, "wide", split_axis=0, concat_axis=0, tiled=True),
        lax.all_to_all(back_mass, "wide", split_axis=0, concat_axis=0, tiled=True),
    )
    owner_hot = (wanted_flat[None, :] == jnp.arange(owned, dtype=jnp.int32)[:, None]).astype(
        jnp.bfloat16
    )
    owner_sums = jnp.dot(
        owner_hot, came_sums.reshape(peers * cap, rows * width), preferred_element_type=jnp.float32
    )
    owner_mass = jnp.dot(
        owner_hot, came_mass.reshape(peers * cap, rows), preferred_element_type=jnp.float32
    )
    share_sums, share_mass = (
        lax.psum_scatter(
            owner_sums.reshape(owned, rows, width).astype(jnp.bfloat16),
            "rep",
            scatter_dimension=0,
            tiled=True,
        ).astype(jnp.float32),
        lax.psum_scatter(
            owner_mass.astype(jnp.bfloat16), "rep", scatter_dimension=0, tiled=True
        ).astype(jnp.float32),
    )
    share = share_sums.shape[0]
    first_block = lax.axis_index("rep") * share
    previous = lax.dynamic_slice_in_dim(table, first_block, share, 0)
    fresh = (share_sums + PRIOR * previous) / (share_mass[:, :, None] + PRIOR)
    return (fresh.reshape(share * rows, width), energy.reshape(1, 1, bal, half))


LOW = -1e30
FLOOR = -1e29
MEGA = 2**20
PAD = 16
SWAPS = 2
HBM = pl.BlockSpec(memory_space=pl.ANY)
VMEM = pl.BlockSpec(memory_space=pltpu.VMEM)
SMEM = pl.BlockSpec(memory_space=pltpu.SMEM)


def swapped(value, axis):
    return lax.ppermute(value, axis, [(0, 1), (1, 0)])


def paired(value, flip):
    count = lax.axis_size("wide")
    return lax.ppermute(value, "wide", [(w, w ^ flip) for w in range(count)])


def after(value, *others):
    return lax.optimization_barrier((value, *others))[0]


def shape(dims, dtype=jnp.float32):
    return jax.ShapeDtypeStruct(dims, dtype)


def call(kernel, name, in_specs, args, outs, scratch=(), needs=()):
    count = len(args)

    def run(*refs):
        kernel(*refs[:count], *refs[count + len(needs) :])

    return pl.pallas_call(
        run,
        in_specs=in_specs + [HBM] * len(needs),
        out_specs=[VMEM] * len(outs),
        out_shape=outs,
        scratch_shapes=scratch,
        compiler_params=pltpu.CompilerParams(vmem_limit_bytes=16 * MEGA),
        cost_estimate=pl.CostEstimate(flops=1, bytes_accessed=1, transcendentals=0),
        name=name,
    )(*args, *needs)


def bias_kernel(facts_ref, bias_ref, *, slots_in, pool, bal, lists, owned, flips, span):
    me = lax.axis_index("wide")
    lanes = slots_in * span
    row = lax.broadcasted_iota(jnp.int32, (2 * owned, 128), 0)
    block_id = jnp.where(row < owned, me * owned + row, (me ^ flips[1]) * owned + row - owned)
    place = lax.broadcasted_iota(jnp.int32, (1, 128), 1) // span
    for k in range(2):
        for lo in range(0, lanes, 128):
            listed = [jnp.full((1, 128), -1, jnp.int32) for j in range(lists)]
            for p in range(128 // span):
                target = facts_ref[flips[0] if k else 0, lo // span + p]
                live = target >= 0
                target = jnp.maximum(target, 0)
                source = me ^ (target // bal)
                first = slots_in + pool + (target % bal) * lists
                for j in range(lists):
                    block = facts_ref[source, slots_in + facts_ref[source, first + j]]
                    listed[j] = jnp.where(place == p, jnp.where(live, block, -1), listed[j])
            times = jnp.zeros((2 * owned, 128), jnp.float32)
            for j in range(lists):
                times = times + jnp.where(block_id == listed[j], 1.0, 0.0)
            logs = jnp.log(jnp.maximum(times, 1.0))
            bias_ref[k, :, lo : lo + 128] = jnp.where(times > 0, logs, LOW)


def join_kernel(own_ref, *refs):
    oth_refs, (c_ref, square_ref) = refs[:-2], refs[-2:]
    width = own_ref.shape[1]
    lo = 0
    for oth_ref in oth_refs:
        part = pl.ds(lo, oth_ref.shape[0])
        own, oth = own_ref[part, :], oth_ref[...]
        c_ref[part, 0:width] = own
        c_ref[part, width:] = oth
        total = jnp.zeros((part.size, 128), jnp.float32)
        for half in (own, oth):
            for lane in range(0, width, 128):
                piece = half[:, lane : lane + 128].astype(jnp.float32)
                total = total + piece * piece
        total = jnp.sum(total, axis=1, keepdims=True) * (math.sqrt(D) / 2.0)
        square_ref[part, :] = jnp.broadcast_to(total, (part.size, 128))
        lo += part.size


def joined(own, oths):
    count, width = own.shape
    outs = [shape((count, 2 * width), own.dtype), shape((count, 128))]
    return call(join_kernel, "join", [VMEM] * (1 + len(oths)), [own, *oths], outs)


def tiles(lanes):
    return [(lo, min(256, lanes - lo)) for lo in range(0, lanes, 256)]


def score_kernel(bias_ref, x_ref, c0_ref, csq0_ref, c1_ref, csq1_ref, *refs, chunk, first):
    before_refs, em_refs, (stats_ref, dots_ref) = refs[:-4], refs[-4:-2], refs[-2:]
    lead = 0
    for ref in before_refs:
        row, lane = 4 * (lead // stats_ref.shape[1]), lead % stats_ref.shape[1]
        stats_ref[row : row + 4, lane : lane + ref.shape[1]] = ref[...]
        lead += ref.shape[1]
    row, lane = 4 * (lead // stats_ref.shape[1]), lead % stats_ref.shape[1]
    count = bias_ref.shape[1] // 2
    rows = dots_ref.shape[1] // count
    turn = 0
    for lo, size in tiles(x_ref.shape[0]):
        for s, (c_ref, csq_ref) in enumerate(((c0_ref, csq0_ref), (c1_ref, csq1_ref))):
            part = slice(lo, lo + size)
            buf = dots_ref.at[turn % 2]
            turn += 1
            buf[:, 0:size] = lax.dot_general(
                c_ref[...], x_ref[part, :], (((1,), (1,)), ((), ())), preferred_element_type=jnp.float32
            )

            def logits(g):
                block = pl.ds(g * rows, rows)
                less = jnp.concatenate([csq_ref[block, :]] * (size // 128), axis=1)
                return (buf[block, 0:size] - less).reshape(rows // 8, 8, size)

            of_chunk = slice(first + lo, first + lo + size)
            bias = [bias_ref[chunk, s * count + g : s * count + g + 1, of_chunk] for g in range(count)]
            best = jnp.full((8, size), FLOOR, jnp.float32)
            for g in range(count):
                best = jnp.maximum(best, jnp.max(logits(g), axis=0) + bias[g])
            top = jnp.max(best, axis=0, keepdims=True)
            total = jnp.zeros((8, size), jnp.float32)
            for g in range(count):
                expo = jnp.exp(logits(g) + (bias[g] - top)[None])
                em_refs[s][pl.ds(g * rows, rows), part] = expo.reshape(rows, size).astype(jnp.bfloat16)
                total = total + jnp.sum(expo, axis=0)
            out = slice(lane + lo, lane + lo + size)
            stats_ref[row + 2 * s : row + 2 * s + 1, out] = top
            stats_ref[row + 2 * s + 1 : row + 2 * s + 2, out] = jnp.sum(total, axis=0, keepdims=True)


def score(bias, chunk, first, x, sets, before=()):
    cols = sets[0][0].shape[0]
    stats = shape((8, bias.shape[2]) if before else (4, x.shape[0]))
    return call(
        lambda *refs: score_kernel(*refs, chunk=chunk, first=first),
        "scores",
        [VMEM] * (6 + len(before)),
        [bias, x, *sets[0], *sets[1], *before],
        [shape((cols, x.shape[0]), jnp.bfloat16)] * 2 + [stats],
        [pltpu.VMEM((2, cols, 256), jnp.float32)],
    )


def combine(parts):
    top = parts[0][0:1]
    for part in parts[1:]:
        top = jnp.maximum(top, part[0:1])
    total = jnp.zeros_like(top)
    for part in parts:
        total = total + part[1:2] * jnp.exp(part[0:1] - top)
    return top, total


def chunk_parts(mine, peer, chunk):
    other = 1 - chunk
    return [
        mine[4 * chunk : 4 * chunk + 2],
        mine[4 * chunk + 2 : 4 * chunk + 4],
        peer[4 * other : 4 * other + 2],
        peer[4 * other + 2 : 4 * other + 4],
    ]


def half_rows(mine, count):
    rep = lax.axis_index("rep")
    return pl.ds(pl.multiple_of((rep if mine else 1 - rep) * count, count), count)


def weighted(mine_ref, peer_ref, em_refs, x_refs, rows, cols, which, mass):
    stats, peer = mine_ref[...], peer_ref[...]
    count = rows.size
    total = jnp.zeros((count, cols.stop - cols.start), jnp.float32)
    masses = jnp.zeros((count, 128), jnp.float32)
    lo = 0
    for em_ref, x_ref in zip(em_refs, x_refs):
        chunk, first = lo // stats.shape[1], lo % stats.shape[1]
        size = em_ref.shape[1]
        parts = chunk_parts(stats, peer, chunk)
        top, denom = combine(parts)
        factor = jnp.where(denom > 0, jnp.exp(parts[which][0:1] - top) / denom, 0.0)
        weights = (em_ref[rows, :].astype(jnp.float32) * factor[:, first : first + size]).astype(jnp.bfloat16)
        if mass:
            wide = weights.astype(jnp.float32)
            for lane in range(0, size, 128):
                masses = masses + wide[:, lane : lane + 128]
        total = total + jnp.dot(weights, x_ref[:, cols], preferred_element_type=jnp.float32)
        lo += size
    return total, masses


def far_kernel(*refs, which, mine):
    stats_ref, peer_ref = refs[0:2]
    em_refs, x_refs, (far_ref, mass_ref) = refs[2:5], refs[5:8], refs[8:]
    count, width = far_ref.shape[0] - PAD, far_ref.shape[1]
    total, masses = weighted(
        stats_ref, peer_ref, em_refs, x_refs, half_rows(mine, count), slice(width, 2 * width), which, True
    )
    masses = jnp.broadcast_to(jnp.sum(masses, axis=1, keepdims=True), (count, 128)).T[0:PAD]
    far_ref[0:count, :] = total.astype(jnp.bfloat16)
    far_ref[count:, :] = masses.astype(jnp.bfloat16)
    mass_ref[...] = masses


def near_kernel(*refs, which, mine, final, outs):
    stats_ref, peer_ref = refs[0:2]
    em_refs, x_refs, (mass_ref, *came_refs) = refs[2:5], refs[5:8], refs[8 : 9 + SWAPS]
    refs = refs[9 + SWAPS :]
    out_refs = refs[final : final + outs]
    count, width = sum(ref.shape[0] for ref in came_refs) - PAD, came_refs[0].shape[1]
    if final:
        previous_ref, sem = refs[1 + outs :]
        copy = pltpu.make_async_copy(refs[0].at[half_rows(mine, count), :], previous_ref, sem)
        copy.start()
    total, unused = weighted(
        stats_ref, peer_ref, em_refs, x_refs, half_rows(mine, count), slice(0, width), which, False
    )
    came = jnp.concatenate([ref[...] for ref in came_refs]).astype(jnp.float32)
    total = total + came[0:count]
    masses = mass_ref[...] + came[count:]
    if final:
        copy.wait()
        total = total + PRIOR * previous_ref[...]
        masses = masses + PRIOR
    lo = 0
    for out_ref in out_refs:
        size = min(out_ref.shape[0], count - lo)
        out_ref[0:size, :] = total[lo : lo + size].astype(out_ref.dtype)
        lo += size
    out_refs[-1][size:, :] = masses.astype(out_refs[-1].dtype)


def far_sums(stats, peer, em, xs, which, mine, needs=()):
    count, width = em[0].shape[0] // 2, xs[0].shape[1] // 2
    return call(
        lambda *refs: far_kernel(*refs, which=which, mine=mine),
        "far",
        [VMEM] * 8,
        [stats, peer, *em, *xs],
        [shape((count + PAD, width), jnp.bfloat16), shape((PAD, width))],
        needs=needs,
    )


def near_sums(stats, peer, em, xs, which, mine, mass, came, dtype, parts=(), previous=None, needs=()):
    count, width = em[0].shape[0] // 2, xs[0].shape[1] // 2
    final = previous is not None
    sizes = list(parts) + [count + PAD - sum(parts)]
    return call(
        lambda *refs: near_kernel(*refs, which=which, mine=mine, final=final, outs=len(sizes)),
        "near",
        [VMEM] * (9 + SWAPS) + [HBM] * final,
        [stats, peer, *em, *xs, mass, *came] + [previous] * final,
        [shape((size, width), dtype) for size in sizes],
        [pltpu.VMEM((count, width), jnp.float32), pltpu.SemaphoreType.DMA] * final,
        needs,
    )


def add_kernel(a_ref, b_ref, out_ref):
    out_ref[...] = (a_ref[...] + b_ref[...].astype(jnp.float32)).astype(out_ref.dtype)


def final_kernel(sums_ref, *refs):
    rep_refs, back_refs, out_ref = refs[0:2], refs[2:4], refs[4]
    count, width = out_ref.shape
    rep = jnp.concatenate([ref[...] for ref in rep_refs]).astype(jnp.float32)
    back = jnp.concatenate([ref[...] for ref in back_refs]).astype(jnp.float32)
    total = sums_ref[...] + rep + back
    mass = jnp.broadcast_to(total[count : count + 1], (128, count)).T
    out_ref[...] = total[:count] / jnp.concatenate([mass] * (width // 128), axis=1)


def energy_kernel(stats_ref, peer_ref, square_ref, out_ref, *last_refs, tau, span):
    top, denom = combine(chunk_parts(stats_ref[...], peer_ref[...], 0))
    energy = -tau * (top - square_ref[...] / tau + jnp.log(denom)) / D
    entries = energy.shape[1] // span
    out_ref[...] = jnp.zeros_like(out_ref)
    for e in range(entries):
        part = energy[:, e * span : (e + 1) * span]
        out_ref[e : e + 1, :] = part
        back = e - (entries - len(last_refs))
        if back >= 0:
            last_refs[back][...] = jnp.broadcast_to(part, last_refs[back].shape)


def place_kernel(facts_ref, energy_ref, *refs, bal):
    came_refs, out_ref = refs[:-1], refs[-1]
    me = lax.axis_index("wide")
    out_ref[...] = jnp.zeros_like(out_ref)

    def put(target, row):
        @pl.when((target >= 0) & (target // bal == me))
        def _():
            out_ref[pl.ds(target % bal, 1), :] = row

    for e in range(bal):
        put(facts_ref[0, e], energy_ref[e : e + 1, :])
    for h, came_ref in enumerate(came_refs):
        source = (me - h - 1) % facts_ref.shape[0]
        put(facts_ref[me ^ source, bal + h], came_ref[0:1, :])


def grid_plan(samples, centroids, move_target, fetch_ids, cand):
    rows = samples.shape[3]
    width = samples.shape[4]
    slots_in = samples.shape[2]
    bal = cand.shape[2]
    lists = cand.shape[3]
    pool = fetch_ids.shape[2]
    owned = centroids.shape[0] // rows
    peers = lax.axis_size("wide")
    sub = lax.axis_index("sub")
    tau = 2.0 * math.sqrt(D)
    handed = slots_in - bal
    span = rows // 2
    lanes = slots_in * span
    cut = bal * span
    pair_x, pair_c = 2, 1

    facts = jnp.concatenate(
        [move_target.reshape(slots_in), fetch_ids.reshape(pool), cand.reshape(bal * lists)]
    )
    facts = jnp.stack([facts] + [paired(facts, flip) for flip in range(1, peers)])
    bias = call(
        lambda *refs: bias_kernel(
            *refs, slots_in=slots_in, pool=pool, bal=bal, lists=lists, owned=owned,
            flips=(pair_x, pair_c), span=span,
        ),
        "bias",
        [SMEM],
        [facts],
        [shape((2, 2 * owned, lanes))],
    )[0]

    c0_own = (centroids * (2.0 / tau)).astype(jnp.bfloat16)
    c0_oth = swapped(c0_own, "sub")
    c1_own = paired(after(c0_own, facts), pair_c)

    blocks = samples.reshape(slots_in, rows, width)
    give = lax.dynamic_slice_in_dim(blocks, (1 - sub) * span, span, 1).reshape(lanes, width)
    took = swapped(give, "sub")
    own = lax.dynamic_slice_in_dim(blocks, sub * span, span, 1).reshape(lanes, width)
    full = jnp.concatenate([own, took], axis=1)
    x0 = (full[:cut], full[cut:])
    x1 = [paired(after(part, facts), pair_x) for part in x0]
    quarter = owned * rows // 4
    c1_oth = [swapped(c1_own[lo : lo + quarter], "sub") for lo in range(0, owned * rows, quarter)]
    sets = (joined(c0_own, [c0_oth]), joined(c1_own, c1_oth))
    work_sq = jnp.sum(jnp.square(full.astype(jnp.float32)), axis=1).reshape(1, lanes)

    *em0, stats0 = score(bias, 0, 0, full, sets)
    *em1a, stats1 = score(bias, 1, 0, x1[0], sets)
    *em1b, stats = score(bias, 1, cut, x1[1], sets, (stats0, stats1))
    em = list(zip(em0, em1a, em1b))
    peer = paired(stats, pair_x)

    xs = (full, *x1)
    half = jnp.bfloat16
    energy, *last = call(
        lambda *refs: energy_kernel(*refs, tau=tau, span=span),
        "energy",
        [VMEM] * 3,
        [stats, peer, work_sq],
        [shape((slots_in, span))] + [shape((8, span))] * handed,
    )

    first = (288,)
    equal = (264,)
    far_a, mass_a = far_sums(stats, peer, em[1], xs, 1, False)
    far_b, mass_b = far_sums(stats, peer, em[1], xs, 1, True, [far_a])

    def split_swap(far):
        return [swapped(part, "sub") for part in jnp.split(far, SWAPS)]

    near_a, near_b = split_swap(far_a), split_swap(far_b)
    sent_a = near_sums(
        stats, peer, em[1], xs, 1, False, mass_a, near_a, half, first, needs=[far_b]
    )
    came_a = [swapped(part, "rep") for part in sent_a]
    far_c, mass_c = far_sums(stats, peer, em[0], xs, 0, False, sent_a[:1])
    far_d, mass_d = far_sums(stats, peer, em[0], xs, 0, True, [far_c])
    near_c, near_d = split_swap(far_c), split_swap(far_d)
    part_b = near_sums(
        stats, peer, em[1], xs, 1, True, mass_b, near_b, jnp.float32, first, needs=[far_d]
    )
    (part_d,) = near_sums(
        stats, peer, em[0], xs, 0, True, mass_d, near_d, jnp.float32, (), centroids, part_b[:1]
    )

    energy, *last = call(
        lambda *refs: energy_kernel(*refs, tau=tau, span=span),
        "energy",
        [VMEM] * 3,
        [stats, peer, work_sq],
        [shape((slots_in, span))] + [shape((8, span))] * handed,
        needs=sent_a[:1],
    )
    came_last = [passed_along(last[h], "wide", h + 1) for h in range(handed)]

    came_back = []
    needs = [part_d, *came_last]
    for part, came in zip(part_b, came_a):
        back = call(
            add_kernel, "add", [VMEM] * 2, [part, came], [shape(part.shape, half)], needs=needs
        )[0]
        needs = [back]
        if not came_back:
            sent_c = near_sums(
                stats, peer, em[0], xs, 0, False, mass_c, near_c, half, equal, needs=needs
            )
            came_c = [swapped(part, "rep") for part in sent_c]
        came_back.append(paired(back, pair_c))
    energy = call(
        lambda *refs: place_kernel(*refs, bal=bal),
        "place",
        [SMEM] + [VMEM] * (1 + handed),
        [facts, energy, *came_last],
        [shape((bal, span))],
        needs=[back],
    )[0]
    fresh = call(
        final_kernel,
        "final",
        [VMEM] * 5,
        [part_d, *came_c, *came_back],
        [shape((owned * rows // 2, width))],
    )[0]
    return (fresh, energy.reshape(1, 1, bal, span))


def body(samples, centroids, move_target, fetch_ids, cand):
    sizes = [lax.axis_size(axis) for axis in ("wide", "rep", "sub")]
    if sizes == [4, 2, 2]:
        return grid_plan(samples, centroids, move_target, fetch_ids, cand)
    return exchange_plan(samples, centroids, move_target, fetch_ids, cand)


def solution(mesh):
    return jax.shard_map(
        body,
        mesh=mesh,
        in_specs=(
            P(("groups", "wide"), "rep", None, None, "sub"),
            P(("groups", "wide"), "sub"),
            P(("groups", "wide"), "rep", None),
            P(("groups", "wide"), "rep", None),
            P(("groups", "wide"), "rep", None, None),
        ),
        out_specs=(P(("groups", "wide", "rep"), "sub"), P(("groups", "wide"), "rep", None, "sub")),
        check_vma=False,
    )
```

```python
import math

import jax
import jax.numpy as jnp
from jax import lax
from jax.experimental import pallas as pl
from jax.experimental.pallas import tpu as pltpu
from jax.sharding import PartitionSpec as P

D = 1024


PRIOR = 1.0


def passed_along(value, axis, steps):
    count = lax.axis_size(axis)
    pairs = [(source, (source + steps) % count) for source in range(count)]
    return lax.ppermute(value, axis, pairs)


def pick_rows(table, index, present):
    picked = jnp.take(table, jnp.maximum(index, 0), axis=0)
    shape = (present.shape[0],) + (1,) * (picked.ndim - 1)
    return jnp.where(present.reshape(shape), picked, jnp.zeros_like(picked))


def soften(scores, tau):
    logits = scores / tau
    top = jnp.max(logits, axis=-1, keepdims=True)
    expo = jnp.exp(logits - top)
    total = jnp.sum(expo, axis=-1, keepdims=True)
    weights = (expo / total).astype(jnp.bfloat16)
    energy = -tau * (top[..., 0] + jnp.log(total[..., 0])) / D
    return (weights, energy)


def exchange_plan(samples, centroids, move_target, fetch_ids, cand):
    rows = samples.shape[3]
    width = samples.shape[4]
    slots_in = samples.shape[2]
    bal = cand.shape[2]
    lists = cand.shape[3]
    pool = fetch_ids.shape[2]
    owned = centroids.shape[0] // rows
    peers = lax.axis_size("wide")
    myself = lax.axis_index("wide")
    cap = max(1, 3 * pool // (2 * peers))
    tau = 2.0 * math.sqrt(D)
    handed = slots_in - bal
    blocks = samples.reshape(slots_in, rows, width)
    target = move_target.reshape(slots_in)
    dest = jnp.where(target >= 0, target // bal, -1)
    dest_slot = jnp.where(target >= 0, target % bal, -1)
    got_list = []
    slot_list = []
    for step in range(handed):
        entry = bal + step
        present = target[entry] >= 0
        send_block = jnp.where(present, blocks[entry], jnp.zeros_like(blocks[entry]))[None]
        send_slot = jnp.where(present, target[entry] % bal, -1).reshape(1)
        got_block, got_slot = passed_along((send_block, send_slot), "wide", step + 1)
        got_list.append(got_block)
        slot_list.append(got_slot)
    ids = fetch_ids.reshape(pool)
    owner = ids // owned
    local = ids % owned
    before = jnp.arange(pool)[None, :] < jnp.arange(pool)[:, None]
    position = jnp.sum(((owner[None, :] == owner[:, None]) & before).astype(jnp.int32), axis=1)
    slot_of = owner * cap + position
    slot_match = slot_of[None, :] == jnp.arange(peers * cap, dtype=jnp.int32)[:, None]
    slot_used = jnp.any(slot_match, axis=1)
    slot_item = jnp.sum(
        jnp.where(slot_match, jnp.arange(pool, dtype=jnp.int32)[None, :], 0), axis=1
    )
    asks = jnp.where(slot_used, jnp.take(local, slot_item), -1).reshape(peers, cap)
    wanted = lax.all_to_all(asks, "wide", split_axis=0, concat_axis=0, tiled=True)
    table = centroids.reshape(owned, rows, width)
    table_half = table.astype(jnp.bfloat16)
    wanted_flat = wanted.reshape(peers * cap)
    reply = pick_rows(table_half, wanted_flat, wanted_flat >= 0).reshape(peers, cap, rows, width)
    answered = lax.all_to_all(reply, "wide", split_axis=0, concat_axis=0, tiled=True)
    fetched = jnp.take(answered.reshape(peers * cap, rows, width), slot_of, axis=0)
    keep_here = dest == myself
    source_blocks = jnp.concatenate([blocks] + got_list, axis=0)
    source_slots = jnp.concatenate([jnp.where(keep_here, dest_slot, -1)] + slot_list, axis=0)
    fill_match = source_slots[None, :] == jnp.arange(bal, dtype=jnp.int32)[:, None]
    live = jnp.any(fill_match, axis=1)
    anchor = jnp.sum(
        jnp.where(fill_match, jnp.arange(slots_in + handed, dtype=jnp.int32)[None, :], 0), axis=1
    )
    work = pick_rows(source_blocks, anchor, live)
    flat_lists = cand.reshape(bal * lists)
    fetched_sq = jnp.sum(jnp.square(fetched.astype(jnp.float32)), axis=-1)

    def slot_scores(carry, items):
        work_one, lists_one = items
        chosen = jnp.take(fetched, lists_one, axis=0).reshape(lists * rows, width)
        dots = jnp.dot(work_one, chosen.T, preferred_element_type=jnp.float32)
        cent_sq = jnp.take(fetched_sq, lists_one, axis=0).reshape(lists * rows)
        work_sq = jnp.sum(jnp.square(work_one.astype(jnp.float32)), axis=-1)
        return (carry, 2.0 * dots - cent_sq[None, :] - work_sq[:, None])

    unused, partial_scores = lax.scan(slot_scores, 0, (work, cand.reshape(bal, lists)))
    half = rows // lax.axis_size("sub")
    lowest = lax.axis_index("sub") * half
    scores = lax.psum(partial_scores, "sub")
    weights, energy = soften(scores, tau)
    energy = lax.dynamic_slice_in_dim(energy, lowest, half, 1)
    weights = jnp.where(live[:, None, None], weights, jnp.zeros_like(weights))
    energy = jnp.where(live[:, None], energy, jnp.zeros_like(energy))
    pool_range = jnp.arange(pool, dtype=jnp.int32)

    def slot_sums(total, items):
        weights_one, work_one, lists_one = items
        term = jnp.dot(weights_one.T, work_one, preferred_element_type=jnp.float32).reshape(
            lists, rows * width
        )
        hot = (lists_one[None, :] == pool_range[:, None]).astype(jnp.float32)
        return (total + jnp.dot(hot, term, precision=lax.Precision.HIGHEST), 0)

    start_sums = jnp.zeros((pool, rows * width), jnp.float32)
    pooled, unused_two = lax.scan(slot_sums, start_sums, (weights, work, cand.reshape(bal, lists)))
    pool_sums = pooled.astype(jnp.bfloat16)
    mass = jnp.sum(weights.astype(jnp.float32), axis=1).reshape(bal * lists, rows)
    onehot = (flat_lists[None, :] == pool_range[:, None]).astype(jnp.float32)
    pool_mass = jnp.dot(onehot, mass, precision=lax.Precision.HIGHEST).astype(jnp.bfloat16)
    back_sums = pick_rows(pool_sums, slot_item, slot_used).reshape(peers, cap, rows, width)
    back_mass = pick_rows(pool_mass, slot_item, slot_used).reshape(peers, cap, rows)
    came_sums, came_mass = (
        lax.all_to_all(back_sums, "wide", split_axis=0, concat_axis=0, tiled=True),
        lax.all_to_all(back_mass, "wide", split_axis=0, concat_axis=0, tiled=True),
    )
    owner_hot = (wanted_flat[None, :] == jnp.arange(owned, dtype=jnp.int32)[:, None]).astype(
        jnp.bfloat16
    )
    owner_sums = jnp.dot(
        owner_hot, came_sums.reshape(peers * cap, rows * width), preferred_element_type=jnp.float32
    )
    owner_mass = jnp.dot(
        owner_hot, came_mass.reshape(peers * cap, rows), preferred_element_type=jnp.float32
    )
    share_sums, share_mass = (
        lax.psum_scatter(
            owner_sums.reshape(owned, rows, width).astype(jnp.bfloat16),
            "rep",
            scatter_dimension=0,
            tiled=True,
        ).astype(jnp.float32),
        lax.psum_scatter(
            owner_mass.astype(jnp.bfloat16), "rep", scatter_dimension=0, tiled=True
        ).astype(jnp.float32),
    )
    share = share_sums.shape[0]
    first_block = lax.axis_index("rep") * share
    previous = lax.dynamic_slice_in_dim(table, first_block, share, 0)
    fresh = (share_sums + PRIOR * previous) / (share_mass[:, :, None] + PRIOR)
    return (fresh.reshape(share * rows, width), energy.reshape(1, 1, bal, half))


LOW = -1e30
FLOOR = -1e29
MEGA = 2**20
PAD = 16
HBM = pl.BlockSpec(memory_space=pl.ANY)
VMEM = pl.BlockSpec(memory_space=pltpu.VMEM)
SMEM = pl.BlockSpec(memory_space=pltpu.SMEM)


def swapped(value, axis):
    return lax.ppermute(value, axis, [(0, 1), (1, 0)])


def paired(value, flip):
    count = lax.axis_size("wide")
    return lax.ppermute(value, "wide", [(w, w ^ flip) for w in range(count)])


def after(value, *others):
    return lax.optimization_barrier((value, *others))[0]


def shape(dims, dtype=jnp.float32):
    return jax.ShapeDtypeStruct(dims, dtype)


def call(kernel, name, in_specs, args, outs, scratch=(), needs=(), flops=1):
    count = len(args)

    def run(*refs):
        kernel(*refs[:count], *refs[count + len(needs) :])

    return pl.pallas_call(
        run,
        in_specs=in_specs + [HBM] * len(needs),
        out_specs=[VMEM] * len(outs),
        out_shape=outs,
        scratch_shapes=scratch,
        compiler_params=pltpu.CompilerParams(vmem_limit_bytes=16 * MEGA),
        cost_estimate=pl.CostEstimate(flops=flops, bytes_accessed=1, transcendentals=0),
        name=name,
    )(*args, *needs)


def bias_kernel(facts_ref, bias_ref, *, slots_in, bal, lists, owned, flips, span):
    me = lax.axis_index("wide")
    lanes = slots_in * span
    row = lax.broadcasted_iota(jnp.int32, (2 * owned, 128), 0)
    swung = (row + lax.axis_index("rep") * (owned // 2)) % owned
    block_id = jnp.where(row < owned, me * owned + row, (me ^ flips[1]) * owned + swung)
    place = lax.broadcasted_iota(jnp.int32, (1, 128), 1) // span
    for k in range(2):
        for lo in range(0, lanes, 128):
            listed = [jnp.full((1, 128), -1, jnp.int32) for j in range(lists)]
            for p in range(128 // span):
                target = facts_ref[flips[0] if k else 0, 0, lo // span + p]
                live = target >= 0
                target = jnp.maximum(target, 0)
                source = me ^ (target // bal)
                for j in range(lists):
                    block = facts_ref[source, 1, facts_ref[source, 2 + target % bal, j]]
                    listed[j] = jnp.where(place == p, jnp.where(live, block, -1), listed[j])
            times = jnp.zeros((2 * owned, 128), jnp.float32)
            for j in range(lists):
                times = times + jnp.where(block_id == listed[j], 1.0, 0.0)
            logs = jnp.log(jnp.maximum(times, 1.0))
            bias_ref[k, :, lo : lo + 128] = jnp.where(times > 0, logs, LOW)


def join_kernel(*refs):
    half_refs, (c_ref, square_ref) = refs[:-2], refs[-2:]
    width = half_refs[0].shape[1]
    lo = 0
    for own_ref, oth_ref in zip(half_refs[0::2], half_refs[1::2]):
        part = pl.ds(lo, oth_ref.shape[0])
        own, oth = own_ref[...], oth_ref[...]
        c_ref[part, 0:width] = own
        c_ref[part, width:] = oth
        total = jnp.zeros((part.size, 128), jnp.float32)
        for half in (own, oth):
            for lane in range(0, width, 128):
                piece = half[:, lane : lane + 128].astype(jnp.float32)
                total = total + piece * piece
        total = jnp.sum(total, axis=1, keepdims=True) * (math.sqrt(D) / 2.0)
        square_ref[part, :] = jnp.broadcast_to(total, (part.size, 128))
        lo += part.size


def joined(pairs, needs=()):
    count, width = sum(own.shape[0] for own, oth in pairs), pairs[0][0].shape[1]
    outs = [shape((count, 2 * width), jnp.bfloat16), shape((count, 128))]
    flat = [part for pair in pairs for part in pair]
    return call(join_kernel, "join", [VMEM] * len(flat), flat, outs, needs=needs)


def tiles(lanes):
    return [(lo, min(256, lanes - lo)) for lo in range(0, lanes, 256)]


def score_kernel(bias_ref, x_ref, *refs, chunk, sets, at):
    c_refs, refs = refs[: 2 * len(sets)], refs[2 * len(sets) :]
    before_refs, refs = refs[: len(at) - 1], refs[len(at) - 1 :]
    em_refs, (stats_ref, dots_ref) = refs[: len(sets)], refs[len(sets) :]
    for ref, (row, lane) in zip(before_refs, at[1:]):
        stats_ref[row : row + ref.shape[0], lane : lane + ref.shape[1]] = ref[...]
    count = bias_ref.shape[1] // 2
    rows = dots_ref.shape[1] // count
    turn = 0
    for lo, size in tiles(x_ref.shape[0]):
        for i, s in enumerate(sets):
            c_ref, csq_ref = c_refs[2 * i : 2 * i + 2]
            part = slice(lo, lo + size)
            buf = dots_ref.at[turn % 2]
            turn += 1
            buf[:, 0:size] = lax.dot_general(
                c_ref[...], x_ref[part, :], (((1,), (1,)), ((), ())), preferred_element_type=jnp.float32
            )

            def logits(g):
                block = pl.ds(g * rows, rows)
                less = jnp.concatenate([csq_ref[block, :]] * (size // 128), axis=1)
                return (buf[block, 0:size] - less).reshape(rows // 8, 8, size)

            bias = [bias_ref[chunk, s * count + g : s * count + g + 1, part] for g in range(count)]
            best = jnp.full((8, size), FLOOR, jnp.float32)
            for g in range(count):
                best = jnp.maximum(best, jnp.max(logits(g), axis=0) + bias[g])
            top = jnp.max(best, axis=0, keepdims=True)
            total = jnp.zeros((8, size), jnp.float32)
            for g in range(count):
                expo = jnp.exp(logits(g) + (bias[g] - top)[None])
                em_refs[i][pl.ds(g * rows, rows), part] = expo.reshape(rows, size).astype(jnp.bfloat16)
                total = total + jnp.sum(expo, axis=0)
            row, lane = at[0][0] + 2 * i, at[0][1] + lo
            stats_ref[row : row + 1, lane : lane + size] = top
            stats_ref[row + 1 : row + 2, lane : lane + size] = jnp.sum(total, axis=0, keepdims=True)


def score(bias, chunk, x, sets, before=()):
    cols = next(iter(sets.values()))[0].shape[0]
    count = len(sets)
    at = [(4 * chunk, 0) if before else (0, 0)] + [(row, lane) for part, row, lane in before]
    stats = shape((8, bias.shape[2]) if before else (2 * count, x.shape[0]))
    return call(
        lambda *refs: score_kernel(*refs, chunk=chunk, sets=list(sets), at=at),
        "scores",
        [VMEM] * (2 + 2 * count + len(before)),
        [bias, x, *[part for c in sets.values() for part in c], *[part[0] for part in before]],
        [shape((cols, x.shape[0]), jnp.bfloat16)] * count + [stats],
        [pltpu.VMEM((2, cols, 256), jnp.float32)],
    )


def combine(parts):
    top = parts[0][0:1]
    for part in parts[1:]:
        top = jnp.maximum(top, part[0:1])
    total = jnp.zeros_like(top)
    for part in parts:
        total = total + part[1:2] * jnp.exp(part[0:1] - top)
    return top, total


def chunk_parts(mine, peer, chunk):
    other = 1 - chunk
    return [
        mine[4 * chunk : 4 * chunk + 2],
        mine[4 * chunk + 2 : 4 * chunk + 4],
        peer[4 * other : 4 * other + 2],
        peer[4 * other + 2 : 4 * other + 4],
    ]


def half_rows(mine, count, which=0):
    if which:
        return pl.ds(0 if mine else count, count)
    rep = lax.axis_index("rep")
    return pl.ds(pl.multiple_of((rep if mine else 1 - rep) * count, count), count)


def weighted(mine_ref, peer_ref, em_refs, x_refs, rows, cols, which, mass):
    stats, peer = mine_ref[...], peer_ref[...]
    count = rows.size
    total = jnp.zeros((count, cols.stop - cols.start), jnp.float32)
    masses = jnp.zeros((count, 128), jnp.float32)
    lo = 0
    for em_ref, x_ref in zip(em_refs, x_refs):
        chunk, first = lo // stats.shape[1], lo % stats.shape[1]
        size = em_ref.shape[1]
        parts = chunk_parts(stats, peer, chunk)
        top, denom = combine(parts)
        factor = jnp.where(denom > 0, jnp.exp(parts[which][0:1] - top) / denom, 0.0)
        weights = (em_ref[rows, :].astype(jnp.float32) * factor[:, first : first + size]).astype(jnp.bfloat16)
        if mass:
            wide = weights.astype(jnp.float32)
            for lane in range(0, size, 128):
                masses = masses + wide[:, lane : lane + 128]
        total = total + jnp.dot(weights, x_ref[:, cols], preferred_element_type=jnp.float32)
        lo += size
    return total, masses


def far_kernel(*refs, which, mine):
    stats_ref, peer_ref = refs[0:2]
    em_refs, x_refs, (far_ref, mass_ref) = refs[2:4], refs[4:6], refs[6:]
    count, width = far_ref.shape[0] - PAD, far_ref.shape[1]
    total, masses = weighted(
        stats_ref, peer_ref, em_refs, x_refs, half_rows(mine, count, which), slice(width, 2 * width), which, True
    )
    masses = jnp.broadcast_to(jnp.sum(masses, axis=1, keepdims=True), (count, 128)).T[0:PAD]
    far_ref[0:count, :] = total.astype(jnp.bfloat16)
    far_ref[count:, :] = masses.astype(jnp.bfloat16)
    mass_ref[...] = masses


def near_kernel(*refs, which, mine, final, outs, swaps):
    stats_ref, peer_ref = refs[0:2]
    em_refs, x_refs, (mass_ref, *came_refs) = refs[2:4], refs[4:6], refs[6 : 7 + swaps]
    refs = refs[7 + swaps :]
    out_refs = refs[final : final + outs]
    count, width = sum(ref.shape[0] for ref in came_refs) - PAD, came_refs[0].shape[1]
    if final:
        previous_ref, sem = refs[1 + outs :]
        copy = pltpu.make_async_copy(refs[0].at[half_rows(mine, count), :], previous_ref, sem)
        copy.start()
    total, unused = weighted(
        stats_ref, peer_ref, em_refs, x_refs, half_rows(mine, count, which), slice(0, width), which, False
    )
    came = jnp.concatenate([ref[...] for ref in came_refs]).astype(jnp.float32)
    total = total + came[0:count]
    masses = mass_ref[...] + came[count:]
    if final:
        copy.wait()
        total = total + PRIOR * previous_ref[...]
        masses = masses + PRIOR
    lo = 0
    for out_ref in out_refs:
        size = min(out_ref.shape[0], count - lo)
        out_ref[0:size, :] = total[lo : lo + size].astype(out_ref.dtype)
        lo += size
    out_refs[-1][size:, :] = masses.astype(out_refs[-1].dtype)


def far_sums(stats, peer, em, xs, which, mine, needs=()):
    count, width = em[0].shape[0] // 2, xs[0].shape[1] // 2
    return call(
        lambda *refs: far_kernel(*refs, which=which, mine=mine),
        "far",
        [VMEM] * 6,
        [stats, peer, *em, *xs],
        [shape((count + PAD, width), jnp.bfloat16), shape((PAD, width))],
        needs=needs,
    )


def near_sums(stats, peer, em, xs, which, mine, mass, came, dtype, parts=(), previous=None, needs=()):
    count, width = em[0].shape[0] // 2, xs[0].shape[1] // 2
    final = previous is not None
    sizes = list(parts) + [count + PAD - sum(parts)]
    return call(
        lambda *refs: near_kernel(*refs, which=which, mine=mine, final=final, outs=len(sizes), swaps=len(came)),
        "near",
        [VMEM] * (7 + len(came)) + [HBM] * final,
        [stats, peer, *em, *xs, mass, *came] + [previous] * final,
        [shape((size, width), dtype) for size in sizes],
        [pltpu.VMEM((count, width), jnp.float32), pltpu.SemaphoreType.DMA] * final,
        needs,
    )


def add_kernel(a_ref, b_ref, out_ref):
    out_ref[...] = (a_ref[...] + b_ref[...].astype(jnp.float32)).astype(out_ref.dtype)


def early_kernel(came_ref, out_ref):
    out_ref[...] = came_ref[...].astype(out_ref.dtype)


def final_kernel(early_ref, sums_ref, *refs, parts):
    rep_refs, back_refs, out_ref = refs[:parts], refs[parts:-1], refs[-1]
    count, width = out_ref.shape
    first = early_ref.shape[0]
    rep = jnp.concatenate([ref[...] for ref in rep_refs]).astype(jnp.float32)
    back = jnp.concatenate([ref[...] for ref in back_refs]).astype(jnp.float32)
    later = sums_ref[first:, :] + rep[first:] + back
    mass = jnp.broadcast_to(later[count - first : count - first + 1], (128, count)).T
    mass = jnp.concatenate([mass] * (width // 128), axis=1)
    out_ref[0:first, :] = (sums_ref[0:first, :] + early_ref[...] + rep[0:first]) / mass[0:first]
    out_ref[first:, :] = later[: count - first] / mass[first:]


def energy_kernel(stats_ref, peer_ref, x0_ref, x1_ref, out_ref, last_ref, *, tau, span, handed):
    last_ref[...] = jnp.zeros_like(last_ref)
    for chunk, x_ref in enumerate((x0_ref, x1_ref)):
        lanes, depth = x_ref.shape
        square = jnp.zeros((lanes, 128), jnp.float32)
        for lane in range(0, depth, 128):
            part = x_ref[:, lane : lane + 128].astype(jnp.float32)
            square = square + part * part
        square = jnp.sum(jnp.broadcast_to(jnp.sum(square, axis=1, keepdims=True), (lanes, 128)).T[0:1], axis=0, keepdims=True)
        top, denom = combine(chunk_parts(stats_ref[...], peer_ref[...], chunk))
        energy = -tau * (top - square / tau + jnp.log(denom)) / D
        entries = lanes // span
        for e in range(entries):
            part = energy[:, e * span : (e + 1) * span]
            if chunk == 0:
                out_ref[e : e + 1, :] = part
            if e >= entries - handed:
                row = handed * chunk + e - (entries - handed)
                last_ref[row : row + 1, :] = part


def place_kernel(facts_ref, energy_ref, last_ref, came_ref, out_ref, *, bal):
    me = lax.axis_index("wide")
    out_ref[...] = jnp.zeros_like(out_ref)

    def put(target, row):
        @pl.when((target >= 0) & (target // bal == me))
        def _():
            out_ref[pl.ds(target % bal, 1), :] = row

    for e in range(bal):
        put(facts_ref[0, 0, e], energy_ref[e : e + 1, :])
    odd = me % 2 == 1
    one = jnp.where(odd, last_ref[2:3, :], came_ref[2:3, :])
    put(facts_ref[jnp.where(odd, 1, 3), 0, bal], one)
    put(facts_ref[2, 0, bal + 1], came_ref[1:2, :])


def grid_plan(samples, centroids, move_target, fetch_ids, cand):
    rows = samples.shape[3]
    width = samples.shape[4]
    slots_in = samples.shape[2]
    bal = cand.shape[2]
    lists = cand.shape[3]
    pool = fetch_ids.shape[2]
    owned = centroids.shape[0] // rows
    peers = lax.axis_size("wide")
    sub = lax.axis_index("sub")
    tau = 2.0 * math.sqrt(D)
    handed = slots_in - bal
    span = rows // 2
    lanes = slots_in * span
    pair_x, pair_c = 1, 2

    table = [move_target.reshape(1, slots_in), fetch_ids.reshape(1, pool), cand.reshape(bal, lists)]
    facts = jnp.concatenate([jnp.pad(part, ((0, 0), (0, pool - part.shape[1]))) for part in table])
    facts = jnp.stack([facts] + [paired(facts, flip) for flip in range(1, peers)])
    bias = call(
        lambda *refs: bias_kernel(
            *refs, slots_in=slots_in, bal=bal, lists=lists, owned=owned, flips=(pair_x, pair_c), span=span
        ),
        "bias",
        [SMEM],
        [facts],
        [shape((2, 2 * owned, lanes))],
    )[0]

    share = owned * rows // 2
    c_half = lax.dynamic_slice_in_dim(centroids, lax.axis_index("rep") * share, share, 0)
    c_half = (c_half * (2.0 / tau)).astype(jnp.bfloat16)
    c0_own = (centroids * (2.0 / tau)).astype(jnp.bfloat16)
    c1_own = [paired(after(c_half, facts), pair_c)]
    c1_own.append(swapped(c1_own[0], "rep"))
    c0_oth = swapped(c0_own, "sub")

    blocks = samples.reshape(slots_in, rows, width)
    give = lax.dynamic_slice_in_dim(blocks, (1 - sub) * span, span, 1).reshape(lanes, width)
    took = swapped(give, "sub")
    own = lax.dynamic_slice_in_dim(blocks, sub * span, span, 1).reshape(lanes, width)
    full = jnp.concatenate([own, took], axis=1)
    x1 = paired(after(full, facts), pair_x)

    set_a = joined([(c0_own, c0_oth)])
    em_a0, stats_a0 = score(bias, 0, full, {0: set_a})
    c1_oth = [swapped(part, "sub") for part in (c1_own[0], after(c1_own[1], stats_a0))]
    set_b = joined(list(zip(c1_own, c1_oth)), [stats_a0])
    em_b0, stats_b0 = score(bias, 0, full, {1: set_b})
    before = [(stats_a0, 0, 0), (stats_b0, 2, 0)]
    em_a1, em_b1, stats = score(bias, 1, x1, {0: set_a, 1: set_b}, before)
    em = ((em_a0, em_a1), (em_b0, em_b1))
    peer = paired(stats, pair_x)

    xs = (full, x1)
    half = jnp.bfloat16
    first, equal = (272,), (264,)

    far_a, mass_a = far_sums(stats, peer, em[1], xs, 1, False)
    far_b, mass_b = far_sums(stats, peer, em[1], xs, 1, True, [far_a])
    far_c, mass_c = far_sums(stats, peer, em[0], xs, 0, False, [far_b])
    near_a = [swapped(part, "sub") for part in jnp.split(far_a, 2)]
    near_b, near_c = [[swapped(far, "sub")] for far in (far_b, far_c)]
    sent_a = near_sums(
        stats, peer, em[1], xs, 1, False, mass_a, near_a, half, first, needs=[far_c]
    )
    part_b = near_sums(
        stats, peer, em[1], xs, 1, True, mass_b, near_b, jnp.float32, first, needs=sent_a[:1]
    )
    energy, last = call(
        lambda *refs: energy_kernel(*refs, tau=tau, span=span, handed=handed),
        "energy",
        [VMEM] * 4,
        [stats, peer, *xs],
        [shape((slots_in, span)), shape((8, span))],
        needs=part_b[:1],
    )
    came_last = paired(last, 2)

    def returned(part, came, needs):
        back = call(
            add_kernel, "add", [VMEM] * 2, [part, came], [shape(part.shape, half)], needs=needs
        )[0]
        return back, paired(back, pair_c)

    back, came_back_0 = returned(part_b[0], swapped(sent_a[0], "rep"), [came_last])
    came = swapped(after(sent_a[1], back), "rep")
    sent_c = near_sums(
        stats, peer, em[0], xs, 0, False, mass_c, near_c, half, equal, needs=[back]
    )
    came_c = [swapped(part, "rep") for part in sent_c]
    back, came_back_1 = returned(part_b[1], came, [])
    came_back = [came_back_0, came_back_1]
    far_d, mass_d = far_sums(stats, peer, em[0], xs, 0, True, [back])
    near_d = [swapped(far_d, "sub")]
    (part_d,) = near_sums(
        stats, peer, em[0], xs, 0, True, mass_d, near_d, jnp.float32, (), centroids, sent_c[:1]
    )
    early = call(
        early_kernel,
        "early",
        [VMEM],
        [came_back[0]],
        [shape((first[0], width))],
        flops=2 * 10**10,
    )[0]
    energy = call(
        lambda *refs: place_kernel(*refs, bal=bal),
        "place",
        [SMEM] + [VMEM] * 3,
        [facts, energy, last, came_last],
        [shape((bal, span))],
        needs=[back],
    )[0]
    fresh = call(
        lambda *refs: final_kernel(*refs, parts=len(came_c)),
        "final",
        [VMEM] * (2 + len(came_c) + len(came_back[1:])),
        [early, part_d, *came_c, *came_back[1:]],
        [shape((share, width))],
    )[0]
    return (fresh, energy.reshape(1, 1, bal, span))


def body(samples, centroids, move_target, fetch_ids, cand):
    sizes = [lax.axis_size(axis) for axis in ("wide", "rep", "sub")]
    if sizes == [4, 2, 2] and samples.shape[2] - cand.shape[2] == 2:
        return grid_plan(samples, centroids, move_target, fetch_ids, cand)
    return exchange_plan(samples, centroids, move_target, fetch_ids, cand)


def solution(mesh):
    return jax.shard_map(
        body,
        mesh=mesh,
        in_specs=(
            P(("groups", "wide"), "rep", None, None, "sub"),
            P(("groups", "wide"), "sub"),
            P(("groups", "wide"), "rep", None),
            P(("groups", "wide"), "rep", None),
            P(("groups", "wide"), "rep", None, None),
        ),
        out_specs=(P(("groups", "wide", "rep"), "sub"), P(("groups", "wide"), "rep", None, "sub")),
        check_vma=False,
    )
```

```python
import math

import jax
import jax.numpy as jnp
from jax import lax
from jax.experimental import pallas as pl
from jax.experimental.pallas import tpu as pltpu
from jax.sharding import PartitionSpec as P

D = 1024


PRIOR = 1.0


def passed_along(value, axis, steps):
    count = lax.axis_size(axis)
    pairs = [(source, (source + steps) % count) for source in range(count)]
    return lax.ppermute(value, axis, pairs)


def pick_rows(table, index, present):
    picked = jnp.take(table, jnp.maximum(index, 0), axis=0)
    shape = (present.shape[0],) + (1,) * (picked.ndim - 1)
    return jnp.where(present.reshape(shape), picked, jnp.zeros_like(picked))


def soften(scores, tau):
    logits = scores / tau
    top = jnp.max(logits, axis=-1, keepdims=True)
    expo = jnp.exp(logits - top)
    total = jnp.sum(expo, axis=-1, keepdims=True)
    weights = (expo / total).astype(jnp.bfloat16)
    energy = -tau * (top[..., 0] + jnp.log(total[..., 0])) / D
    return (weights, energy)


def exchange_plan(samples, centroids, move_target, fetch_ids, cand):
    rows = samples.shape[3]
    width = samples.shape[4]
    slots_in = samples.shape[2]
    bal = cand.shape[2]
    lists = cand.shape[3]
    pool = fetch_ids.shape[2]
    owned = centroids.shape[0] // rows
    peers = lax.axis_size("wide")
    myself = lax.axis_index("wide")
    cap = max(1, 3 * pool // (2 * peers))
    tau = 2.0 * math.sqrt(D)
    handed = slots_in - bal
    blocks = samples.reshape(slots_in, rows, width)
    target = move_target.reshape(slots_in)
    dest = jnp.where(target >= 0, target // bal, -1)
    dest_slot = jnp.where(target >= 0, target % bal, -1)
    got_list = []
    slot_list = []
    for step in range(handed):
        entry = bal + step
        present = target[entry] >= 0
        send_block = jnp.where(present, blocks[entry], jnp.zeros_like(blocks[entry]))[None]
        send_slot = jnp.where(present, target[entry] % bal, -1).reshape(1)
        got_block, got_slot = passed_along((send_block, send_slot), "wide", step + 1)
        got_list.append(got_block)
        slot_list.append(got_slot)
    ids = fetch_ids.reshape(pool)
    owner = ids // owned
    local = ids % owned
    before = jnp.arange(pool)[None, :] < jnp.arange(pool)[:, None]
    position = jnp.sum(((owner[None, :] == owner[:, None]) & before).astype(jnp.int32), axis=1)
    slot_of = owner * cap + position
    slot_match = slot_of[None, :] == jnp.arange(peers * cap, dtype=jnp.int32)[:, None]
    slot_used = jnp.any(slot_match, axis=1)
    slot_item = jnp.sum(
        jnp.where(slot_match, jnp.arange(pool, dtype=jnp.int32)[None, :], 0), axis=1
    )
    asks = jnp.where(slot_used, jnp.take(local, slot_item), -1).reshape(peers, cap)
    wanted = lax.all_to_all(asks, "wide", split_axis=0, concat_axis=0, tiled=True)
    table = centroids.reshape(owned, rows, width)
    table_half = table.astype(jnp.bfloat16)
    wanted_flat = wanted.reshape(peers * cap)
    reply = pick_rows(table_half, wanted_flat, wanted_flat >= 0).reshape(peers, cap, rows, width)
    answered = lax.all_to_all(reply, "wide", split_axis=0, concat_axis=0, tiled=True)
    fetched = jnp.take(answered.reshape(peers * cap, rows, width), slot_of, axis=0)
    keep_here = dest == myself
    source_blocks = jnp.concatenate([blocks] + got_list, axis=0)
    source_slots = jnp.concatenate([jnp.where(keep_here, dest_slot, -1)] + slot_list, axis=0)
    fill_match = source_slots[None, :] == jnp.arange(bal, dtype=jnp.int32)[:, None]
    live = jnp.any(fill_match, axis=1)
    anchor = jnp.sum(
        jnp.where(fill_match, jnp.arange(slots_in + handed, dtype=jnp.int32)[None, :], 0), axis=1
    )
    work = pick_rows(source_blocks, anchor, live)
    flat_lists = cand.reshape(bal * lists)
    fetched_sq = jnp.sum(jnp.square(fetched.astype(jnp.float32)), axis=-1)

    def slot_scores(carry, items):
        work_one, lists_one = items
        chosen = jnp.take(fetched, lists_one, axis=0).reshape(lists * rows, width)
        dots = jnp.dot(work_one, chosen.T, preferred_element_type=jnp.float32)
        cent_sq = jnp.take(fetched_sq, lists_one, axis=0).reshape(lists * rows)
        work_sq = jnp.sum(jnp.square(work_one.astype(jnp.float32)), axis=-1)
        return (carry, 2.0 * dots - cent_sq[None, :] - work_sq[:, None])

    unused, partial_scores = lax.scan(slot_scores, 0, (work, cand.reshape(bal, lists)))
    half = rows // lax.axis_size("sub")
    lowest = lax.axis_index("sub") * half
    scores = lax.psum(partial_scores, "sub")
    weights, energy = soften(scores, tau)
    energy = lax.dynamic_slice_in_dim(energy, lowest, half, 1)
    weights = jnp.where(live[:, None, None], weights, jnp.zeros_like(weights))
    energy = jnp.where(live[:, None], energy, jnp.zeros_like(energy))
    pool_range = jnp.arange(pool, dtype=jnp.int32)

    def slot_sums(total, items):
        weights_one, work_one, lists_one = items
        term = jnp.dot(weights_one.T, work_one, preferred_element_type=jnp.float32).reshape(
            lists, rows * width
        )
        hot = (lists_one[None, :] == pool_range[:, None]).astype(jnp.float32)
        return (total + jnp.dot(hot, term, precision=lax.Precision.HIGHEST), 0)

    start_sums = jnp.zeros((pool, rows * width), jnp.float32)
    pooled, unused_two = lax.scan(slot_sums, start_sums, (weights, work, cand.reshape(bal, lists)))
    pool_sums = pooled.astype(jnp.bfloat16)
    mass = jnp.sum(weights.astype(jnp.float32), axis=1).reshape(bal * lists, rows)
    onehot = (flat_lists[None, :] == pool_range[:, None]).astype(jnp.float32)
    pool_mass = jnp.dot(onehot, mass, precision=lax.Precision.HIGHEST).astype(jnp.bfloat16)
    back_sums = pick_rows(pool_sums, slot_item, slot_used).reshape(peers, cap, rows, width)
    back_mass = pick_rows(pool_mass, slot_item, slot_used).reshape(peers, cap, rows)
    came_sums, came_mass = (
        lax.all_to_all(back_sums, "wide", split_axis=0, concat_axis=0, tiled=True),
        lax.all_to_all(back_mass, "wide", split_axis=0, concat_axis=0, tiled=True),
    )
    owner_hot = (wanted_flat[None, :] == jnp.arange(owned, dtype=jnp.int32)[:, None]).astype(
        jnp.bfloat16
    )
    owner_sums = jnp.dot(
        owner_hot, came_sums.reshape(peers * cap, rows * width), preferred_element_type=jnp.float32
    )
    owner_mass = jnp.dot(
        owner_hot, came_mass.reshape(peers * cap, rows), preferred_element_type=jnp.float32
    )
    share_sums, share_mass = (
        lax.psum_scatter(
            owner_sums.reshape(owned, rows, width).astype(jnp.bfloat16),
            "rep",
            scatter_dimension=0,
            tiled=True,
        ).astype(jnp.float32),
        lax.psum_scatter(
            owner_mass.astype(jnp.bfloat16), "rep", scatter_dimension=0, tiled=True
        ).astype(jnp.float32),
    )
    share = share_sums.shape[0]
    first_block = lax.axis_index("rep") * share
    previous = lax.dynamic_slice_in_dim(table, first_block, share, 0)
    fresh = (share_sums + PRIOR * previous) / (share_mass[:, :, None] + PRIOR)
    return (fresh.reshape(share * rows, width), energy.reshape(1, 1, bal, half))


LOW = -1e30
FLOOR = -1e29
MEGA = 2**20
PAD = 16
BLOCK = 128
SETS = (0, 8, 12)
HBM = pl.BlockSpec(memory_space=pl.ANY)
VMEM = pl.BlockSpec(memory_space=pltpu.VMEM)
SMEM = pl.BlockSpec(memory_space=pltpu.SMEM)


def swapped(value, axis):
    return lax.ppermute(value, axis, [(0, 1), (1, 0)])


def paired(value, flip):
    count = lax.axis_size("wide")
    return lax.ppermute(value, "wide", [(w, w ^ flip) for w in range(count)])


def after(value, *others):
    return lax.optimization_barrier((value, *others))[0]


def shape(dims, dtype=jnp.float32):
    return jax.ShapeDtypeStruct(dims, dtype)


def call(kernel, name, in_specs, args, outs, scratch=(), needs=(), flops=1):
    count = len(args)

    def run(*refs):
        kernel(*refs[:count], *refs[count + len(needs) :])

    return pl.pallas_call(
        run,
        in_specs=in_specs + [HBM] * len(needs),
        out_specs=[VMEM] * len(outs),
        out_shape=outs,
        scratch_shapes=scratch,
        compiler_params=pltpu.CompilerParams(vmem_limit_bytes=16 * MEGA),
        cost_estimate=pl.CostEstimate(flops=flops, bytes_accessed=1, transcendentals=0),
        name=name,
    )(*args, *needs)


def bias_kernel(facts_ref, bias_ref, *, slots_in, bal, lists, owned, flips, span):
    me = lax.axis_index("wide")
    lanes = slots_in * span
    row = lax.broadcasted_iota(jnp.int32, (2 * owned, 128), 0)
    swung = (row + lax.axis_index("rep") * (owned // 2)) % owned
    block_id = jnp.where(row < owned, me * owned + row, (me ^ flips[1]) * owned + swung)
    place = lax.broadcasted_iota(jnp.int32, (1, 128), 1) // span
    for k in range(2):
        for lo in range(0, lanes, 128):
            listed = [jnp.full((1, 128), -1, jnp.int32) for j in range(lists)]
            for p in range(128 // span):
                target = facts_ref[flips[0] if k else 0, 0, lo // span + p]
                live = target >= 0
                target = jnp.maximum(target, 0)
                source = me ^ (target // bal)
                for j in range(lists):
                    block = facts_ref[source, 1, facts_ref[source, 2 + target % bal, j]]
                    listed[j] = jnp.where(place == p, jnp.where(live, block, -1), listed[j])
            times = jnp.zeros((2 * owned, 128), jnp.float32)
            for j in range(lists):
                times = times + jnp.where(block_id == listed[j], 1.0, 0.0)
            logs = jnp.log(jnp.maximum(times, 1.0))
            bias_ref[k, :, lo : lo + 128] = jnp.where(times > 0, logs, LOW)


def join_kernel(*refs):
    half_refs, (c_ref, square_ref) = refs[:-2], refs[-2:]
    width = half_refs[0].shape[1]
    lo = 0
    for own_ref, oth_ref in zip(half_refs[0::2], half_refs[1::2]):
        part = pl.ds(lo, oth_ref.shape[0])
        own, oth = own_ref[...], oth_ref[...]
        c_ref[part, 0:width] = own
        c_ref[part, width:] = oth
        total = jnp.zeros((part.size, 128), jnp.float32)
        for half in (own, oth):
            for lane in range(0, width, 128):
                piece = half[:, lane : lane + 128].astype(jnp.float32)
                total = total + piece * piece
        total = jnp.sum(total, axis=1, keepdims=True) * (math.sqrt(D) / 2.0)
        square_ref[part, :] = jnp.broadcast_to(total, (part.size, 128))
        lo += part.size


def joined(pairs, needs=()):
    count, width = sum(own.shape[0] for own, oth in pairs), pairs[0][0].shape[1]
    outs = [shape((count, 2 * width), jnp.bfloat16), shape((count, 128))]
    flat = [part for pair in pairs for part in pair]
    return call(join_kernel, "join", [VMEM] * len(flat), flat, outs, needs=needs)


def tiles(lanes):
    return [(lo, min(256, lanes - lo)) for lo in range(0, lanes, 256)]


def score_kernel(bias_ref, x_ref, *refs, chunk, first, sets, at):
    c_refs, refs = refs[: 2 * len(sets)], refs[2 * len(sets) :]
    before_refs, refs = refs[: len(at) - 1], refs[len(at) - 1 :]
    em_refs, (stats_ref, dots_ref) = refs[: len(sets)], refs[len(sets) :]
    for ref, (row, lane) in zip(before_refs, at[1:]):
        stats_ref[row : row + ref.shape[0], lane : lane + ref.shape[1]] = ref[...]
    turn = 0
    for lo, size in tiles(x_ref.shape[0]):
        for i, s in enumerate(sets):
            c_ref, csq_ref = c_refs[2 * i : 2 * i + 2]
            count, base = c_ref.shape[0] // BLOCK, SETS[s]
            part = slice(lo, lo + size)
            buf = dots_ref.at[turn % 2]
            turn += 1
            buf[0 : c_ref.shape[0], 0:size] = lax.dot_general(
                c_ref[...], x_ref[part, :], (((1,), (1,)), ((), ())), preferred_element_type=jnp.float32
            )

            def logits(g):
                block = pl.ds(g * BLOCK, BLOCK)
                less = jnp.concatenate([csq_ref[block, :]] * (size // 128), axis=1)
                return (buf[block, 0:size] - less).reshape(BLOCK // 8, 8, size)

            of_chunk = slice(first + lo, first + lo + size)
            bias = [bias_ref[chunk, base + g : base + g + 1, of_chunk] for g in range(count)]
            best = jnp.full((8, size), FLOOR, jnp.float32)
            for g in range(count):
                best = jnp.maximum(best, jnp.max(logits(g), axis=0) + bias[g])
            top = jnp.max(best, axis=0, keepdims=True)
            total = jnp.zeros((8, size), jnp.float32)
            for g in range(count):
                expo = jnp.exp(logits(g) + (bias[g] - top)[None])
                em_refs[i][pl.ds(g * BLOCK, BLOCK), part] = expo.reshape(BLOCK, size).astype(jnp.bfloat16)
                total = total + jnp.sum(expo, axis=0)
            row, lane = at[0][0] + 2 * i, at[0][1] + lo
            stats_ref[row : row + 1, lane : lane + size] = top
            stats_ref[row + 1 : row + 2, lane : lane + size] = jnp.sum(total, axis=0, keepdims=True)


def score(bias, chunk, x, sets, before=(), first=0):
    cols = [c.shape[0] for c, square in sets.values()]
    count = len(sets)
    at = [(8 * chunk, first) if before else (0, 0)] + [(row, lane) for part, row, lane in before]
    stats = shape((16, bias.shape[2]) if before else (2 * count, x.shape[0]))
    return call(
        lambda *refs: score_kernel(*refs, chunk=chunk, first=first, sets=list(sets), at=at),
        "scores",
        [VMEM] * (2 + 2 * count + len(before)),
        [bias, x, *[part for c in sets.values() for part in c], *[part[0] for part in before]],
        [shape((size, x.shape[0]), jnp.bfloat16) for size in cols] + [stats],
        [pltpu.VMEM((2, max(cols), 256), jnp.float32)],
    )


def combine(parts):
    top = parts[0][0:1]
    for part in parts[1:]:
        top = jnp.maximum(top, part[0:1])
    total = jnp.zeros_like(top)
    for part in parts:
        total = total + part[1:2] * jnp.exp(part[0:1] - top)
    return top, total


def chunk_parts(mine, peer, chunk):
    rows = [8 * chunk + 2 * s for s in range(len(SETS))]
    other = [8 * (1 - chunk) + 2 * s for s in range(len(SETS))]
    return [mine[row : row + 2] for row in rows] + [peer[row : row + 2] for row in other]


def half_rows(mine, count, which=0):
    if which:
        return pl.ds(0, count)
    rep = lax.axis_index("rep")
    return pl.ds(pl.multiple_of((rep if mine else 1 - rep) * count, count), count)


def weighted(mine_ref, peer_ref, em_refs, x_refs, rows, cols, which, mass):
    stats, peer = mine_ref[...], peer_ref[...]
    count = rows.size
    total = jnp.zeros((count, cols.stop - cols.start), jnp.float32)
    masses = jnp.zeros((count, 128), jnp.float32)
    lo = 0
    for em_ref, x_ref in zip(em_refs, x_refs):
        chunk, first = lo // stats.shape[1], lo % stats.shape[1]
        size = em_ref.shape[1]
        parts = chunk_parts(stats, peer, chunk)
        top, denom = combine(parts)
        factor = jnp.where(denom > 0, jnp.exp(parts[which][0:1] - top) / denom, 0.0)
        weights = (em_ref[rows, :].astype(jnp.float32) * factor[:, first : first + size]).astype(jnp.bfloat16)
        if mass:
            wide = weights.astype(jnp.float32)
            for lane in range(0, size, 128):
                masses = masses + wide[:, lane : lane + 128]
        total = total + jnp.dot(weights, x_ref[:, cols], preferred_element_type=jnp.float32)
        lo += size
    return total, masses


def far_kernel(*refs, which, mine):
    stats_ref, peer_ref = refs[0:2]
    em_refs, x_refs, (far_ref, mass_ref) = refs[2:5], refs[5:8], refs[8:]
    count, width = far_ref.shape[0] - PAD, far_ref.shape[1]
    total, masses = weighted(
        stats_ref, peer_ref, em_refs, x_refs, half_rows(mine, count, which), slice(width, 2 * width), which, True
    )
    masses = jnp.broadcast_to(jnp.sum(masses, axis=1, keepdims=True), (count, 128)).T[0:PAD]
    far_ref[0:count, :] = total.astype(jnp.bfloat16)
    far_ref[count:, :] = masses.astype(jnp.bfloat16)
    mass_ref[...] = masses


def near_kernel(*refs, which, mine, final, outs, swaps):
    stats_ref, peer_ref = refs[0:2]
    em_refs, x_refs, (mass_ref, *came_refs) = refs[2:5], refs[5:8], refs[8 : 9 + swaps]
    refs = refs[9 + swaps :]
    out_refs = refs[final : final + outs]
    count, width = sum(ref.shape[0] for ref in came_refs) - PAD, came_refs[0].shape[1]
    if final:
        previous_ref, sem = refs[1 + outs :]
        copy = pltpu.make_async_copy(refs[0].at[half_rows(mine, count), :], previous_ref, sem)
        copy.start()
    total, unused = weighted(
        stats_ref, peer_ref, em_refs, x_refs, half_rows(mine, count, which), slice(0, width), which, False
    )
    came = jnp.concatenate([ref[...] for ref in came_refs]).astype(jnp.float32)
    total = total + came[0:count]
    masses = mass_ref[...] + came[count:]
    if final:
        copy.wait()
        total = total + PRIOR * previous_ref[...]
        masses = masses + PRIOR
    lo = 0
    for out_ref in out_refs:
        size = min(out_ref.shape[0], count - lo)
        out_ref[0:size, :] = total[lo : lo + size].astype(out_ref.dtype)
        lo += size
    out_refs[-1][size:, :] = masses.astype(out_refs[-1].dtype)


def far_sums(stats, peer, em, xs, which, mine, needs=()):
    width = xs[0].shape[1] // 2
    count = em[0].shape[0] if which else em[0].shape[0] // 2
    return call(
        lambda *refs: far_kernel(*refs, which=which, mine=mine),
        "far",
        [VMEM] * 8,
        [stats, peer, *em, *xs],
        [shape((count + PAD, width), jnp.bfloat16), shape((PAD, width))],
        needs=needs,
    )


def near_sums(stats, peer, em, xs, which, mine, mass, came, dtype, parts=(), previous=None, needs=()):
    width = xs[0].shape[1] // 2
    count = em[0].shape[0] if which else em[0].shape[0] // 2
    final = previous is not None
    sizes = list(parts) + [count + PAD - sum(parts)]
    return call(
        lambda *refs: near_kernel(*refs, which=which, mine=mine, final=final, outs=len(sizes), swaps=len(came)),
        "near",
        [VMEM] * (9 + len(came)) + [HBM] * final,
        [stats, peer, *em, *xs, mass, *came] + [previous] * final,
        [shape((size, width), dtype) for size in sizes],
        [pltpu.VMEM((count, width), jnp.float32), pltpu.SemaphoreType.DMA] * final,
        needs,
    )


def add_kernel(a_ref, b_ref, *refs):
    out_ref = refs[-1]
    total = a_ref[...] + b_ref[...].astype(jnp.float32)
    out_ref[...] = total.astype(out_ref.dtype)
    if len(refs) == 2:
        count, width = out_ref.shape
        rest = jnp.concatenate([refs[0][k : k + 1, :] for k in range(4)], axis=1)
        rest = jnp.concatenate([rest, jnp.zeros((1, width - rest.shape[1]), jnp.float32)], axis=1)
        rows = [total[count - PAD : count - PAD + 8]]
        for k in range(3):
            rows.append(rest.astype(jnp.bfloat16).astype(jnp.float32))
            rest = rest - rows[-1]
        rows.append(jnp.zeros((5, width), jnp.float32))
        out_ref[count - PAD :, :] = jnp.concatenate(rows).astype(out_ref.dtype)


def early_kernel(came_ref, out_ref):
    out_ref[...] = came_ref[...].astype(out_ref.dtype)


def final_kernel(energy_ref, masks_ref, sums_ref, *refs, parts):
    rep_refs, back_refs, (out_ref, placed_ref) = refs[:parts], refs[parts:-2], refs[-2:]
    count, width = out_ref.shape
    bal, span = placed_ref.shape
    rep = jnp.concatenate([ref[...] for ref in rep_refs]).astype(jnp.float32)
    back = jnp.concatenate([ref[...].astype(jnp.float32) for ref in back_refs])
    total = sums_ref[...] + rep + back
    mass = jnp.broadcast_to(total[count : count + 1], (128, count)).T
    out_ref[...] = total[:count] / jnp.concatenate([mass] * (width // 128), axis=1)
    came = back[count + 8 : count + 9] + back[count + 9 : count + 10] + back[count + 10 : count + 11]
    placed = energy_ref[...]
    placed = jnp.where(masks_ref[0:bal, :] > 0, came[:, span : 2 * span], placed)
    placed_ref[...] = jnp.where(masks_ref[bal:, :] > 0, came[:, 2 * span : 3 * span], placed)


def energy_kernel(stats_ref, peer_ref, x0_ref, *refs, tau, span, handed):
    x1_refs, (out_ref, last_ref) = refs[:-2], refs[-2:]
    last_ref[...] = jnp.zeros_like(last_ref)
    for chunk, x_refs in enumerate(((x0_ref,), x1_refs)):
        squares = []
        for x_ref in x_refs:
            square = jnp.zeros((x_ref.shape[0], 128), jnp.float32)
            for lane in range(0, x_ref.shape[1], 128):
                part = x_ref[:, lane : lane + 128].astype(jnp.float32)
                square = square + part * part
            square = jnp.sum(square, axis=1, keepdims=True)
            squares.append(jnp.broadcast_to(square, (x_ref.shape[0], 128)).T[0:1])
        square = jnp.concatenate(squares, axis=1)
        lanes = square.shape[1]
        top, denom = combine(chunk_parts(stats_ref[...], peer_ref[...], chunk))
        energy = -tau * (top - square / tau + jnp.log(denom)) / D
        entries = lanes // span
        for e in range(entries):
            part = energy[:, e * span : (e + 1) * span]
            if chunk == 0:
                out_ref[e : e + 1, :] = part
            if e >= entries - handed:
                row = handed * chunk + e - (entries - handed)
                last_ref[row : row + 1, :] = part


def place_kernel(facts_ref, energy_ref, last_ref, out_ref, masks_ref):
    out_ref[...] = jnp.zeros_like(out_ref)
    masks_ref[...] = jnp.zeros_like(masks_ref)
    bal = out_ref.shape[0]
    me = lax.axis_index("wide")

    def put(ref, first, row, entry, energy):
        target = facts_ref[row, 0, entry]

        @pl.when((target >= 0) & (target // bal == me))
        def _():
            ref[pl.ds(first + target % bal, 1), :] = energy

    for e in range(bal):
        put(out_ref, 0, 0, e, energy_ref[e : e + 1, :])
    ones = jnp.ones((1, out_ref.shape[1]), jnp.float32)
    put(masks_ref, 0, 2, bal + 1, ones)

    @pl.when(me % 2 == 1)
    def _():
        put(out_ref, 0, 1, bal, last_ref[2:3, :])

    @pl.when(me % 2 == 0)
    def _():
        put(masks_ref, bal, 3, bal, ones)


def grid_plan(samples, centroids, move_target, fetch_ids, cand):
    rows = samples.shape[3]
    width = samples.shape[4]
    slots_in = samples.shape[2]
    bal = cand.shape[2]
    lists = cand.shape[3]
    pool = fetch_ids.shape[2]
    owned = centroids.shape[0] // rows
    peers = lax.axis_size("wide")
    sub = lax.axis_index("sub")
    tau = 2.0 * math.sqrt(D)
    handed = slots_in - bal
    span = rows // 2
    lanes = slots_in * span
    cut = 6 * span
    pair_x, pair_c = 1, 2

    table = [move_target.reshape(1, slots_in), fetch_ids.reshape(1, pool), cand.reshape(bal, lists)]
    facts = jnp.concatenate([jnp.pad(part, ((0, 0), (0, pool - part.shape[1]))) for part in table])
    facts = jnp.stack([facts] + [paired(facts, flip) for flip in range(1, peers)])
    bias = call(
        lambda *refs: bias_kernel(
            *refs, slots_in=slots_in, bal=bal, lists=lists, owned=owned, flips=(pair_x, pair_c), span=span
        ),
        "bias",
        [SMEM],
        [facts],
        [shape((2, 2 * owned, lanes))],
    )[0]

    share = owned * rows // 2
    c_half = lax.dynamic_slice_in_dim(centroids, lax.axis_index("rep") * share, share, 0)
    c_half = (c_half * (2.0 / tau)).astype(jnp.bfloat16)
    c0_own = (centroids * (2.0 / tau)).astype(jnp.bfloat16)
    c1_own = [paired(after(c_half, facts), pair_c)]
    c1_own.append(swapped(c1_own[0], "rep"))
    c0_oth = swapped(c0_own, "sub")

    blocks = samples.reshape(slots_in, rows, width)
    give = lax.dynamic_slice_in_dim(blocks, (1 - sub) * span, span, 1).reshape(lanes, width)
    took = swapped(give, "sub")
    own = lax.dynamic_slice_in_dim(blocks, sub * span, span, 1).reshape(lanes, width)
    full = jnp.concatenate([own, took], axis=1)
    x1 = [paired(after(part, facts), pair_x) for part in (full[:cut], full[cut:])]

    set_0 = joined([(c0_own, c0_oth)])
    set_1 = joined([(c1_own[0], swapped(c1_own[0], "sub"))])
    *em_0, stats_0 = score(bias, 0, full, {0: set_0, 1: set_1})
    *em_1, stats_1 = score(bias, 1, x1[0], {0: set_0, 1: set_1})
    later = lax.optimization_barrier((c1_own[1], stats_0, stats_1))[0]
    later = jnp.split(later, 2)
    set_2 = joined([(part, swapped(part, "sub")) for part in later])
    em_02, stats_02 = score(bias, 0, full, {2: set_2})
    em_12, stats_12 = score(bias, 1, x1[0], {2: set_2})
    before = [(stats_0, 0, 0), (stats_02, 4, 0), (stats_1, 8, 0), (stats_12, 12, 0)]
    *em_2, stats = score(bias, 1, x1[1], {0: set_0, 1: set_1, 2: set_2}, before, cut)
    em = list(zip((*em_0, em_02), (*em_1, em_12), em_2))
    peer = paired(stats, pair_x)

    xs = (full, *x1)
    half = jnp.bfloat16
    first, equal = (192,176), (264,)

    far_a, mass_a = far_sums(stats, peer, em[2], xs, 2, False)
    far_b, mass_b = far_sums(stats, peer, em[1], xs, 1, True, [far_a])
    near_a = [swapped(part, "sub") for part in jnp.split(far_a, 2)]
    sent_a = near_sums(
        stats, peer, em[2], xs, 2, False, mass_a, near_a, half, first, needs=[far_b]
    )
    far_c, mass_c = far_sums(stats, peer, em[0], xs, 0, False, sent_a[:1])
    near_c = [swapped(part, "sub") for part in jnp.split(far_c, 4)]
    near_b = [swapped(after(far_b, sent_a[0]), "sub")]
    part_b = near_sums(
        stats, peer, em[1], xs, 1, True, mass_b, near_b, jnp.float32, first, needs=sent_a[:1]
    )
    energy, last = call(
        lambda *refs: energy_kernel(*refs, tau=tau, span=span, handed=handed),
        "energy",
        [VMEM] * 5,
        [stats, peer, *xs],
        [shape((slots_in, span)), shape((8, span))],
        needs=part_b[:1],
    )

    def returned(part, came, needs, energies=()):
        args = [part, came, *energies]
        back = call(
            add_kernel, "add", [VMEM] * len(args), args, [shape(part.shape, half)], needs=needs
        )[0]
        return back, paired(back, pair_c)

    came_back, backs = [], []
    for i, part in enumerate(part_b):
        sent = after(sent_a[i], backs[-1]) if i >= 1 else sent_a[i]
        energies = [last] if i == len(first) else []
        back, came = returned(part, swapped(sent, "rep"), backs[-1:], energies)
        backs.append(back)
        came_back.append(came)
        if i == 1:
            sent_c = near_sums(
                stats, peer, em[0], xs, 0, False, mass_c, near_c, half, equal, needs=[back]
            )
            came_c = [swapped(part, "rep") for part in sent_c]
    far_d, mass_d = far_sums(stats, peer, em[0], xs, 0, True, backs[-1:])
    near_d = [swapped(far_d, "sub")]
    (part_d,) = near_sums(
        stats, peer, em[0], xs, 0, True, mass_d, near_d, jnp.float32, (), centroids, sent_c[:1]
    )
    early = []
    for came in came_back[:-1]:
        early += call(
            early_kernel, "early", [VMEM], [came], [shape(came.shape)], needs=early[-1:], flops=2 * 10**10
        )
    placed = call(
        place_kernel,
        "place",
        [SMEM] + [VMEM] * 2,
        [facts, energy, last],
        [shape((bal, span)), shape((2 * bal, span))],
        needs=backs[-1:],
    )
    fresh, energy = call(
        lambda *refs: final_kernel(*refs, parts=len(came_c)),
        "final",
        [VMEM] * (4 + len(came_c) + len(early)),
        [*placed, part_d, *came_c, *early, came_back[-1]],
        [shape((share, width)), shape((bal, span))],
    )
    return (fresh, energy.reshape(1, 1, bal, span))


def body(samples, centroids, move_target, fetch_ids, cand):
    sizes = [lax.axis_size(axis) for axis in ("wide", "rep", "sub")]
    if sizes == [4, 2, 2] and samples.shape[2] - cand.shape[2] == 2:
        return grid_plan(samples, centroids, move_target, fetch_ids, cand)
    return exchange_plan(samples, centroids, move_target, fetch_ids, cand)


def solution(mesh):
    return jax.shard_map(
        body,
        mesh=mesh,
        in_specs=(
            P(("groups", "wide"), "rep", None, None, "sub"),
            P(("groups", "wide"), "sub"),
            P(("groups", "wide"), "rep", None),
            P(("groups", "wide"), "rep", None),
            P(("groups", "wide"), "rep", None, None),
        ),
        out_specs=(P(("groups", "wide", "rep"), "sub"), P(("groups", "wide"), "rep", None, "sub")),
        check_vma=False,
    )
```

```python
import math

import jax
import jax.numpy as jnp
from jax import lax
from jax.experimental import pallas as pl
from jax.experimental.pallas import tpu as pltpu
from jax.sharding import PartitionSpec as P

D = 1024


PRIOR = 1.0


def passed_along(value, axis, steps):
    count = lax.axis_size(axis)
    pairs = [(source, (source + steps) % count) for source in range(count)]
    return lax.ppermute(value, axis, pairs)


def pick_rows(table, index, present):
    picked = jnp.take(table, jnp.maximum(index, 0), axis=0)
    shape = (present.shape[0],) + (1,) * (picked.ndim - 1)
    return jnp.where(present.reshape(shape), picked, jnp.zeros_like(picked))


def soften(scores, tau):
    logits = scores / tau
    top = jnp.max(logits, axis=-1, keepdims=True)
    expo = jnp.exp(logits - top)
    total = jnp.sum(expo, axis=-1, keepdims=True)
    weights = (expo / total).astype(jnp.bfloat16)
    energy = -tau * (top[..., 0] + jnp.log(total[..., 0])) / D
    return (weights, energy)


def exchange_plan(samples, centroids, move_target, fetch_ids, cand):
    rows = samples.shape[3]
    width = samples.shape[4]
    slots_in = samples.shape[2]
    bal = cand.shape[2]
    lists = cand.shape[3]
    pool = fetch_ids.shape[2]
    owned = centroids.shape[0] // rows
    peers = lax.axis_size("wide")
    myself = lax.axis_index("wide")
    cap = max(1, 3 * pool // (2 * peers))
    tau = 2.0 * math.sqrt(D)
    handed = slots_in - bal
    blocks = samples.reshape(slots_in, rows, width)
    target = move_target.reshape(slots_in)
    dest = jnp.where(target >= 0, target // bal, -1)
    dest_slot = jnp.where(target >= 0, target % bal, -1)
    got_list = []
    slot_list = []
    for step in range(handed):
        entry = bal + step
        present = target[entry] >= 0
        send_block = jnp.where(present, blocks[entry], jnp.zeros_like(blocks[entry]))[None]
        send_slot = jnp.where(present, target[entry] % bal, -1).reshape(1)
        got_block, got_slot = passed_along((send_block, send_slot), "wide", step + 1)
        got_list.append(got_block)
        slot_list.append(got_slot)
    ids = fetch_ids.reshape(pool)
    owner = ids // owned
    local = ids % owned
    before = jnp.arange(pool)[None, :] < jnp.arange(pool)[:, None]
    position = jnp.sum(((owner[None, :] == owner[:, None]) & before).astype(jnp.int32), axis=1)
    slot_of = owner * cap + position
    slot_match = slot_of[None, :] == jnp.arange(peers * cap, dtype=jnp.int32)[:, None]
    slot_used = jnp.any(slot_match, axis=1)
    slot_item = jnp.sum(
        jnp.where(slot_match, jnp.arange(pool, dtype=jnp.int32)[None, :], 0), axis=1
    )
    asks = jnp.where(slot_used, jnp.take(local, slot_item), -1).reshape(peers, cap)
    wanted = lax.all_to_all(asks, "wide", split_axis=0, concat_axis=0, tiled=True)
    table = centroids.reshape(owned, rows, width)
    table_half = table.astype(jnp.bfloat16)
    wanted_flat = wanted.reshape(peers * cap)
    reply = pick_rows(table_half, wanted_flat, wanted_flat >= 0).reshape(peers, cap, rows, width)
    answered = lax.all_to_all(reply, "wide", split_axis=0, concat_axis=0, tiled=True)
    fetched = jnp.take(answered.reshape(peers * cap, rows, width), slot_of, axis=0)
    keep_here = dest == myself
    source_blocks = jnp.concatenate([blocks] + got_list, axis=0)
    source_slots = jnp.concatenate([jnp.where(keep_here, dest_slot, -1)] + slot_list, axis=0)
    fill_match = source_slots[None, :] == jnp.arange(bal, dtype=jnp.int32)[:, None]
    live = jnp.any(fill_match, axis=1)
    anchor = jnp.sum(
        jnp.where(fill_match, jnp.arange(slots_in + handed, dtype=jnp.int32)[None, :], 0), axis=1
    )
    work = pick_rows(source_blocks, anchor, live)
    flat_lists = cand.reshape(bal * lists)
    fetched_sq = jnp.sum(jnp.square(fetched.astype(jnp.float32)), axis=-1)

    def slot_scores(carry, items):
        work_one, lists_one = items
        chosen = jnp.take(fetched, lists_one, axis=0).reshape(lists * rows, width)
        dots = jnp.dot(work_one, chosen.T, preferred_element_type=jnp.float32)
        cent_sq = jnp.take(fetched_sq, lists_one, axis=0).reshape(lists * rows)
        work_sq = jnp.sum(jnp.square(work_one.astype(jnp.float32)), axis=-1)
        return (carry, 2.0 * dots - cent_sq[None, :] - work_sq[:, None])

    unused, partial_scores = lax.scan(slot_scores, 0, (work, cand.reshape(bal, lists)))
    half = rows // lax.axis_size("sub")
    lowest = lax.axis_index("sub") * half
    scores = lax.psum(partial_scores, "sub")
    weights, energy = soften(scores, tau)
    energy = lax.dynamic_slice_in_dim(energy, lowest, half, 1)
    weights = jnp.where(live[:, None, None], weights, jnp.zeros_like(weights))
    energy = jnp.where(live[:, None], energy, jnp.zeros_like(energy))
    pool_range = jnp.arange(pool, dtype=jnp.int32)

    def slot_sums(total, items):
        weights_one, work_one, lists_one = items
        term = jnp.dot(weights_one.T, work_one, preferred_element_type=jnp.float32).reshape(
            lists, rows * width
        )
        hot = (lists_one[None, :] == pool_range[:, None]).astype(jnp.float32)
        return (total + jnp.dot(hot, term, precision=lax.Precision.HIGHEST), 0)

    start_sums = jnp.zeros((pool, rows * width), jnp.float32)
    pooled, unused_two = lax.scan(slot_sums, start_sums, (weights, work, cand.reshape(bal, lists)))
    pool_sums = pooled.astype(jnp.bfloat16)
    mass = jnp.sum(weights.astype(jnp.float32), axis=1).reshape(bal * lists, rows)
    onehot = (flat_lists[None, :] == pool_range[:, None]).astype(jnp.float32)
    pool_mass = jnp.dot(onehot, mass, precision=lax.Precision.HIGHEST).astype(jnp.bfloat16)
    back_sums = pick_rows(pool_sums, slot_item, slot_used).reshape(peers, cap, rows, width)
    back_mass = pick_rows(pool_mass, slot_item, slot_used).reshape(peers, cap, rows)
    came_sums, came_mass = (
        lax.all_to_all(back_sums, "wide", split_axis=0, concat_axis=0, tiled=True),
        lax.all_to_all(back_mass, "wide", split_axis=0, concat_axis=0, tiled=True),
    )
    owner_hot = (wanted_flat[None, :] == jnp.arange(owned, dtype=jnp.int32)[:, None]).astype(
        jnp.bfloat16
    )
    owner_sums = jnp.dot(
        owner_hot, came_sums.reshape(peers * cap, rows * width), preferred_element_type=jnp.float32
    )
    owner_mass = jnp.dot(
        owner_hot, came_mass.reshape(peers * cap, rows), preferred_element_type=jnp.float32
    )
    share_sums, share_mass = (
        lax.psum_scatter(
            owner_sums.reshape(owned, rows, width).astype(jnp.bfloat16),
            "rep",
            scatter_dimension=0,
            tiled=True,
        ).astype(jnp.float32),
        lax.psum_scatter(
            owner_mass.astype(jnp.bfloat16), "rep", scatter_dimension=0, tiled=True
        ).astype(jnp.float32),
    )
    share = share_sums.shape[0]
    first_block = lax.axis_index("rep") * share
    previous = lax.dynamic_slice_in_dim(table, first_block, share, 0)
    fresh = (share_sums + PRIOR * previous) / (share_mass[:, :, None] + PRIOR)
    return (fresh.reshape(share * rows, width), energy.reshape(1, 1, bal, half))


LOW = -1e30
FLOOR = -1e29
MEGA = 2**20
PAD = 16
BLOCK = 128
SETS = (0, 8, 12)
HBM = pl.BlockSpec(memory_space=pl.ANY)
VMEM = pl.BlockSpec(memory_space=pltpu.VMEM)
SMEM = pl.BlockSpec(memory_space=pltpu.SMEM)


def swapped(value, axis):
    return lax.ppermute(value, axis, [(0, 1), (1, 0)])


def paired(value, flip):
    count = lax.axis_size("wide")
    return lax.ppermute(value, "wide", [(w, w ^ flip) for w in range(count)])


def after(value, *others):
    return lax.optimization_barrier((value, *others))[0]


def shape(dims, dtype=jnp.float32):
    return jax.ShapeDtypeStruct(dims, dtype)


def call(kernel, name, in_specs, args, outs, scratch=(), needs=(), flops=1):
    count = len(args)

    def run(*refs):
        kernel(*refs[:count], *refs[count + len(needs) :])

    return pl.pallas_call(
        run,
        in_specs=in_specs + [HBM] * len(needs),
        out_specs=[VMEM] * len(outs),
        out_shape=outs,
        scratch_shapes=scratch,
        compiler_params=pltpu.CompilerParams(vmem_limit_bytes=16 * MEGA),
        cost_estimate=pl.CostEstimate(flops=flops, bytes_accessed=1, transcendentals=0),
        name=name,
    )(*args, *needs)


def bias_kernel(facts_ref, bias_ref, *, slots_in, bal, lists, owned, flips, span):
    me = lax.axis_index("wide")
    lanes = slots_in * span
    row = lax.broadcasted_iota(jnp.int32, (2 * owned, 128), 0)
    swung = (row + lax.axis_index("rep") * (owned // 2)) % owned
    block_id = jnp.where(row < owned, me * owned + row, (me ^ flips[1]) * owned + swung)
    place = lax.broadcasted_iota(jnp.int32, (1, 128), 1) // span
    for k in range(2):
        for lo in range(0, lanes, 128):
            listed = [jnp.full((1, 128), -1, jnp.int32) for j in range(lists)]
            for p in range(128 // span):
                target = facts_ref[flips[0] if k else 0, 0, lo // span + p]
                live = target >= 0
                target = jnp.maximum(target, 0)
                source = me ^ (target // bal)
                for j in range(lists):
                    block = facts_ref[source, 1, facts_ref[source, 2 + target % bal, j]]
                    listed[j] = jnp.where(place == p, jnp.where(live, block, -1), listed[j])
            times = jnp.zeros((2 * owned, 128), jnp.float32)
            for j in range(lists):
                times = times + jnp.where(block_id == listed[j], 1.0, 0.0)
            logs = jnp.log(jnp.maximum(times, 1.0))
            bias_ref[k, :, lo : lo + 128] = jnp.where(times > 0, logs, LOW)


def join_kernel(*refs):
    half_refs, (c_ref, square_ref) = refs[:-2], refs[-2:]
    width = half_refs[0].shape[1]
    lo = 0
    for own_ref, oth_ref in zip(half_refs[0::2], half_refs[1::2]):
        part = pl.ds(lo, oth_ref.shape[0])
        own, oth = own_ref[...], oth_ref[...]
        c_ref[part, 0:width] = own
        c_ref[part, width:] = oth
        total = jnp.zeros((part.size, 128), jnp.float32)
        for half in (own, oth):
            for lane in range(0, width, 128):
                piece = half[:, lane : lane + 128].astype(jnp.float32)
                total = total + piece * piece
        total = jnp.sum(total, axis=1, keepdims=True) * (math.sqrt(D) / 2.0)
        square_ref[part, :] = jnp.broadcast_to(total, (part.size, 128))
        lo += part.size


def joined(pairs, needs=()):
    count, width = sum(own.shape[0] for own, oth in pairs), pairs[0][0].shape[1]
    outs = [shape((count, 2 * width), jnp.bfloat16), shape((count, 128))]
    flat = [part for pair in pairs for part in pair]
    return call(join_kernel, "join", [VMEM] * len(flat), flat, outs, needs=needs)


def tiles(lanes):
    return [(lo, min(256, lanes - lo)) for lo in range(0, lanes, 256)]


def score_kernel(bias_ref, x_ref, *refs, chunk, first, sets, at):
    c_refs, refs = refs[: 2 * len(sets)], refs[2 * len(sets) :]
    before_refs, refs = refs[: len(at) - 1], refs[len(at) - 1 :]
    em_refs, (stats_ref, dots_ref) = refs[: len(sets)], refs[len(sets) :]
    for ref, (row, lane) in zip(before_refs, at[1:]):
        stats_ref[row : row + ref.shape[0], lane : lane + ref.shape[1]] = ref[...]
    turn = 0
    for lo, size in tiles(x_ref.shape[0]):
        for i, s in enumerate(sets):
            c_ref, csq_ref = c_refs[2 * i : 2 * i + 2]
            count, base = c_ref.shape[0] // BLOCK, SETS[s]
            part = slice(lo, lo + size)
            buf = dots_ref.at[turn % 2]
            turn += 1
            buf[0 : c_ref.shape[0], 0:size] = lax.dot_general(
                c_ref[...], x_ref[part, :], (((1,), (1,)), ((), ())), preferred_element_type=jnp.float32
            )

            def logits(g):
                block = pl.ds(g * BLOCK, BLOCK)
                less = jnp.concatenate([csq_ref[block, :]] * (size // 128), axis=1)
                return (buf[block, 0:size] - less).reshape(BLOCK // 8, 8, size)

            of_chunk = slice(first + lo, first + lo + size)
            bias = [bias_ref[chunk, base + g : base + g + 1, of_chunk] for g in range(count)]
            best = jnp.full((8, size), FLOOR, jnp.float32)
            for g in range(count):
                best = jnp.maximum(best, jnp.max(logits(g), axis=0) + bias[g])
            top = jnp.max(best, axis=0, keepdims=True)
            total = jnp.zeros((8, size), jnp.float32)
            for g in range(count):
                expo = jnp.exp(logits(g) + (bias[g] - top)[None])
                em_refs[i][pl.ds(g * BLOCK, BLOCK), part] = expo.reshape(BLOCK, size).astype(jnp.bfloat16)
                total = total + jnp.sum(expo, axis=0)
            row, lane = at[0][0] + 2 * i, at[0][1] + lo
            stats_ref[row : row + 1, lane : lane + size] = top
            stats_ref[row + 1 : row + 2, lane : lane + size] = jnp.sum(total, axis=0, keepdims=True)


def score(bias, chunk, x, sets, before=(), first=0):
    cols = [c.shape[0] for c, square in sets.values()]
    count = len(sets)
    at = [(8 * chunk, first) if before else (0, 0)] + [(row, lane) for part, row, lane in before]
    stats = shape((16, bias.shape[2]) if before else (2 * count, x.shape[0]))
    return call(
        lambda *refs: score_kernel(*refs, chunk=chunk, first=first, sets=list(sets), at=at),
        "scores",
        [VMEM] * (2 + 2 * count + len(before)),
        [bias, x, *[part for c in sets.values() for part in c], *[part[0] for part in before]],
        [shape((size, x.shape[0]), jnp.bfloat16) for size in cols] + [stats],
        [pltpu.VMEM((2, max(cols), 256), jnp.float32)],
    )


def combine(parts):
    top = parts[0][0:1]
    for part in parts[1:]:
        top = jnp.maximum(top, part[0:1])
    total = jnp.zeros_like(top)
    for part in parts:
        total = total + part[1:2] * jnp.exp(part[0:1] - top)
    return top, total


def chunk_parts(mine, peer, chunk):
    rows = [8 * chunk + 2 * s for s in range(len(SETS))]
    other = [8 * (1 - chunk) + 2 * s for s in range(len(SETS))]
    return [mine[row : row + 2] for row in rows] + [peer[row : row + 2] for row in other]


def half_rows(mine, count, which=0):
    if which:
        return pl.ds(0, count)
    rep = lax.axis_index("rep")
    return pl.ds(pl.multiple_of((rep if mine else 1 - rep) * count, count), count)


def weighted(mine_ref, peer_ref, em_refs, x_refs, rows, cols, which, mass):
    stats, peer = mine_ref[...], peer_ref[...]
    count = rows.size
    total = jnp.zeros((count, cols.stop - cols.start), jnp.float32)
    masses = jnp.zeros((count, 128), jnp.float32)
    lo = 0
    for em_ref, x_ref in zip(em_refs, x_refs):
        chunk, first = lo // stats.shape[1], lo % stats.shape[1]
        size = em_ref.shape[1]
        parts = chunk_parts(stats, peer, chunk)
        top, denom = combine(parts)
        factor = jnp.where(denom > 0, jnp.exp(parts[which][0:1] - top) / denom, 0.0)
        weights = (em_ref[rows, :].astype(jnp.float32) * factor[:, first : first + size]).astype(jnp.bfloat16)
        if mass:
            wide = weights.astype(jnp.float32)
            for lane in range(0, size, 128):
                masses = masses + wide[:, lane : lane + 128]
        total = total + jnp.dot(weights, x_ref[:, cols], preferred_element_type=jnp.float32)
        lo += size
    return total, masses


def far_kernel(*refs, which, mine):
    stats_ref, peer_ref = refs[0:2]
    em_refs, x_refs, (far_ref, mass_ref) = refs[2:5], refs[5:8], refs[8:]
    count, width = far_ref.shape[0] - PAD, far_ref.shape[1]
    total, masses = weighted(
        stats_ref, peer_ref, em_refs, x_refs, half_rows(mine, count, which), slice(width, 2 * width), which, True
    )
    masses = jnp.broadcast_to(jnp.sum(masses, axis=1, keepdims=True), (count, 128)).T[0:PAD]
    far_ref[0:count, :] = total.astype(jnp.bfloat16)
    far_ref[count:, :] = masses.astype(jnp.bfloat16)
    mass_ref[...] = masses


def near_kernel(*refs, which, mine, final, outs, swaps):
    stats_ref, peer_ref = refs[0:2]
    em_refs, x_refs, (mass_ref, *came_refs) = refs[2:5], refs[5:8], refs[8 : 9 + swaps]
    refs = refs[9 + swaps :]
    out_refs = refs[final : final + outs]
    count, width = sum(ref.shape[0] for ref in came_refs) - PAD, came_refs[0].shape[1]
    if final:
        previous_ref, sem = refs[1 + outs :]
        copy = pltpu.make_async_copy(refs[0].at[half_rows(mine, count), :], previous_ref, sem)
        copy.start()
    total, unused = weighted(
        stats_ref, peer_ref, em_refs, x_refs, half_rows(mine, count, which), slice(0, width), which, False
    )
    came = jnp.concatenate([ref[...] for ref in came_refs]).astype(jnp.float32)
    total = total + came[0:count]
    masses = mass_ref[...] + came[count:]
    if final:
        copy.wait()
        total = total + PRIOR * previous_ref[...]
        masses = masses + PRIOR
    lo = 0
    for out_ref in out_refs:
        size = min(out_ref.shape[0], count - lo)
        out_ref[0:size, :] = total[lo : lo + size].astype(out_ref.dtype)
        lo += size
    out_refs[-1][size:, :] = masses.astype(out_refs[-1].dtype)


def far_sums(stats, peer, em, xs, which, mine, needs=()):
    width = xs[0].shape[1] // 2
    count = em[0].shape[0] if which else em[0].shape[0] // 2
    return call(
        lambda *refs: far_kernel(*refs, which=which, mine=mine),
        "far",
        [VMEM] * 8,
        [stats, peer, *em, *xs],
        [shape((count + PAD, width), jnp.bfloat16), shape((PAD, width))],
        needs=needs,
    )


def near_sums(stats, peer, em, xs, which, mine, mass, came, dtype, parts=(), previous=None, needs=()):
    width = xs[0].shape[1] // 2
    count = em[0].shape[0] if which else em[0].shape[0] // 2
    final = previous is not None
    sizes = list(parts) + [count + PAD - sum(parts)]
    return call(
        lambda *refs: near_kernel(*refs, which=which, mine=mine, final=final, outs=len(sizes), swaps=len(came)),
        "near",
        [VMEM] * (9 + len(came)) + [HBM] * final,
        [stats, peer, *em, *xs, mass, *came] + [previous] * final,
        [shape((size, width), dtype) for size in sizes],
        [pltpu.VMEM((count, width), jnp.float32), pltpu.SemaphoreType.DMA] * final,
        needs,
    )


def add_kernel(a_ref, b_ref, *refs):
    out_ref = refs[-1]
    total = a_ref[...] + b_ref[...].astype(jnp.float32)
    out_ref[...] = total.astype(out_ref.dtype)
    if len(refs) == 2:
        count, width = out_ref.shape
        rest = jnp.concatenate([refs[0][k : k + 1, :] for k in range(4)], axis=1)
        rest = jnp.concatenate([rest, jnp.zeros((1, width - rest.shape[1]), jnp.float32)], axis=1)
        rows = [total[count - PAD : count - PAD + 8]]
        for k in range(3):
            rows.append(rest.astype(jnp.bfloat16).astype(jnp.float32))
            rest = rest - rows[-1]
        rows.append(jnp.zeros((5, width), jnp.float32))
        out_ref[count - PAD :, :] = jnp.concatenate(rows).astype(out_ref.dtype)


def early_kernel(came_ref, out_ref):
    out_ref[...] = came_ref[...].astype(out_ref.dtype)


def final_kernel(energy_ref, masks_ref, sums_ref, *refs, parts):
    rep_refs, back_refs, (out_ref, placed_ref) = refs[:parts], refs[parts:-2], refs[-2:]
    count, width = out_ref.shape
    bal, span = placed_ref.shape
    rep = jnp.concatenate([ref[...] for ref in rep_refs]).astype(jnp.float32)
    back = jnp.concatenate([ref[...].astype(jnp.float32) for ref in back_refs])
    total = sums_ref[...] + rep + back
    mass = jnp.broadcast_to(total[count : count + 1], (128, count)).T
    out_ref[...] = total[:count] / jnp.concatenate([mass] * (width // 128), axis=1)
    came = back[count + 8 : count + 9] + back[count + 9 : count + 10] + back[count + 10 : count + 11]
    placed = energy_ref[...]
    placed = jnp.where(masks_ref[0:bal, :] > 0, came[:, span : 2 * span], placed)
    placed_ref[...] = jnp.where(masks_ref[bal:, :] > 0, came[:, 2 * span : 3 * span], placed)


def energy_kernel(stats_ref, peer_ref, x0_ref, *refs, tau, span, handed):
    x1_refs, (out_ref, last_ref) = refs[:-2], refs[-2:]
    last_ref[...] = jnp.zeros_like(last_ref)
    for chunk, x_refs in enumerate(((x0_ref,), x1_refs)):
        squares = []
        for x_ref in x_refs:
            square = jnp.zeros((x_ref.shape[0], 128), jnp.float32)
            for lane in range(0, x_ref.shape[1], 128):
                part = x_ref[:, lane : lane + 128].astype(jnp.float32)
                square = square + part * part
            square = jnp.sum(square, axis=1, keepdims=True)
            squares.append(jnp.broadcast_to(square, (x_ref.shape[0], 128)).T[0:1])
        square = jnp.concatenate(squares, axis=1)
        lanes = square.shape[1]
        top, denom = combine(chunk_parts(stats_ref[...], peer_ref[...], chunk))
        energy = -tau * (top - square / tau + jnp.log(denom)) / D
        entries = lanes // span
        for e in range(entries):
            part = energy[:, e * span : (e + 1) * span]
            if chunk == 0:
                out_ref[e : e + 1, :] = part
            if e >= entries - handed:
                row = handed * chunk + e - (entries - handed)
                last_ref[row : row + 1, :] = part


def place_kernel(facts_ref, energy_ref, last_ref, out_ref, masks_ref):
    out_ref[...] = jnp.zeros_like(out_ref)
    masks_ref[...] = jnp.zeros_like(masks_ref)
    bal = out_ref.shape[0]
    me = lax.axis_index("wide")

    def put(ref, first, row, entry, energy):
        target = facts_ref[row, 0, entry]

        @pl.when((target >= 0) & (target // bal == me))
        def _():
            ref[pl.ds(first + target % bal, 1), :] = energy

    for e in range(bal):
        put(out_ref, 0, 0, e, energy_ref[e : e + 1, :])
    ones = jnp.ones((1, out_ref.shape[1]), jnp.float32)
    put(masks_ref, 0, 2, bal + 1, ones)

    @pl.when(me % 2 == 1)
    def _():
        put(out_ref, 0, 1, bal, last_ref[2:3, :])

    @pl.when(me % 2 == 0)
    def _():
        put(masks_ref, bal, 3, bal, ones)


def grid_plan(samples, centroids, move_target, fetch_ids, cand):
    rows = samples.shape[3]
    width = samples.shape[4]
    slots_in = samples.shape[2]
    bal = cand.shape[2]
    lists = cand.shape[3]
    pool = fetch_ids.shape[2]
    owned = centroids.shape[0] // rows
    peers = lax.axis_size("wide")
    sub = lax.axis_index("sub")
    tau = 2.0 * math.sqrt(D)
    handed = slots_in - bal
    span = rows // 2
    lanes = slots_in * span
    cut = 6 * span
    pair_x, pair_c = 1, 2

    table = [move_target.reshape(1, slots_in), fetch_ids.reshape(1, pool), cand.reshape(bal, lists)]
    facts = jnp.concatenate([jnp.pad(part, ((0, 0), (0, pool - part.shape[1]))) for part in table])
    facts = jnp.stack([facts] + [paired(facts, flip) for flip in range(1, peers)])
    bias = call(
        lambda *refs: bias_kernel(
            *refs, slots_in=slots_in, bal=bal, lists=lists, owned=owned, flips=(pair_x, pair_c), span=span
        ),
        "bias",
        [SMEM],
        [facts],
        [shape((2, 2 * owned, lanes))],
    )[0]

    share = owned * rows // 2
    c_half = lax.dynamic_slice_in_dim(centroids, lax.axis_index("rep") * share, share, 0)
    c_half = (c_half * (2.0 / tau)).astype(jnp.bfloat16)
    c0_own = (centroids * (2.0 / tau)).astype(jnp.bfloat16)
    c1_own = [paired(after(c_half, facts), pair_c)]
    c1_own.append(swapped(c1_own[0], "rep"))
    c0_oth = swapped(c0_own, "sub")

    blocks = samples.reshape(slots_in, rows, width)
    give = lax.dynamic_slice_in_dim(blocks, (1 - sub) * span, span, 1).reshape(lanes, width)
    took = swapped(give, "sub")
    own = lax.dynamic_slice_in_dim(blocks, sub * span, span, 1).reshape(lanes, width)
    full = jnp.concatenate([own, took], axis=1)
    x1 = [paired(after(part, facts), pair_x) for part in (full[:cut], full[cut:])]

    set_0 = joined([(c0_own, c0_oth)])
    set_1 = joined([(c1_own[0], swapped(c1_own[0], "sub"))])
    *em_0, stats_0 = score(bias, 0, full, {0: set_0, 1: set_1})
    *em_1, stats_1 = score(bias, 1, x1[0], {0: set_0, 1: set_1})
    later = lax.optimization_barrier((c1_own[1], stats_0, stats_1))[0]
    later = jnp.split(later, 2)
    set_2 = joined([(part, swapped(part, "sub")) for part in later])
    em_02, stats_02 = score(bias, 0, full, {2: set_2})
    em_12, stats_12 = score(bias, 1, x1[0], {2: set_2})
    before = [(stats_0, 0, 0), (stats_02, 4, 0), (stats_1, 8, 0), (stats_12, 12, 0)]
    *em_2, stats = score(bias, 1, x1[1], {0: set_0, 1: set_1, 2: set_2}, before, cut)
    em = list(zip((*em_0, em_02), (*em_1, em_12), em_2))
    peer = paired(stats, pair_x)

    xs = (full, *x1)
    half = jnp.bfloat16
    first, equal = (144,192), (264,)

    far_a, mass_a = far_sums(stats, peer, em[2], xs, 2, False)
    far_b, mass_b = far_sums(stats, peer, em[1], xs, 1, True, [far_a])
    near_a = [swapped(part, "sub") for part in jnp.split(far_a, 2)]
    sent_a = near_sums(
        stats, peer, em[2], xs, 2, False, mass_a, near_a, half, first, needs=[far_b]
    )
    far_c, mass_c = far_sums(stats, peer, em[0], xs, 0, False, sent_a[:1])
    near_c = [swapped(part, "sub") for part in jnp.split(far_c, 4)]
    near_b = [swapped(after(far_b, sent_a[0]), "sub")]
    part_b = near_sums(
        stats, peer, em[1], xs, 1, True, mass_b, near_b, jnp.float32, first, needs=sent_a[:1]
    )
    energy, last = call(
        lambda *refs: energy_kernel(*refs, tau=tau, span=span, handed=handed),
        "energy",
        [VMEM] * 5,
        [stats, peer, *xs],
        [shape((slots_in, span)), shape((8, span))],
        needs=part_b[:1],
    )

    def returned(part, came, needs, energies=()):
        args = [part, came, *energies]
        back = call(
            add_kernel, "add", [VMEM] * len(args), args, [shape(part.shape, half)], needs=needs
        )[0]
        return back, paired(back, pair_c)

    came_back, backs = [], []
    for i, part in enumerate(part_b):
        sent = after(sent_a[i], backs[-1]) if i >= 2 else sent_a[i]
        energies = [last] if i == len(first) else []
        back, came = returned(part, swapped(sent, "rep"), backs[-1:], energies)
        backs.append(back)
        came_back.append(came)
        if i == 1:
            sent_c = near_sums(
                stats, peer, em[0], xs, 0, False, mass_c, near_c, half, equal, needs=[back]
            )
            came_c = [swapped(part, "rep") for part in sent_c]
    far_d, mass_d = far_sums(stats, peer, em[0], xs, 0, True, backs[-1:])
    near_d = [swapped(far_d, "sub")]
    (part_d,) = near_sums(
        stats, peer, em[0], xs, 0, True, mass_d, near_d, jnp.float32, (), centroids, sent_c[:1]
    )
    early = []
    for came in came_back[:-1]:
        early += call(
            early_kernel, "early", [VMEM], [came], [shape(came.shape)], needs=early[-1:], flops=2 * 10**10
        )
    placed = call(
        place_kernel,
        "place",
        [SMEM] + [VMEM] * 2,
        [facts, energy, last],
        [shape((bal, span)), shape((2 * bal, span))],
        needs=backs[-1:],
    )
    fresh, energy = call(
        lambda *refs: final_kernel(*refs, parts=len(came_c)),
        "final",
        [VMEM] * (4 + len(came_c) + len(early)),
        [*placed, part_d, *came_c, *early, came_back[-1]],
        [shape((share, width)), shape((bal, span))],
    )
    return (fresh, energy.reshape(1, 1, bal, span))


def body(samples, centroids, move_target, fetch_ids, cand):
    sizes = [lax.axis_size(axis) for axis in ("wide", "rep", "sub")]
    if sizes == [4, 2, 2] and samples.shape[2] - cand.shape[2] == 2:
        return grid_plan(samples, centroids, move_target, fetch_ids, cand)
    return exchange_plan(samples, centroids, move_target, fetch_ids, cand)


def solution(mesh):
    return jax.shard_map(
        body,
        mesh=mesh,
        in_specs=(
            P(("groups", "wide"), "rep", None, None, "sub"),
            P(("groups", "wide"), "sub"),
            P(("groups", "wide"), "rep", None),
            P(("groups", "wide"), "rep", None),
            P(("groups", "wide"), "rep", None, None),
        ),
        out_specs=(P(("groups", "wide", "rep"), "sub"), P(("groups", "wide"), "rep", None, "sub")),
        check_vma=False,
    )
```

```python
import math

import jax
import jax.numpy as jnp
from jax import lax
from jax.experimental import pallas as pl
from jax.experimental.pallas import tpu as pltpu
from jax.sharding import PartitionSpec as P

D = 1024


PRIOR = 1.0


def passed_along(value, axis, steps):
    count = lax.axis_size(axis)
    pairs = [(source, (source + steps) % count) for source in range(count)]
    return lax.ppermute(value, axis, pairs)


def pick_rows(table, index, present):
    picked = jnp.take(table, jnp.maximum(index, 0), axis=0)
    shape = (present.shape[0],) + (1,) * (picked.ndim - 1)
    return jnp.where(present.reshape(shape), picked, jnp.zeros_like(picked))


def soften(scores, tau):
    logits = scores / tau
    top = jnp.max(logits, axis=-1, keepdims=True)
    expo = jnp.exp(logits - top)
    total = jnp.sum(expo, axis=-1, keepdims=True)
    weights = (expo / total).astype(jnp.bfloat16)
    energy = -tau * (top[..., 0] + jnp.log(total[..., 0])) / D
    return (weights, energy)


def exchange_plan(samples, centroids, move_target, fetch_ids, cand):
    rows = samples.shape[3]
    width = samples.shape[4]
    slots_in = samples.shape[2]
    bal = cand.shape[2]
    lists = cand.shape[3]
    pool = fetch_ids.shape[2]
    owned = centroids.shape[0] // rows
    peers = lax.axis_size("wide")
    myself = lax.axis_index("wide")
    cap = max(1, 3 * pool // (2 * peers))
    tau = 2.0 * math.sqrt(D)
    handed = slots_in - bal
    blocks = samples.reshape(slots_in, rows, width)
    target = move_target.reshape(slots_in)
    dest = jnp.where(target >= 0, target // bal, -1)
    dest_slot = jnp.where(target >= 0, target % bal, -1)
    got_list = []
    slot_list = []
    for step in range(handed):
        entry = bal + step
        present = target[entry] >= 0
        send_block = jnp.where(present, blocks[entry], jnp.zeros_like(blocks[entry]))[None]
        send_slot = jnp.where(present, target[entry] % bal, -1).reshape(1)
        got_block, got_slot = passed_along((send_block, send_slot), "wide", step + 1)
        got_list.append(got_block)
        slot_list.append(got_slot)
    ids = fetch_ids.reshape(pool)
    owner = ids // owned
    local = ids % owned
    before = jnp.arange(pool)[None, :] < jnp.arange(pool)[:, None]
    position = jnp.sum(((owner[None, :] == owner[:, None]) & before).astype(jnp.int32), axis=1)
    slot_of = owner * cap + position
    slot_match = slot_of[None, :] == jnp.arange(peers * cap, dtype=jnp.int32)[:, None]
    slot_used = jnp.any(slot_match, axis=1)
    slot_item = jnp.sum(
        jnp.where(slot_match, jnp.arange(pool, dtype=jnp.int32)[None, :], 0), axis=1
    )
    asks = jnp.where(slot_used, jnp.take(local, slot_item), -1).reshape(peers, cap)
    wanted = lax.all_to_all(asks, "wide", split_axis=0, concat_axis=0, tiled=True)
    table = centroids.reshape(owned, rows, width)
    table_half = table.astype(jnp.bfloat16)
    wanted_flat = wanted.reshape(peers * cap)
    reply = pick_rows(table_half, wanted_flat, wanted_flat >= 0).reshape(peers, cap, rows, width)
    answered = lax.all_to_all(reply, "wide", split_axis=0, concat_axis=0, tiled=True)
    fetched = jnp.take(answered.reshape(peers * cap, rows, width), slot_of, axis=0)
    keep_here = dest == myself
    source_blocks = jnp.concatenate([blocks] + got_list, axis=0)
    source_slots = jnp.concatenate([jnp.where(keep_here, dest_slot, -1)] + slot_list, axis=0)
    fill_match = source_slots[None, :] == jnp.arange(bal, dtype=jnp.int32)[:, None]
    live = jnp.any(fill_match, axis=1)
    anchor = jnp.sum(
        jnp.where(fill_match, jnp.arange(slots_in + handed, dtype=jnp.int32)[None, :], 0), axis=1
    )
    work = pick_rows(source_blocks, anchor, live)
    flat_lists = cand.reshape(bal * lists)
    fetched_sq = jnp.sum(jnp.square(fetched.astype(jnp.float32)), axis=-1)

    def slot_scores(carry, items):
        work_one, lists_one = items
        chosen = jnp.take(fetched, lists_one, axis=0).reshape(lists * rows, width)
        dots = jnp.dot(work_one, chosen.T, preferred_element_type=jnp.float32)
        cent_sq = jnp.take(fetched_sq, lists_one, axis=0).reshape(lists * rows)
        work_sq = jnp.sum(jnp.square(work_one.astype(jnp.float32)), axis=-1)
        return (carry, 2.0 * dots - cent_sq[None, :] - work_sq[:, None])

    unused, partial_scores = lax.scan(slot_scores, 0, (work, cand.reshape(bal, lists)))
    half = rows // lax.axis_size("sub")
    lowest = lax.axis_index("sub") * half
    scores = lax.psum(partial_scores, "sub")
    weights, energy = soften(scores, tau)
    energy = lax.dynamic_slice_in_dim(energy, lowest, half, 1)
    weights = jnp.where(live[:, None, None], weights, jnp.zeros_like(weights))
    energy = jnp.where(live[:, None], energy, jnp.zeros_like(energy))
    pool_range = jnp.arange(pool, dtype=jnp.int32)

    def slot_sums(total, items):
        weights_one, work_one, lists_one = items
        term = jnp.dot(weights_one.T, work_one, preferred_element_type=jnp.float32).reshape(
            lists, rows * width
        )
        hot = (lists_one[None, :] == pool_range[:, None]).astype(jnp.float32)
        return (total + jnp.dot(hot, term, precision=lax.Precision.HIGHEST), 0)

    start_sums = jnp.zeros((pool, rows * width), jnp.float32)
    pooled, unused_two = lax.scan(slot_sums, start_sums, (weights, work, cand.reshape(bal, lists)))
    pool_sums = pooled.astype(jnp.bfloat16)
    mass = jnp.sum(weights.astype(jnp.float32), axis=1).reshape(bal * lists, rows)
    onehot = (flat_lists[None, :] == pool_range[:, None]).astype(jnp.float32)
    pool_mass = jnp.dot(onehot, mass, precision=lax.Precision.HIGHEST).astype(jnp.bfloat16)
    back_sums = pick_rows(pool_sums, slot_item, slot_used).reshape(peers, cap, rows, width)
    back_mass = pick_rows(pool_mass, slot_item, slot_used).reshape(peers, cap, rows)
    came_sums, came_mass = (
        lax.all_to_all(back_sums, "wide", split_axis=0, concat_axis=0, tiled=True),
        lax.all_to_all(back_mass, "wide", split_axis=0, concat_axis=0, tiled=True),
    )
    owner_hot = (wanted_flat[None, :] == jnp.arange(owned, dtype=jnp.int32)[:, None]).astype(
        jnp.bfloat16
    )
    owner_sums = jnp.dot(
        owner_hot, came_sums.reshape(peers * cap, rows * width), preferred_element_type=jnp.float32
    )
    owner_mass = jnp.dot(
        owner_hot, came_mass.reshape(peers * cap, rows), preferred_element_type=jnp.float32
    )
    share_sums, share_mass = (
        lax.psum_scatter(
            owner_sums.reshape(owned, rows, width).astype(jnp.bfloat16),
            "rep",
            scatter_dimension=0,
            tiled=True,
        ).astype(jnp.float32),
        lax.psum_scatter(
            owner_mass.astype(jnp.bfloat16), "rep", scatter_dimension=0, tiled=True
        ).astype(jnp.float32),
    )
    share = share_sums.shape[0]
    first_block = lax.axis_index("rep") * share
    previous = lax.dynamic_slice_in_dim(table, first_block, share, 0)
    fresh = (share_sums + PRIOR * previous) / (share_mass[:, :, None] + PRIOR)
    return (fresh.reshape(share * rows, width), energy.reshape(1, 1, bal, half))


LOW = -1e30
FLOOR = -1e29
MEGA = 2**20
PAD = 16
BLOCK = 128
SETS = (0, 8, 12)
HBM = pl.BlockSpec(memory_space=pl.ANY)
VMEM = pl.BlockSpec(memory_space=pltpu.VMEM)
SMEM = pl.BlockSpec(memory_space=pltpu.SMEM)


def swapped(value, axis):
    return lax.ppermute(value, axis, [(0, 1), (1, 0)])


def paired(value, flip):
    count = lax.axis_size("wide")
    return lax.ppermute(value, "wide", [(w, w ^ flip) for w in range(count)])


def after(value, *others):
    return lax.optimization_barrier((value, *others))[0]


def shape(dims, dtype=jnp.float32):
    return jax.ShapeDtypeStruct(dims, dtype)


def call(kernel, name, in_specs, args, outs, scratch=(), needs=(), flops=1):
    count = len(args)

    def run(*refs):
        kernel(*refs[:count], *refs[count + len(needs) :])

    return pl.pallas_call(
        run,
        in_specs=in_specs + [HBM] * len(needs),
        out_specs=[VMEM] * len(outs),
        out_shape=outs,
        scratch_shapes=scratch,
        compiler_params=pltpu.CompilerParams(vmem_limit_bytes=16 * MEGA),
        cost_estimate=pl.CostEstimate(flops=flops, bytes_accessed=1, transcendentals=0),
        name=name,
    )(*args, *needs)


def bias_kernel(facts_ref, bias_ref, *, slots_in, bal, lists, owned, flips, span):
    me = lax.axis_index("wide")
    lanes = slots_in * span
    row = lax.broadcasted_iota(jnp.int32, (2 * owned, 128), 0)
    swung = (row + lax.axis_index("rep") * (owned // 2)) % owned
    block_id = jnp.where(row < owned, me * owned + row, (me ^ flips[1]) * owned + swung)
    place = lax.broadcasted_iota(jnp.int32, (1, 128), 1) // span
    for k in range(2):
        for lo in range(0, lanes, 128):
            listed = [jnp.full((1, 128), -1, jnp.int32) for j in range(lists)]
            for p in range(128 // span):
                target = facts_ref[flips[0] if k else 0, 0, lo // span + p]
                live = target >= 0
                target = jnp.maximum(target, 0)
                source = me ^ (target // bal)
                for j in range(lists):
                    block = facts_ref[source, 1, facts_ref[source, 2 + target % bal, j]]
                    listed[j] = jnp.where(place == p, jnp.where(live, block, -1), listed[j])
            times = jnp.zeros((2 * owned, 128), jnp.float32)
            for j in range(lists):
                times = times + jnp.where(block_id == listed[j], 1.0, 0.0)
            logs = jnp.log(jnp.maximum(times, 1.0))
            bias_ref[k, :, lo : lo + 128] = jnp.where(times > 0, logs, LOW)


def join_kernel(*refs):
    half_refs, (c_ref, square_ref) = refs[:-2], refs[-2:]
    width = half_refs[0].shape[1]
    lo = 0
    for own_ref, oth_ref in zip(half_refs[0::2], half_refs[1::2]):
        part = pl.ds(lo, oth_ref.shape[0])
        own, oth = own_ref[...], oth_ref[...]
        c_ref[part, 0:width] = own
        c_ref[part, width:] = oth
        total = jnp.zeros((part.size, 128), jnp.float32)
        for half in (own, oth):
            for lane in range(0, width, 128):
                piece = half[:, lane : lane + 128].astype(jnp.float32)
                total = total + piece * piece
        total = jnp.sum(total, axis=1, keepdims=True) * (math.sqrt(D) / 2.0)
        square_ref[part, :] = jnp.broadcast_to(total, (part.size, 128))
        lo += part.size


def joined(pairs, needs=()):
    count, width = sum(own.shape[0] for own, oth in pairs), pairs[0][0].shape[1]
    outs = [shape((count, 2 * width), jnp.bfloat16), shape((count, 128))]
    flat = [part for pair in pairs for part in pair]
    return call(join_kernel, "join", [VMEM] * len(flat), flat, outs, needs=needs)


def tiles(lanes):
    return [(lo, min(256, lanes - lo)) for lo in range(0, lanes, 256)]


def score_kernel(bias_ref, x_ref, *refs, chunk, first, sets, at):
    c_refs, refs = refs[: 2 * len(sets)], refs[2 * len(sets) :]
    before_refs, refs = refs[: len(at) - 1], refs[len(at) - 1 :]
    em_refs, (stats_ref, dots_ref) = refs[: len(sets)], refs[len(sets) :]
    for ref, (row, lane) in zip(before_refs, at[1:]):
        stats_ref[row : row + ref.shape[0], lane : lane + ref.shape[1]] = ref[...]
    turn = 0
    for lo, size in tiles(x_ref.shape[0]):
        for i, s in enumerate(sets):
            c_ref, csq_ref = c_refs[2 * i : 2 * i + 2]
            count, base = c_ref.shape[0] // BLOCK, SETS[s]
            part = slice(lo, lo + size)
            buf = dots_ref.at[turn % 2]
            turn += 1
            buf[0 : c_ref.shape[0], 0:size] = lax.dot_general(
                c_ref[...], x_ref[part, :], (((1,), (1,)), ((), ())), preferred_element_type=jnp.float32
            )

            def logits(g):
                block = pl.ds(g * BLOCK, BLOCK)
                less = jnp.concatenate([csq_ref[block, :]] * (size // 128), axis=1)
                return (buf[block, 0:size] - less).reshape(BLOCK // 8, 8, size)

            of_chunk = slice(first + lo, first + lo + size)
            bias = [bias_ref[chunk, base + g : base + g + 1, of_chunk] for g in range(count)]
            best = jnp.full((8, size), FLOOR, jnp.float32)
            for g in range(count):
                best = jnp.maximum(best, jnp.max(logits(g), axis=0) + bias[g])
            top = jnp.max(best, axis=0, keepdims=True)
            total = jnp.zeros((8, size), jnp.float32)
            for g in range(count):
                expo = jnp.exp(logits(g) + (bias[g] - top)[None])
                em_refs[i][pl.ds(g * BLOCK, BLOCK), part] = expo.reshape(BLOCK, size).astype(jnp.bfloat16)
                total = total + jnp.sum(expo, axis=0)
            row, lane = at[0][0] + 2 * i, at[0][1] + lo
            stats_ref[row : row + 1, lane : lane + size] = top
            stats_ref[row + 1 : row + 2, lane : lane + size] = jnp.sum(total, axis=0, keepdims=True)


def score(bias, chunk, x, sets, before=(), first=0):
    cols = [c.shape[0] for c, square in sets.values()]
    count = len(sets)
    at = [(8 * chunk, first) if before else (0, 0)] + [(row, lane) for part, row, lane in before]
    stats = shape((16, bias.shape[2]) if before else (2 * count, x.shape[0]))
    return call(
        lambda *refs: score_kernel(*refs, chunk=chunk, first=first, sets=list(sets), at=at),
        "scores",
        [VMEM] * (2 + 2 * count + len(before)),
        [bias, x, *[part for c in sets.values() for part in c], *[part[0] for part in before]],
        [shape((size, x.shape[0]), jnp.bfloat16) for size in cols] + [stats],
        [pltpu.VMEM((2, max(cols), 256), jnp.float32)],
    )


def combine(parts):
    top = parts[0][0:1]
    for part in parts[1:]:
        top = jnp.maximum(top, part[0:1])
    total = jnp.zeros_like(top)
    for part in parts:
        total = total + part[1:2] * jnp.exp(part[0:1] - top)
    return top, total


def chunk_parts(mine, peer, chunk):
    rows = [8 * chunk + 2 * s for s in range(len(SETS))]
    other = [8 * (1 - chunk) + 2 * s for s in range(len(SETS))]
    return [mine[row : row + 2] for row in rows] + [peer[row : row + 2] for row in other]


def half_rows(mine, count, which=0):
    if which:
        return pl.ds(0, count)
    rep = lax.axis_index("rep")
    return pl.ds(pl.multiple_of((rep if mine else 1 - rep) * count, count), count)


def weighted(mine_ref, peer_ref, em_refs, x_refs, rows, cols, which, mass, skip=0):
    stats, peer = mine_ref[...], peer_ref[...]
    count = rows.size
    total = jnp.zeros((count - skip, cols.stop - cols.start), jnp.float32)
    masses = jnp.zeros((count, 128), jnp.float32)
    lo = 0
    for em_ref, x_ref in zip(em_refs, x_refs):
        chunk, first = lo // stats.shape[1], lo % stats.shape[1]
        size = em_ref.shape[1]
        parts = chunk_parts(stats, peer, chunk)
        top, denom = combine(parts)
        factor = jnp.where(denom > 0, jnp.exp(parts[which][0:1] - top) / denom, 0.0)
        weights = (em_ref[rows, :].astype(jnp.float32) * factor[:, first : first + size]).astype(jnp.bfloat16)
        if mass:
            wide = weights.astype(jnp.float32)
            for lane in range(0, size, 128):
                masses = masses + wide[:, lane : lane + 128]
        total = total + jnp.dot(weights[skip:], x_ref[:, cols], preferred_element_type=jnp.float32)
        lo += size
    return total, masses


def far_kernel(*refs, which, mine, skip):
    stats_ref, peer_ref = refs[0:2]
    em_refs, x_refs, (far_ref, mass_ref) = refs[2:5], refs[5:8], refs[8:]
    count, width = far_ref.shape[0] - PAD + skip, far_ref.shape[1]
    rows, cols = half_rows(mine, count, which), slice(width, 2 * width)
    total, masses = weighted(stats_ref, peer_ref, em_refs, x_refs, rows, cols, which, True, skip)
    masses = jnp.broadcast_to(jnp.sum(masses, axis=1, keepdims=True), (count, 128)).T[0:PAD]
    far_ref[0 : count - skip, :] = total.astype(jnp.bfloat16)
    far_ref[count - skip :, :] = masses.astype(jnp.bfloat16)
    mass_ref[...] = masses


def near_kernel(*refs, which, mine, final, outs, swaps, skip):
    stats_ref, peer_ref = refs[0:2]
    em_refs, x_refs, (mass_ref, *came_refs) = refs[2:5], refs[5:8], refs[8 : 9 + swaps]
    refs = refs[9 + swaps :]
    out_refs = refs[final : final + outs]
    count, width = sum(ref.shape[0] for ref in came_refs) - PAD + skip, came_refs[0].shape[1]
    if final:
        previous_ref, sem = refs[1 + outs :]
        copy = pltpu.make_async_copy(refs[0].at[half_rows(mine, count), :], previous_ref, sem)
        copy.start()
    rows = pl.ds(skip, count - skip) if skip else half_rows(mine, count, which)
    total, unused = weighted(stats_ref, peer_ref, em_refs, x_refs, rows, slice(0, width), which, False)
    count = count - skip
    came = jnp.concatenate([ref[...] for ref in came_refs]).astype(jnp.float32)
    total = total + came[0:count]
    masses = mass_ref[...] + came[count:]
    if final:
        copy.wait()
        total = total + PRIOR * previous_ref[...]
        masses = masses + PRIOR
    lo = 0
    for out_ref in out_refs:
        size = min(out_ref.shape[0], count - lo)
        out_ref[0:size, :] = total[lo : lo + size].astype(out_ref.dtype)
        lo += size
    out_refs[-1][size:, :] = masses.astype(out_refs[-1].dtype)


def far_sums(stats, peer, em, xs, which, mine, needs=(), skip=0):
    width = xs[0].shape[1] // 2
    count = em[0].shape[0] if which else em[0].shape[0] // 2
    return call(
        lambda *refs: far_kernel(*refs, which=which, mine=mine, skip=skip),
        "far",
        [VMEM] * 8,
        [stats, peer, *em, *xs],
        [shape((count - skip + PAD, width), jnp.bfloat16), shape((PAD, width))],
        needs=needs,
    )


def lead_kernel(*refs, which, far):
    out_ref = refs[-1]
    count, width = out_ref.shape
    cols = slice(width, 2 * width) if far else slice(0, width)
    total, unused = weighted(refs[0], refs[1], refs[2:5], refs[5:8], pl.ds(0, count), cols, which, False)
    if not far:
        total = total + refs[8][...].astype(jnp.float32)
    out_ref[...] = total.astype(out_ref.dtype)


def lead_sums(stats, peer, em, xs, which, count, came=(), needs=()):
    width = xs[0].shape[1] // 2
    return call(
        lambda *refs: lead_kernel(*refs, which=which, far=not came),
        "lead",
        [VMEM] * (8 + len(came)),
        [stats, peer, *em, *xs, *came],
        [shape((count, width), jnp.bfloat16)],
        needs=needs,
    )[0]


def near_sums(stats, peer, em, xs, which, mine, mass, came, dtype, parts=(), previous=None, needs=(), skip=0):
    width = xs[0].shape[1] // 2
    count = em[0].shape[0] if which else em[0].shape[0] // 2
    final = previous is not None
    sizes = list(parts) + [count + PAD - skip - sum(parts)]
    return call(
        lambda *refs: near_kernel(*refs, which=which, mine=mine, final=final, outs=len(sizes), swaps=len(came), skip=skip),
        "near",
        [VMEM] * (9 + len(came)) + [HBM] * final,
        [stats, peer, *em, *xs, mass, *came] + [previous] * final,
        [shape((size, width), dtype) for size in sizes],
        [pltpu.VMEM((count, width), jnp.float32), pltpu.SemaphoreType.DMA] * final,
        needs,
    )


def add_kernel(a_ref, b_ref, *refs):
    out_ref = refs[-1]
    total = a_ref[...] + b_ref[...].astype(jnp.float32)
    out_ref[...] = total.astype(out_ref.dtype)
    if len(refs) == 2:
        count, width = out_ref.shape
        rest = jnp.concatenate([refs[0][k : k + 1, :] for k in range(4)], axis=1)
        rest = jnp.concatenate([rest, jnp.zeros((1, width - rest.shape[1]), jnp.float32)], axis=1)
        rows = [total[count - PAD : count - PAD + 8]]
        for k in range(3):
            rows.append(rest.astype(jnp.bfloat16).astype(jnp.float32))
            rest = rest - rows[-1]
        rows.append(jnp.zeros((5, width), jnp.float32))
        out_ref[count - PAD :, :] = jnp.concatenate(rows).astype(out_ref.dtype)


def early_kernel(came_ref, out_ref):
    out_ref[...] = came_ref[...].astype(out_ref.dtype)


def final_kernel(energy_ref, masks_ref, sums_ref, *refs, parts):
    rep_refs, back_refs, (out_ref, placed_ref) = refs[:parts], refs[parts:-2], refs[-2:]
    count, width = out_ref.shape
    bal, span = placed_ref.shape
    rep = jnp.concatenate([ref[...] for ref in rep_refs]).astype(jnp.float32)
    back = jnp.concatenate([ref[...].astype(jnp.float32) for ref in back_refs])
    total = sums_ref[...] + rep + back
    mass = jnp.broadcast_to(total[count : count + 1], (128, count)).T
    out_ref[...] = total[:count] / jnp.concatenate([mass] * (width // 128), axis=1)
    came = back[count + 8 : count + 9] + back[count + 9 : count + 10] + back[count + 10 : count + 11]
    placed = energy_ref[...]
    placed = jnp.where(masks_ref[0:bal, :] > 0, came[:, span : 2 * span], placed)
    placed_ref[...] = jnp.where(masks_ref[bal:, :] > 0, came[:, 2 * span : 3 * span], placed)


def energy_kernel(stats_ref, peer_ref, x0_ref, *refs, tau, span, handed):
    x1_refs, (out_ref, last_ref) = refs[:-2], refs[-2:]
    last_ref[...] = jnp.zeros_like(last_ref)
    for chunk, x_refs in enumerate(((x0_ref,), x1_refs)):
        squares = []
        for x_ref in x_refs:
            square = jnp.zeros((x_ref.shape[0], 128), jnp.float32)
            for lane in range(0, x_ref.shape[1], 128):
                part = x_ref[:, lane : lane + 128].astype(jnp.float32)
                square = square + part * part
            square = jnp.sum(square, axis=1, keepdims=True)
            squares.append(jnp.broadcast_to(square, (x_ref.shape[0], 128)).T[0:1])
        square = jnp.concatenate(squares, axis=1)
        lanes = square.shape[1]
        top, denom = combine(chunk_parts(stats_ref[...], peer_ref[...], chunk))
        energy = -tau * (top - square / tau + jnp.log(denom)) / D
        entries = lanes // span
        for e in range(entries):
            part = energy[:, e * span : (e + 1) * span]
            if chunk == 0:
                out_ref[e : e + 1, :] = part
            if e >= entries - handed:
                row = handed * chunk + e - (entries - handed)
                last_ref[row : row + 1, :] = part


def place_kernel(facts_ref, energy_ref, last_ref, out_ref, masks_ref):
    out_ref[...] = jnp.zeros_like(out_ref)
    masks_ref[...] = jnp.zeros_like(masks_ref)
    bal = out_ref.shape[0]
    me = lax.axis_index("wide")

    def put(ref, first, row, entry, energy):
        target = facts_ref[row, 0, entry]

        @pl.when((target >= 0) & (target // bal == me))
        def _():
            ref[pl.ds(first + target % bal, 1), :] = energy

    for e in range(bal):
        put(out_ref, 0, 0, e, energy_ref[e : e + 1, :])
    ones = jnp.ones((1, out_ref.shape[1]), jnp.float32)
    put(masks_ref, 0, 2, bal + 1, ones)

    @pl.when(me % 2 == 1)
    def _():
        put(out_ref, 0, 1, bal, last_ref[2:3, :])

    @pl.when(me % 2 == 0)
    def _():
        put(masks_ref, bal, 3, bal, ones)


def grid_plan(samples, centroids, move_target, fetch_ids, cand):
    rows = samples.shape[3]
    width = samples.shape[4]
    slots_in = samples.shape[2]
    bal = cand.shape[2]
    lists = cand.shape[3]
    pool = fetch_ids.shape[2]
    owned = centroids.shape[0] // rows
    peers = lax.axis_size("wide")
    sub = lax.axis_index("sub")
    tau = 2.0 * math.sqrt(D)
    handed = slots_in - bal
    span = rows // 2
    lanes = slots_in * span
    cut = 6 * span
    pair_x, pair_c = 1, 2

    table = [move_target.reshape(1, slots_in), fetch_ids.reshape(1, pool), cand.reshape(bal, lists)]
    facts = jnp.concatenate([jnp.pad(part, ((0, 0), (0, pool - part.shape[1]))) for part in table])
    facts = jnp.stack([facts] + [paired(facts, flip) for flip in range(1, peers)])
    bias = call(
        lambda *refs: bias_kernel(
            *refs, slots_in=slots_in, bal=bal, lists=lists, owned=owned, flips=(pair_x, pair_c), span=span
        ),
        "bias",
        [SMEM],
        [facts],
        [shape((2, 2 * owned, lanes))],
    )[0]

    share = owned * rows // 2
    c_half = lax.dynamic_slice_in_dim(centroids, lax.axis_index("rep") * share, share, 0)
    c_half = (c_half * (2.0 / tau)).astype(jnp.bfloat16)
    c0_own = (centroids * (2.0 / tau)).astype(jnp.bfloat16)
    c1_own = [paired(after(c_half, facts), pair_c)]
    c1_own.append(swapped(c1_own[0], "rep"))
    c0_oth = swapped(c0_own, "sub")

    blocks = samples.reshape(slots_in, rows, width)
    give = lax.dynamic_slice_in_dim(blocks, (1 - sub) * span, span, 1).reshape(lanes, width)
    took = swapped(give, "sub")
    own = lax.dynamic_slice_in_dim(blocks, sub * span, span, 1).reshape(lanes, width)
    full = jnp.concatenate([own, took], axis=1)
    x1 = [paired(after(part, facts), pair_x) for part in (full[:cut], full[cut:])]

    set_0 = joined([(c0_own, c0_oth)])
    set_1 = joined([(c1_own[0], swapped(c1_own[0], "sub"))])
    *em_0, stats_0 = score(bias, 0, full, {0: set_0, 1: set_1})
    *em_1, stats_1 = score(bias, 1, x1[0], {0: set_0, 1: set_1})
    later = lax.optimization_barrier((c1_own[1], stats_0, stats_1))[0]
    later = jnp.split(later, 2)
    set_2 = joined([(part, swapped(part, "sub")) for part in later])
    em_02, stats_02 = score(bias, 0, full, {2: set_2})
    em_12, stats_12 = score(bias, 1, x1[0], {2: set_2})
    before = [(stats_0, 0, 0), (stats_02, 4, 0), (stats_1, 8, 0), (stats_12, 12, 0)]
    *em_2, stats = score(bias, 1, x1[1], {0: set_0, 1: set_1, 2: set_2}, before, cut)
    em = list(zip((*em_0, em_02), (*em_1, em_12), em_2))
    peer = paired(stats, pair_x)

    xs = (full, *x1)
    half = jnp.bfloat16
    first, equal = (144,192), (264,)

    lead = first[0]
    lead_far = lead_sums(stats, peer, em[2], xs, 2, lead)
    far_a, mass_a = far_sums(stats, peer, em[2], xs, 2, False, [lead_far], lead)
    far_b, mass_b = far_sums(stats, peer, em[1], xs, 1, True, [far_a])
    sent_a = [lead_sums(stats, peer, em[2], xs, 2, lead, [swapped(lead_far, "sub")], [far_b])]
    near_a = [swapped(after(far_a, sent_a[0]), "sub")]
    sent_a += near_sums(
        stats, peer, em[2], xs, 2, False, mass_a, near_a, half, first[1:], needs=[far_b], skip=lead
    )
    near_b = [swapped(after(far_b, sent_a[0]), "sub")]
    part_b = near_sums(
        stats, peer, em[1], xs, 1, True, mass_b, near_b, jnp.float32, first, needs=sent_a[:1]
    )
    energy, last = call(
        lambda *refs: energy_kernel(*refs, tau=tau, span=span, handed=handed),
        "energy",
        [VMEM] * 5,
        [stats, peer, *xs],
        [shape((slots_in, span)), shape((8, span))],
        needs=part_b[:1],
    )

    def returned(part, came, needs, energies=()):
        args = [part, came, *energies]
        back = call(
            add_kernel, "add", [VMEM] * len(args), args, [shape(part.shape, half)], needs=needs
        )[0]
        return back, paired(back, pair_c)

    came_back, backs = [], []
    for i, part in enumerate(part_b):
        sent = after(sent_a[i], backs[-1]) if i >= 2 else sent_a[i]
        energies = [last] if i == len(first) else []
        back, came = returned(part, swapped(sent, "rep"), backs[-1:], energies)
        backs.append(back)
        came_back.append(came)
        if i == 0:
            far_c, mass_c = far_sums(stats, peer, em[0], xs, 0, False, backs[:1])
            near_c = [swapped(part, "sub") for part in jnp.split(far_c, 4)]
        if i == 1:
            sent_c = near_sums(
                stats, peer, em[0], xs, 0, False, mass_c, near_c, half, equal, needs=[back]
            )
            came_c = [swapped(part, "rep") for part in sent_c]
    far_d, mass_d = far_sums(stats, peer, em[0], xs, 0, True, backs[-1:])
    near_d = [swapped(far_d, "sub")]
    (part_d,) = near_sums(
        stats, peer, em[0], xs, 0, True, mass_d, near_d, jnp.float32, (), centroids, sent_c[:1]
    )
    early = []
    for came in came_back[:-1]:
        early += call(
            early_kernel, "early", [VMEM], [came], [shape(came.shape)], needs=early[-1:], flops=2 * 10**10
        )
    placed = call(
        place_kernel,
        "place",
        [SMEM] + [VMEM] * 2,
        [facts, energy, last],
        [shape((bal, span)), shape((2 * bal, span))],
        needs=backs[-1:],
    )
    fresh, energy = call(
        lambda *refs: final_kernel(*refs, parts=len(came_c)),
        "final",
        [VMEM] * (4 + len(came_c) + len(early)),
        [*placed, part_d, *came_c, *early, came_back[-1]],
        [shape((share, width)), shape((bal, span))],
    )
    return (fresh, energy.reshape(1, 1, bal, span))


def body(samples, centroids, move_target, fetch_ids, cand):
    sizes = [lax.axis_size(axis) for axis in ("wide", "rep", "sub")]
    if sizes == [4, 2, 2] and samples.shape[2] - cand.shape[2] == 2:
        return grid_plan(samples, centroids, move_target, fetch_ids, cand)
    return exchange_plan(samples, centroids, move_target, fetch_ids, cand)


def solution(mesh):
    return jax.shard_map(
        body,
        mesh=mesh,
        in_specs=(
            P(("groups", "wide"), "rep", None, None, "sub"),
            P(("groups", "wide"), "sub"),
            P(("groups", "wide"), "rep", None),
            P(("groups", "wide"), "rep", None),
            P(("groups", "wide"), "rep", None, None),
        ),
        out_specs=(P(("groups", "wide", "rep"), "sub"), P(("groups", "wide"), "rep", None, "sub")),
        check_vma=False,
    )
```

```python
import math

import jax
import jax.numpy as jnp
from jax import lax
from jax.experimental import pallas as pl
from jax.experimental.pallas import tpu as pltpu
from jax.sharding import PartitionSpec as P

D = 1024


PRIOR = 1.0


def passed_along(value, axis, steps):
    count = lax.axis_size(axis)
    pairs = [(source, (source + steps) % count) for source in range(count)]
    return lax.ppermute(value, axis, pairs)


def pick_rows(table, index, present):
    picked = jnp.take(table, jnp.maximum(index, 0), axis=0)
    shape = (present.shape[0],) + (1,) * (picked.ndim - 1)
    return jnp.where(present.reshape(shape), picked, jnp.zeros_like(picked))


def soften(scores, tau):
    logits = scores / tau
    top = jnp.max(logits, axis=-1, keepdims=True)
    expo = jnp.exp(logits - top)
    total = jnp.sum(expo, axis=-1, keepdims=True)
    weights = (expo / total).astype(jnp.bfloat16)
    energy = -tau * (top[..., 0] + jnp.log(total[..., 0])) / D
    return (weights, energy)


def exchange_plan(samples, centroids, move_target, fetch_ids, cand):
    rows = samples.shape[3]
    width = samples.shape[4]
    slots_in = samples.shape[2]
    bal = cand.shape[2]
    lists = cand.shape[3]
    pool = fetch_ids.shape[2]
    owned = centroids.shape[0] // rows
    peers = lax.axis_size("wide")
    myself = lax.axis_index("wide")
    cap = max(1, 3 * pool // (2 * peers))
    tau = 2.0 * math.sqrt(D)
    handed = slots_in - bal
    blocks = samples.reshape(slots_in, rows, width)
    target = move_target.reshape(slots_in)
    dest = jnp.where(target >= 0, target // bal, -1)
    dest_slot = jnp.where(target >= 0, target % bal, -1)
    got_list = []
    slot_list = []
    for step in range(handed):
        entry = bal + step
        present = target[entry] >= 0
        send_block = jnp.where(present, blocks[entry], jnp.zeros_like(blocks[entry]))[None]
        send_slot = jnp.where(present, target[entry] % bal, -1).reshape(1)
        got_block, got_slot = passed_along((send_block, send_slot), "wide", step + 1)
        got_list.append(got_block)
        slot_list.append(got_slot)
    ids = fetch_ids.reshape(pool)
    owner = ids // owned
    local = ids % owned
    before = jnp.arange(pool)[None, :] < jnp.arange(pool)[:, None]
    position = jnp.sum(((owner[None, :] == owner[:, None]) & before).astype(jnp.int32), axis=1)
    slot_of = owner * cap + position
    slot_match = slot_of[None, :] == jnp.arange(peers * cap, dtype=jnp.int32)[:, None]
    slot_used = jnp.any(slot_match, axis=1)
    slot_item = jnp.sum(
        jnp.where(slot_match, jnp.arange(pool, dtype=jnp.int32)[None, :], 0), axis=1
    )
    asks = jnp.where(slot_used, jnp.take(local, slot_item), -1).reshape(peers, cap)
    wanted = lax.all_to_all(asks, "wide", split_axis=0, concat_axis=0, tiled=True)
    table = centroids.reshape(owned, rows, width)
    table_half = table.astype(jnp.bfloat16)
    wanted_flat = wanted.reshape(peers * cap)
    reply = pick_rows(table_half, wanted_flat, wanted_flat >= 0).reshape(peers, cap, rows, width)
    answered = lax.all_to_all(reply, "wide", split_axis=0, concat_axis=0, tiled=True)
    fetched = jnp.take(answered.reshape(peers * cap, rows, width), slot_of, axis=0)
    keep_here = dest == myself
    source_blocks = jnp.concatenate([blocks] + got_list, axis=0)
    source_slots = jnp.concatenate([jnp.where(keep_here, dest_slot, -1)] + slot_list, axis=0)
    fill_match = source_slots[None, :] == jnp.arange(bal, dtype=jnp.int32)[:, None]
    live = jnp.any(fill_match, axis=1)
    anchor = jnp.sum(
        jnp.where(fill_match, jnp.arange(slots_in + handed, dtype=jnp.int32)[None, :], 0), axis=1
    )
    work = pick_rows(source_blocks, anchor, live)
    flat_lists = cand.reshape(bal * lists)
    fetched_sq = jnp.sum(jnp.square(fetched.astype(jnp.float32)), axis=-1)

    def slot_scores(carry, items):
        work_one, lists_one = items
        chosen = jnp.take(fetched, lists_one, axis=0).reshape(lists * rows, width)
        dots = jnp.dot(work_one, chosen.T, preferred_element_type=jnp.float32)
        cent_sq = jnp.take(fetched_sq, lists_one, axis=0).reshape(lists * rows)
        work_sq = jnp.sum(jnp.square(work_one.astype(jnp.float32)), axis=-1)
        return (carry, 2.0 * dots - cent_sq[None, :] - work_sq[:, None])

    unused, partial_scores = lax.scan(slot_scores, 0, (work, cand.reshape(bal, lists)))
    half = rows // lax.axis_size("sub")
    lowest = lax.axis_index("sub") * half
    scores = lax.psum(partial_scores, "sub")
    weights, energy = soften(scores, tau)
    energy = lax.dynamic_slice_in_dim(energy, lowest, half, 1)
    weights = jnp.where(live[:, None, None], weights, jnp.zeros_like(weights))
    energy = jnp.where(live[:, None], energy, jnp.zeros_like(energy))
    pool_range = jnp.arange(pool, dtype=jnp.int32)

    def slot_sums(total, items):
        weights_one, work_one, lists_one = items
        term = jnp.dot(weights_one.T, work_one, preferred_element_type=jnp.float32).reshape(
            lists, rows * width
        )
        hot = (lists_one[None, :] == pool_range[:, None]).astype(jnp.float32)
        return (total + jnp.dot(hot, term, precision=lax.Precision.HIGHEST), 0)

    start_sums = jnp.zeros((pool, rows * width), jnp.float32)
    pooled, unused_two = lax.scan(slot_sums, start_sums, (weights, work, cand.reshape(bal, lists)))
    pool_sums = pooled.astype(jnp.bfloat16)
    mass = jnp.sum(weights.astype(jnp.float32), axis=1).reshape(bal * lists, rows)
    onehot = (flat_lists[None, :] == pool_range[:, None]).astype(jnp.float32)
    pool_mass = jnp.dot(onehot, mass, precision=lax.Precision.HIGHEST).astype(jnp.bfloat16)
    back_sums = pick_rows(pool_sums, slot_item, slot_used).reshape(peers, cap, rows, width)
    back_mass = pick_rows(pool_mass, slot_item, slot_used).reshape(peers, cap, rows)
    came_sums, came_mass = (
        lax.all_to_all(back_sums, "wide", split_axis=0, concat_axis=0, tiled=True),
        lax.all_to_all(back_mass, "wide", split_axis=0, concat_axis=0, tiled=True),
    )
    owner_hot = (wanted_flat[None, :] == jnp.arange(owned, dtype=jnp.int32)[:, None]).astype(
        jnp.bfloat16
    )
    owner_sums = jnp.dot(
        owner_hot, came_sums.reshape(peers * cap, rows * width), preferred_element_type=jnp.float32
    )
    owner_mass = jnp.dot(
        owner_hot, came_mass.reshape(peers * cap, rows), preferred_element_type=jnp.float32
    )
    share_sums, share_mass = (
        lax.psum_scatter(
            owner_sums.reshape(owned, rows, width).astype(jnp.bfloat16),
            "rep",
            scatter_dimension=0,
            tiled=True,
        ).astype(jnp.float32),
        lax.psum_scatter(
            owner_mass.astype(jnp.bfloat16), "rep", scatter_dimension=0, tiled=True
        ).astype(jnp.float32),
    )
    share = share_sums.shape[0]
    first_block = lax.axis_index("rep") * share
    previous = lax.dynamic_slice_in_dim(table, first_block, share, 0)
    fresh = (share_sums + PRIOR * previous) / (share_mass[:, :, None] + PRIOR)
    return (fresh.reshape(share * rows, width), energy.reshape(1, 1, bal, half))


LOW = -1e30
FLOOR = -1e29
MEGA = 2**20
PAD = 16
BLOCK = 128
SETS = (0, 8, 12)
HBM = pl.BlockSpec(memory_space=pl.ANY)
VMEM = pl.BlockSpec(memory_space=pltpu.VMEM)
SMEM = pl.BlockSpec(memory_space=pltpu.SMEM)


def swapped(value, axis):
    return lax.ppermute(value, axis, [(0, 1), (1, 0)])


def paired(value, flip):
    count = lax.axis_size("wide")
    return lax.ppermute(value, "wide", [(w, w ^ flip) for w in range(count)])


def after(value, *others):
    return lax.optimization_barrier((value, *others))[0]


def shape(dims, dtype=jnp.float32):
    return jax.ShapeDtypeStruct(dims, dtype)


def call(kernel, name, in_specs, args, outs, scratch=(), needs=(), flops=1):
    count = len(args)

    def run(*refs):
        kernel(*refs[:count], *refs[count + len(needs) :])

    return pl.pallas_call(
        run,
        in_specs=in_specs + [HBM] * len(needs),
        out_specs=[VMEM] * len(outs),
        out_shape=outs,
        scratch_shapes=scratch,
        compiler_params=pltpu.CompilerParams(vmem_limit_bytes=16 * MEGA),
        cost_estimate=pl.CostEstimate(flops=flops, bytes_accessed=1, transcendentals=0),
        name=name,
    )(*args, *needs)


def bias_kernel(facts_ref, bias_ref, *, slots_in, bal, lists, owned, flips, span):
    me = lax.axis_index("wide")
    lanes = slots_in * span
    row = lax.broadcasted_iota(jnp.int32, (2 * owned, 128), 0)
    swung = (row + lax.axis_index("rep") * (owned // 2)) % owned
    block_id = jnp.where(row < owned, me * owned + row, (me ^ flips[1]) * owned + swung)
    place = lax.broadcasted_iota(jnp.int32, (1, 128), 1) // span
    for k in range(2):
        for lo in range(0, lanes, 128):
            listed = [jnp.full((1, 128), -1, jnp.int32) for j in range(lists)]
            for p in range(128 // span):
                target = facts_ref[flips[0] if k else 0, 0, lo // span + p]
                live = target >= 0
                target = jnp.maximum(target, 0)
                source = me ^ (target // bal)
                for j in range(lists):
                    block = facts_ref[source, 1, facts_ref[source, 2 + target % bal, j]]
                    listed[j] = jnp.where(place == p, jnp.where(live, block, -1), listed[j])
            times = jnp.zeros((2 * owned, 128), jnp.float32)
            for j in range(lists):
                times = times + jnp.where(block_id == listed[j], 1.0, 0.0)
            logs = jnp.log(jnp.maximum(times, 1.0))
            bias_ref[k, :, lo : lo + 128] = jnp.where(times > 0, logs, LOW)


def join_kernel(*refs):
    half_refs, (c_ref, square_ref) = refs[:-2], refs[-2:]
    width = half_refs[0].shape[1]
    lo = 0
    for own_ref, oth_ref in zip(half_refs[0::2], half_refs[1::2]):
        part = pl.ds(lo, oth_ref.shape[0])
        own, oth = own_ref[...], oth_ref[...]
        c_ref[part, 0:width] = own
        c_ref[part, width:] = oth
        total = jnp.zeros((part.size, 128), jnp.float32)
        for half in (own, oth):
            for lane in range(0, width, 128):
                piece = half[:, lane : lane + 128].astype(jnp.float32)
                total = total + piece * piece
        total = jnp.sum(total, axis=1, keepdims=True) * (math.sqrt(D) / 2.0)
        square_ref[part, :] = jnp.broadcast_to(total, (part.size, 128))
        lo += part.size


def joined(pairs, needs=()):
    count, width = sum(own.shape[0] for own, oth in pairs), pairs[0][0].shape[1]
    outs = [shape((count, 2 * width), jnp.bfloat16), shape((count, 128))]
    flat = [part for pair in pairs for part in pair]
    return call(join_kernel, "join", [VMEM] * len(flat), flat, outs, needs=needs)


def tiles(lanes):
    return [(lo, min(256, lanes - lo)) for lo in range(0, lanes, 256)]


def score_kernel(bias_ref, x_ref, *refs, chunk, first, sets, at):
    c_refs, refs = refs[: 2 * len(sets)], refs[2 * len(sets) :]
    before_refs, refs = refs[: len(at) - 1], refs[len(at) - 1 :]
    em_refs, (stats_ref, dots_ref) = refs[: len(sets)], refs[len(sets) :]
    for ref, (row, lane) in zip(before_refs, at[1:]):
        stats_ref[row : row + ref.shape[0], lane : lane + ref.shape[1]] = ref[...]
    turn = 0
    for lo, size in tiles(x_ref.shape[0]):
        for i, s in enumerate(sets):
            c_ref, csq_ref = c_refs[2 * i : 2 * i + 2]
            count, base = c_ref.shape[0] // BLOCK, SETS[s]
            part = slice(lo, lo + size)
            buf = dots_ref.at[turn % 2]
            turn += 1
            buf[0 : c_ref.shape[0], 0:size] = lax.dot_general(
                c_ref[...], x_ref[part, :], (((1,), (1,)), ((), ())), preferred_element_type=jnp.float32
            )

            def logits(g):
                block = pl.ds(g * BLOCK, BLOCK)
                less = jnp.concatenate([csq_ref[block, :]] * (size // 128), axis=1)
                return (buf[block, 0:size] - less).reshape(BLOCK // 8, 8, size)

            of_chunk = slice(first + lo, first + lo + size)
            bias = [bias_ref[chunk, base + g : base + g + 1, of_chunk] for g in range(count)]
            best = jnp.full((8, size), FLOOR, jnp.float32)
            for g in range(count):
                best = jnp.maximum(best, jnp.max(logits(g), axis=0) + bias[g])
            top = jnp.max(best, axis=0, keepdims=True)
            total = jnp.zeros((8, size), jnp.float32)
            for g in range(count):
                expo = jnp.exp(logits(g) + (bias[g] - top)[None])
                em_refs[i][pl.ds(g * BLOCK, BLOCK), part] = expo.reshape(BLOCK, size).astype(jnp.bfloat16)
                total = total + jnp.sum(expo, axis=0)
            row, lane = at[0][0] + 2 * i, at[0][1] + lo
            stats_ref[row : row + 1, lane : lane + size] = top
            stats_ref[row + 1 : row + 2, lane : lane + size] = jnp.sum(total, axis=0, keepdims=True)


def score(bias, chunk, x, sets, before=(), first=0):
    cols = [c.shape[0] for c, square in sets.values()]
    count = len(sets)
    at = [(8 * chunk, first) if before else (0, 0)] + [(row, lane) for part, row, lane in before]
    stats = shape((16, bias.shape[2]) if before else (2 * count, x.shape[0]))
    return call(
        lambda *refs: score_kernel(*refs, chunk=chunk, first=first, sets=list(sets), at=at),
        "scores",
        [VMEM] * (2 + 2 * count + len(before)),
        [bias, x, *[part for c in sets.values() for part in c], *[part[0] for part in before]],
        [shape((size, x.shape[0]), jnp.bfloat16) for size in cols] + [stats],
        [pltpu.VMEM((2, max(cols), 256), jnp.float32)],
    )


def combine(parts):
    top = parts[0][0:1]
    for part in parts[1:]:
        top = jnp.maximum(top, part[0:1])
    total = jnp.zeros_like(top)
    for part in parts:
        total = total + part[1:2] * jnp.exp(part[0:1] - top)
    return top, total


def chunk_parts(mine, peer, chunk):
    rows = [8 * chunk + 2 * s for s in range(len(SETS))]
    other = [8 * (1 - chunk) + 2 * s for s in range(len(SETS))]
    return [mine[row : row + 2] for row in rows] + [peer[row : row + 2] for row in other]


def half_rows(mine, count, which=0):
    if which:
        return pl.ds(0, count)
    rep = lax.axis_index("rep")
    return pl.ds(pl.multiple_of((rep if mine else 1 - rep) * count, count), count)


def weighted(mine_ref, peer_ref, em_refs, x_refs, rows, cols, which, mass, skip=0):
    stats, peer = mine_ref[...], peer_ref[...]
    count = rows.size
    total = jnp.zeros((count - skip, cols.stop - cols.start), jnp.float32)
    masses = jnp.zeros((count, 128), jnp.float32)
    lo = 0
    for em_ref, x_ref in zip(em_refs, x_refs):
        chunk, first = lo // stats.shape[1], lo % stats.shape[1]
        size = em_ref.shape[1]
        parts = chunk_parts(stats, peer, chunk)
        top, denom = combine(parts)
        factor = jnp.where(denom > 0, jnp.exp(parts[which][0:1] - top) / denom, 0.0)
        weights = (em_ref[rows, :].astype(jnp.float32) * factor[:, first : first + size]).astype(jnp.bfloat16)
        if mass:
            wide = weights.astype(jnp.float32)
            for lane in range(0, size, 128):
                masses = masses + wide[:, lane : lane + 128]
        total = total + jnp.dot(weights[skip:], x_ref[:, cols], preferred_element_type=jnp.float32)
        lo += size
    return total, masses


def far_kernel(*refs, which, mine, skip):
    stats_ref, peer_ref = refs[0:2]
    em_refs, x_refs, (far_ref, mass_ref) = refs[2:5], refs[5:8], refs[8:]
    count, width = far_ref.shape[0] - PAD + skip, far_ref.shape[1]
    rows, cols = half_rows(mine, count, which), slice(width, 2 * width)
    total, masses = weighted(stats_ref, peer_ref, em_refs, x_refs, rows, cols, which, True, skip)
    masses = jnp.broadcast_to(jnp.sum(masses, axis=1, keepdims=True), (count, 128)).T[0:PAD]
    far_ref[0 : count - skip, :] = total.astype(jnp.bfloat16)
    far_ref[count - skip :, :] = masses.astype(jnp.bfloat16)
    mass_ref[...] = masses


def near_kernel(*refs, which, mine, final, outs, swaps, skip):
    stats_ref, peer_ref = refs[0:2]
    em_refs, x_refs, (mass_ref, *came_refs) = refs[2:5], refs[5:8], refs[8 : 9 + swaps]
    refs = refs[9 + swaps :]
    out_refs = refs[final : final + outs]
    count, width = sum(ref.shape[0] for ref in came_refs) - PAD + skip, came_refs[0].shape[1]
    if final:
        previous_ref, sem = refs[1 + outs :]
        copy = pltpu.make_async_copy(refs[0].at[half_rows(mine, count), :], previous_ref, sem)
        copy.start()
    rows = pl.ds(skip, count - skip) if skip else half_rows(mine, count, which)
    total, unused = weighted(stats_ref, peer_ref, em_refs, x_refs, rows, slice(0, width), which, False)
    count = count - skip
    came = jnp.concatenate([ref[...] for ref in came_refs]).astype(jnp.float32)
    total = total + came[0:count]
    masses = mass_ref[...] + came[count:]
    if final:
        copy.wait()
        total = total + PRIOR * previous_ref[...]
        masses = masses + PRIOR
    lo = 0
    for out_ref in out_refs:
        size = min(out_ref.shape[0], count - lo)
        out_ref[0:size, :] = total[lo : lo + size].astype(out_ref.dtype)
        lo += size
    out_refs[-1][size:, :] = masses.astype(out_refs[-1].dtype)


def far_sums(stats, peer, em, xs, which, mine, needs=(), skip=0):
    width = xs[0].shape[1] // 2
    count = em[0].shape[0] if which else em[0].shape[0] // 2
    return call(
        lambda *refs: far_kernel(*refs, which=which, mine=mine, skip=skip),
        "far",
        [VMEM] * 8,
        [stats, peer, *em, *xs],
        [shape((count - skip + PAD, width), jnp.bfloat16), shape((PAD, width))],
        needs=needs,
    )


def lead_kernel(*refs, which, far):
    out_ref = refs[-1]
    count, width = out_ref.shape
    cols = slice(width, 2 * width) if far else slice(0, width)
    total, unused = weighted(refs[0], refs[1], refs[2:5], refs[5:8], pl.ds(0, count), cols, which, False)
    if not far:
        total = total + refs[8][...].astype(jnp.float32)
    out_ref[...] = total.astype(out_ref.dtype)


def lead_sums(stats, peer, em, xs, which, count, came=(), needs=()):
    width = xs[0].shape[1] // 2
    return call(
        lambda *refs: lead_kernel(*refs, which=which, far=not came),
        "lead",
        [VMEM] * (8 + len(came)),
        [stats, peer, *em, *xs, *came],
        [shape((count, width), jnp.bfloat16)],
        needs=needs,
    )[0]


def near_sums(stats, peer, em, xs, which, mine, mass, came, dtype, parts=(), previous=None, needs=(), skip=0):
    width = xs[0].shape[1] // 2
    count = em[0].shape[0] if which else em[0].shape[0] // 2
    final = previous is not None
    sizes = list(parts) + [count + PAD - skip - sum(parts)]
    return call(
        lambda *refs: near_kernel(*refs, which=which, mine=mine, final=final, outs=len(sizes), swaps=len(came), skip=skip),
        "near",
        [VMEM] * (9 + len(came)) + [HBM] * final,
        [stats, peer, *em, *xs, mass, *came] + [previous] * final,
        [shape((size, width), dtype) for size in sizes],
        [pltpu.VMEM((count, width), jnp.float32), pltpu.SemaphoreType.DMA] * final,
        needs,
    )


def add_kernel(a_ref, b_ref, *refs):
    out_ref = refs[-1]
    total = a_ref[...] + b_ref[...].astype(jnp.float32)
    out_ref[...] = total.astype(out_ref.dtype)
    if len(refs) == 2:
        count, width = out_ref.shape
        rest = jnp.concatenate([refs[0][k : k + 1, :] for k in range(4)], axis=1)
        rest = jnp.concatenate([rest, jnp.zeros((1, width - rest.shape[1]), jnp.float32)], axis=1)
        rows = [total[count - PAD : count - PAD + 8]]
        for k in range(3):
            rows.append(rest.astype(jnp.bfloat16).astype(jnp.float32))
            rest = rest - rows[-1]
        rows.append(jnp.zeros((5, width), jnp.float32))
        out_ref[count - PAD :, :] = jnp.concatenate(rows).astype(out_ref.dtype)


def early_kernel(came_ref, out_ref):
    out_ref[...] = came_ref[...].astype(out_ref.dtype)


def middle_kernel(sums_ref, *refs, parts):
    rep_refs, back_refs, out_ref = refs[:parts], refs[parts:-1], refs[-1]
    rep = jnp.concatenate([ref[...] for ref in rep_refs]).astype(jnp.float32)
    total = sums_ref[...] + rep
    back = jnp.concatenate([ref[...] for ref in back_refs])
    out_ref[0 : back.shape[0], :] = total[0 : back.shape[0]] + back
    out_ref[back.shape[0] :, :] = total[back.shape[0] :]


def final_kernel(energy_ref, masks_ref, sums_ref, last_ref, out_ref, placed_ref):
    count, width = out_ref.shape
    bal, span = placed_ref.shape
    first = sums_ref.shape[0] - last_ref.shape[0]
    last = last_ref[...].astype(jnp.float32)
    later = sums_ref[first:, :] + last
    mass = jnp.broadcast_to(later[count - first : count - first + 1], (128, count)).T
    mass = jnp.concatenate([mass] * (width // 128), axis=1)
    out_ref[0:first, :] = sums_ref[0:first, :] / mass[0:first]
    out_ref[first:, :] = later[: count - first] / mass[first:]
    row = count - first + 8
    came = last[row : row + 1] + last[row + 1 : row + 2] + last[row + 2 : row + 3]
    placed = energy_ref[...]
    placed = jnp.where(masks_ref[0:bal, :] > 0, came[:, span : 2 * span], placed)
    placed_ref[...] = jnp.where(masks_ref[bal:, :] > 0, came[:, 2 * span : 3 * span], placed)


def energy_kernel(stats_ref, peer_ref, x0_ref, *refs, tau, span, handed):
    x1_refs, (out_ref, last_ref) = refs[:-2], refs[-2:]
    last_ref[...] = jnp.zeros_like(last_ref)
    for chunk, x_refs in enumerate(((x0_ref,), x1_refs)):
        squares = []
        for x_ref in x_refs:
            square = jnp.zeros((x_ref.shape[0], 128), jnp.float32)
            for lane in range(0, x_ref.shape[1], 128):
                part = x_ref[:, lane : lane + 128].astype(jnp.float32)
                square = square + part * part
            square = jnp.sum(square, axis=1, keepdims=True)
            squares.append(jnp.broadcast_to(square, (x_ref.shape[0], 128)).T[0:1])
        square = jnp.concatenate(squares, axis=1)
        lanes = square.shape[1]
        top, denom = combine(chunk_parts(stats_ref[...], peer_ref[...], chunk))
        energy = -tau * (top - square / tau + jnp.log(denom)) / D
        entries = lanes // span
        for e in range(entries):
            part = energy[:, e * span : (e + 1) * span]
            if chunk == 0:
                out_ref[e : e + 1, :] = part
            if e >= entries - handed:
                row = handed * chunk + e - (entries - handed)
                last_ref[row : row + 1, :] = part


def place_kernel(facts_ref, energy_ref, last_ref, out_ref, masks_ref):
    out_ref[...] = jnp.zeros_like(out_ref)
    masks_ref[...] = jnp.zeros_like(masks_ref)
    bal = out_ref.shape[0]
    me = lax.axis_index("wide")

    def put(ref, first, row, entry, energy):
        target = facts_ref[row, 0, entry]

        @pl.when((target >= 0) & (target // bal == me))
        def _():
            ref[pl.ds(first + target % bal, 1), :] = energy

    for e in range(bal):
        put(out_ref, 0, 0, e, energy_ref[e : e + 1, :])
    ones = jnp.ones((1, out_ref.shape[1]), jnp.float32)
    put(masks_ref, 0, 2, bal + 1, ones)

    @pl.when(me % 2 == 1)
    def _():
        put(out_ref, 0, 1, bal, last_ref[2:3, :])

    @pl.when(me % 2 == 0)
    def _():
        put(masks_ref, bal, 3, bal, ones)


def grid_plan(samples, centroids, move_target, fetch_ids, cand):
    rows = samples.shape[3]
    width = samples.shape[4]
    slots_in = samples.shape[2]
    bal = cand.shape[2]
    lists = cand.shape[3]
    pool = fetch_ids.shape[2]
    owned = centroids.shape[0] // rows
    peers = lax.axis_size("wide")
    sub = lax.axis_index("sub")
    tau = 2.0 * math.sqrt(D)
    handed = slots_in - bal
    span = rows // 2
    lanes = slots_in * span
    cut = 6 * span
    pair_x, pair_c = 1, 2

    table = [move_target.reshape(1, slots_in), fetch_ids.reshape(1, pool), cand.reshape(bal, lists)]
    facts = jnp.concatenate([jnp.pad(part, ((0, 0), (0, pool - part.shape[1]))) for part in table])
    facts = jnp.stack([facts] + [paired(facts, flip) for flip in range(1, peers)])
    bias = call(
        lambda *refs: bias_kernel(
            *refs, slots_in=slots_in, bal=bal, lists=lists, owned=owned, flips=(pair_x, pair_c), span=span
        ),
        "bias",
        [SMEM],
        [facts],
        [shape((2, 2 * owned, lanes))],
    )[0]

    share = owned * rows // 2
    c_half = lax.dynamic_slice_in_dim(centroids, lax.axis_index("rep") * share, share, 0)
    c_half = (c_half * (2.0 / tau)).astype(jnp.bfloat16)
    c0_own = (centroids * (2.0 / tau)).astype(jnp.bfloat16)
    c1_own = [paired(after(c_half, facts), pair_c)]
    c1_own.append(swapped(c1_own[0], "rep"))
    c0_oth = swapped(c0_own, "sub")

    blocks = samples.reshape(slots_in, rows, width)
    give = lax.dynamic_slice_in_dim(blocks, (1 - sub) * span, span, 1).reshape(lanes, width)
    took = swapped(give, "sub")
    own = lax.dynamic_slice_in_dim(blocks, sub * span, span, 1).reshape(lanes, width)
    full = jnp.concatenate([own, took], axis=1)
    x1 = [paired(after(part, facts), pair_x) for part in (full[:cut], full[cut:])]

    set_0 = joined([(c0_own, c0_oth)])
    set_1 = joined([(c1_own[0], swapped(c1_own[0], "sub"))])
    *em_0, stats_0 = score(bias, 0, full, {0: set_0, 1: set_1})
    *em_1, stats_1 = score(bias, 1, x1[0], {0: set_0, 1: set_1})
    later = lax.optimization_barrier((c1_own[1], stats_0, stats_1))[0]
    later = jnp.split(later, 2)
    set_2 = joined([(part, swapped(part, "sub")) for part in later])
    em_02, stats_02 = score(bias, 0, full, {2: set_2})
    em_12, stats_12 = score(bias, 1, x1[0], {2: set_2})
    before = [(stats_0, 0, 0), (stats_02, 4, 0), (stats_1, 8, 0), (stats_12, 12, 0)]
    *em_2, stats = score(bias, 1, x1[1], {0: set_0, 1: set_1, 2: set_2}, before, cut)
    em = list(zip((*em_0, em_02), (*em_1, em_12), em_2))
    peer = paired(stats, pair_x)

    xs = (full, *x1)
    half = jnp.bfloat16
    first, equal = (144,192), (264,)

    lead = first[0]
    lead_far = lead_sums(stats, peer, em[2], xs, 2, lead)
    far_a, mass_a = far_sums(stats, peer, em[2], xs, 2, False, [lead_far], lead)
    far_b, mass_b = far_sums(stats, peer, em[1], xs, 1, True, [far_a])
    sent_a = [lead_sums(stats, peer, em[2], xs, 2, lead, [swapped(lead_far, "sub")], [far_b])]
    near_a = [swapped(after(far_a, sent_a[0]), "sub")]
    sent_a += near_sums(
        stats, peer, em[2], xs, 2, False, mass_a, near_a, half, first[1:], needs=[far_b], skip=lead
    )
    near_b = [swapped(after(far_b, sent_a[0]), "sub")]
    part_b = near_sums(
        stats, peer, em[1], xs, 1, True, mass_b, near_b, jnp.float32, first, needs=sent_a[:1]
    )
    energy, last = call(
        lambda *refs: energy_kernel(*refs, tau=tau, span=span, handed=handed),
        "energy",
        [VMEM] * 5,
        [stats, peer, *xs],
        [shape((slots_in, span)), shape((8, span))],
        needs=part_b[:1],
    )

    def returned(part, came, needs, energies=()):
        args = [part, came, *energies]
        back = call(
            add_kernel, "add", [VMEM] * len(args), args, [shape(part.shape, half)], needs=needs
        )[0]
        return back, paired(back, pair_c)

    came_back, backs = [], []
    for i, part in enumerate(part_b):
        sent = after(sent_a[i], backs[-1]) if i >= 2 else sent_a[i]
        energies = [last] if i == len(first) else []
        back, came = returned(part, swapped(sent, "rep"), backs[-1:], energies)
        backs.append(back)
        came_back.append(came)
        if i == 0:
            far_c, mass_c = far_sums(stats, peer, em[0], xs, 0, False, backs[:1])
            near_c = [swapped(part, "sub") for part in jnp.split(far_c, 4)]
        if i == 1:
            sent_c = near_sums(
                stats, peer, em[0], xs, 0, False, mass_c, near_c, half, equal, needs=[back]
            )
            came_c = [swapped(part, "rep") for part in sent_c]
    far_d, mass_d = far_sums(stats, peer, em[0], xs, 0, True, backs[-1:])
    near_d = [swapped(far_d, "sub")]
    (part_d,) = near_sums(
        stats, peer, em[0], xs, 0, True, mass_d, near_d, jnp.float32, (), centroids, sent_c[:1]
    )
    early = []
    for came in came_back[:-1]:
        early += call(
            early_kernel, "early", [VMEM], [came], [shape(came.shape)], needs=early[-1:], flops=2 * 10**10
        )
    placed = call(
        place_kernel,
        "place",
        [SMEM] + [VMEM] * 2,
        [facts, energy, last],
        [shape((bal, span)), shape((2 * bal, span))],
        needs=backs[-1:],
    )
    middle = call(
        lambda *refs: middle_kernel(*refs, parts=len(came_c)),
        "middle",
        [VMEM] * (1 + len(came_c) + len(early)),
        [part_d, *came_c, *early],
        [shape(part_d.shape)],
    )[0]
    fresh, energy = call(
        final_kernel,
        "final",
        [VMEM] * 4,
        [*placed, middle, came_back[-1]],
        [shape((share, width)), shape((bal, span))],
    )
    return (fresh, energy.reshape(1, 1, bal, span))


def body(samples, centroids, move_target, fetch_ids, cand):
    sizes = [lax.axis_size(axis) for axis in ("wide", "rep", "sub")]
    if sizes == [4, 2, 2] and samples.shape[2] - cand.shape[2] == 2:
        return grid_plan(samples, centroids, move_target, fetch_ids, cand)
    return exchange_plan(samples, centroids, move_target, fetch_ids, cand)


def solution(mesh):
    return jax.shard_map(
        body,
        mesh=mesh,
        in_specs=(
            P(("groups", "wide"), "rep", None, None, "sub"),
            P(("groups", "wide"), "sub"),
            P(("groups", "wide"), "rep", None),
            P(("groups", "wide"), "rep", None),
            P(("groups", "wide"), "rep", None, None),
        ),
        out_specs=(P(("groups", "wide", "rep"), "sub"), P(("groups", "wide"), "rep", None, "sub")),
        check_vma=False,
    )
```
